32 devices in a mesh: dp: 8 (over z, core), tensor: 4 (over y, x).
Axes of the slice: x: 2, y: 2, z: 4, core: 2. Of those that a mesh axis runs over, the one named last changes fastest.
Arguments:
- tokens: bfloat16 [8192, 1536], P(('dp', 'tensor')), may hold values from -6 to 6
- seq_lengths: int32 [8, 2], P('dp'), may hold values from 0 to 1024, as said below
- gain_attn: float32 [1536], replicated, may hold values from 0.5 to 1.5
- query_weight: bfloat16 [1536, 1536], P('dp', 'tensor'), may hold values from -0.15625 to 0.15625
- key_matrix: bfloat16 [1536, 768], P('dp', 'tensor'), may hold values from -0.15625 to 0.15625
- value_matrix: bfloat16 [1536, 768], P('dp', 'tensor'), may hold values from -0.15625 to 0.15625
- out_weight: bfloat16 [1536, 1536], P('tensor', 'dp'), may hold values from -3.5 to 3.5
- gain_ffn: float32 [1536], replicated, may hold values from 0.5 to 1.5
- gate_weight: bfloat16 [1536, 4096], P('dp', 'tensor'), may hold values from -0.15625 to 0.15625
- up_weight: bfloat16 [1536, 4096], P('dp', 'tensor'), may hold values from -0.15625 to 0.15625
- down_weight: bfloat16 [4096, 1536], P('tensor', 'dp'), may hold values from -0.1875 to 0.1875
- out_grad: bfloat16 [8192, 1536], P(('dp', 'tensor')), may hold values from -6 to 6
Outputs:
- mixed: bfloat16 [8192, 1536], P(('dp', 'tensor'))
- tokens_grad: float32 [8192, 1536], P(('dp', 'tensor'))
- gain_attn_grad: float32 [1536], replicated
- query_weight_grad: float32 [1536, 1536], P('dp', 'tensor')
- key_weight_grad: float32 [1536, 768], P('dp', 'tensor')
- value_weight_grad: float32 [1536, 768], P('dp', 'tensor')
- out_weight_grad: float32 [1536, 1536], P('tensor', 'dp')
- gain_ffn_grad: float32 [1536], replicated
- gate_weight_grad: float32 [1536, 4096], P('dp', 'tensor')
- up_weight_grad: float32 [1536, 4096], P('dp', 'tensor')
- down_weight_grad: float32 [4096, 1536], P('tensor', 'dp')
The draws below stay inside these ranges and needn't reach their ends.
Inputs may be any that keep to these rules, and one draw needn't show every extreme that they name: `seq_lengths`: row r lists the lengths of the sequences packed in order into tokens r * 1024 to (r + 1) * 1024 - 1: its nonzero entries are at least 512 and sum to 1024, zeros stand only after them, and some row holds a sequence of exactly 1024.
All inputs are finite; a program needn't handle non-finite values.
Results may differ from the reference program's by a relative error of at most 0.02.
Values may be sent and summed in bfloat16 or wider, within the bound.
A program may use at most 128 MiB of HBM per device.

```python
import jax
import jax.numpy as jnp
from jax import lax

MODEL_WIDTH = 1536
QUERY_HEAD_COUNT = 16
KEY_VALUE_HEADS = 8
HEAD_SIZE = 96
FF = 4096
PACKED_ROW_TOKENS = 1024
TOKENS = 8192
MAXLEN = 1024
MINLEN = 512
SLOTS = 2
N_DP = 8


def pack_row(row_key, forced):
    remain = jnp.int32(PACKED_ROW_TOKENS)
    chosen = []
    for slot_index in range(SLOTS):
        pick_key, coin_key = jax.random.split(jax.random.fold_in(row_key, slot_index))
        upper_len = jnp.minimum(MAXLEN, remain - MINLEN)
        candidate = jax.random.randint(pick_key, (), MINLEN, jnp.maximum(upper_len, MINLEN) + 1)
        coin_flip = jax.random.randint(coin_key, (), 0, 2)
        take_all = (remain <= MAXLEN) & ((upper_len < MINLEN) | (coin_flip == 1))
        length = jnp.where(remain == 0, 0, jnp.where(take_all, remain, candidate)).astype(jnp.int32)
        if slot_index == 0:
            length = jnp.where(forced, MAXLEN, length).astype(jnp.int32)
        remain = (remain - length).astype(jnp.int32)
        chosen.append(length)
    return jnp.stack(chosen).astype(jnp.int32)


def draw_seq_lengths(key, part):
    key = jax.random.fold_in(key, 11)
    long_key, rest_key = jax.random.split(key)
    long_row = jax.random.randint(long_key, (), 0, N_DP)
    row_keys = jax.random.split(rest_key, N_DP)
    forced = lax.iota(jnp.int32, N_DP) == long_row
    return jax.vmap(pack_row)(row_keys, forced)


def level_of(own_key, extent, cuts, smallest, high):
    def one(axis_at, blocks):
        heights = jax.random.uniform(jax.random.fold_in(jax.random.fold_in(own_key, 6), axis_at), (blocks,), jnp.float32, smallest / len(cuts), high / len(cuts))
        return jnp.repeat(jnp.exp(heights), extent[axis_at] // blocks).reshape((-1,) + (1,) * (len(extent) - axis_at - 1))

    gain = one(*cuts[0])
    for cut in cuts[1:]:
        gain = gain * one(*cut)
    return gain


def centred(key, shape, deviation, limit, cuts=(), held_as=jnp.bfloat16):
    array = deviation * jax.random.normal(key, shape, jnp.float32)
    if cuts:
        array = array * level_of(key, shape, cuts, -0.22, 0.18)
    return jnp.clip(array, -limit, limit).astype(held_as)


def setup_inputs(seed: int = 0) -> dict:
    key_list = jax.random.split(jax.random.key(seed), 13)
    tokens = centred(key_list[0], (TOKENS, MODEL_WIDTH), 1.0, 6.0, ((0, 32),))
    seq_lengths = draw_seq_lengths(jax.random.fold_in(key_list[12], 71), 0)
    gain_attn = jnp.clip(1.0 + 0.1 * jax.random.normal(key_list[2], (MODEL_WIDTH,), jnp.float32), 0.5, 1.5)
    query_weight = centred(key_list[3], (MODEL_WIDTH, QUERY_HEAD_COUNT * HEAD_SIZE), MODEL_WIDTH ** -0.5, 0.15625, ((0, 8), (1, 4)))
    key_matrix = centred(key_list[4], (MODEL_WIDTH, KEY_VALUE_HEADS * HEAD_SIZE), MODEL_WIDTH ** -0.5, 0.15625, ((0, 8), (1, 4)))
    value_matrix = centred(key_list[5], (MODEL_WIDTH, KEY_VALUE_HEADS * HEAD_SIZE), MODEL_WIDTH ** -0.5, 0.15625, ((0, 8), (1, 4)))
    out_weight = centred(key_list[6], (QUERY_HEAD_COUNT * HEAD_SIZE, MODEL_WIDTH), 3 ** -0.5, 3.5, ((0, 4), (1, 8)))
    gain_ffn = jnp.clip(1.0 + 0.1 * jax.random.normal(key_list[7], (MODEL_WIDTH,), jnp.float32), 0.5, 1.5)
    gate_weight = centred(key_list[8], (MODEL_WIDTH, FF), MODEL_WIDTH ** -0.5, 0.15625, ((0, 8), (1, 4)))
    up_weight = centred(key_list[9], (MODEL_WIDTH, FF), MODEL_WIDTH ** -0.5, 0.15625, ((0, 8), (1, 4)))
    down_weight = centred(key_list[10], (FF, MODEL_WIDTH), (FF // 4) ** -0.5, 0.1875, ((0, 4), (1, 8)))
    out_grad = centred(key_list[11], (TOKENS, MODEL_WIDTH), 1.0, 6.0, ((0, 32),))
    return {"tokens": tokens, "seq_lengths": seq_lengths, "gain_attn": gain_attn, "query_weight": query_weight, "key_matrix": key_matrix, "value_matrix": value_matrix, "out_weight": out_weight, "gain_ffn": gain_ffn, "gate_weight": gate_weight, "up_weight": up_weight, "down_weight": down_weight, "out_grad": out_grad}


@jax.custom_vjp
def lower_precision(v):
    return lax.optimization_barrier(v.astype(jnp.bfloat16)).astype(jnp.float32)

@jax.custom_vjp
def low_back(v):
    return v

def low_keep(v):
    return (lower_precision(v), None)

def low_pass(kept, grad):
    return (grad,)

def back_keep(v):
    return (v, None)

def back_low(kept, grad):
    return (lower_precision(grad),)
lower_precision.defvjp(low_keep, low_pass)
low_back.defvjp(back_keep, back_low)
epsilon = 1e-05
rope_base = 100000.0
masked_score = -1e+30

def rms_scale(values, gain_vec):
    factor = lax.rsqrt(lax.optimization_barrier(jnp.mean(values * values, axis=-1, keepdims=True)) + epsilon)
    return values * factor * gain_vec

def layout(lengths, row_len):
    ends_at = jnp.cumsum(lengths).astype(jnp.int32)
    starts_at = (ends_at - lengths).astype(jnp.int32)
    places = lax.iota(jnp.int32, row_len)
    segment_ids = lax.optimization_barrier(jnp.sum((places[:, None] >= ends_at[None, :]).astype(jnp.int32), axis=1)).astype(jnp.int32)
    slot_ids = lax.iota(jnp.int32, lengths.shape[0])
    begins = lax.optimization_barrier(jnp.sum(jnp.where(segment_ids[:, None] == slot_ids[None, :], starts_at[None, :], 0), axis=1)).astype(jnp.int32)
    return (segment_ids, places - begins)

def turning(position, head_width):
    half_width = head_width // 2
    inv_freq = jnp.power(rope_base, -(2.0 * lax.iota(jnp.float32, half_width)) / head_width)
    angles = position.astype(jnp.float32)[:, None] * inv_freq[None, :]
    return (jnp.cos(angles), jnp.sin(angles))

def apply_rotary(values, cosine_table, sine_table):
    half_width = values.shape[-1] // 2
    front_half = values[..., :half_width]
    back_half = values[..., half_width:]
    cos_b = cosine_table[:, None, :]
    sin_b = sine_table[:, None, :]
    return jnp.concatenate([front_half * cos_b - back_half * sin_b, back_half * cos_b + front_half * sin_b], axis=-1)

def attend_packed_row(operands):
    query_rotated, key_rotated, value_activation, segment_ids = operands
    row_len = query_rotated.shape[0]
    rows_per_block = min(512, row_len)
    query_groups = QUERY_HEAD_COUNT // KEY_VALUE_HEADS
    score_scale = HEAD_SIZE ** (-0.5)
    key_places = lax.iota(jnp.int32, row_len)
    highest = lax.Precision.HIGHEST

    def one_block(block_index):
        row_offset = block_index * rows_per_block
        query_block = lax.dynamic_slice_in_dim(query_rotated, row_offset, rows_per_block, 0).reshape(rows_per_block, KEY_VALUE_HEADS, query_groups, HEAD_SIZE)
        seg_blk = lax.dynamic_slice_in_dim(segment_ids, row_offset, rows_per_block, 0)
        scores = jnp.einsum('qgrd,kgd->grqk', query_block, key_rotated, precision=highest) * score_scale
        scores = low_back(scores)
        query_places = row_offset + lax.iota(jnp.int32, rows_per_block)
        allowed = (seg_blk[:, None] == segment_ids[None, :]) & (key_places[None, :] <= query_places[:, None])
        scores = jnp.where(allowed[None, None], scores, masked_score)
        row_peak = lax.optimization_barrier(jnp.max(scores, axis=-1, keepdims=True))
        exp_vals = jnp.exp(scores - row_peak)
        prob_vals = lower_precision(exp_vals / lax.optimization_barrier(jnp.sum(exp_vals, axis=-1, keepdims=True)))
        mixed_blk = jnp.einsum('grqk,kgd->qgrd', prob_vals, value_activation, precision=highest)
        return low_back(lower_precision(mixed_blk)).reshape(rows_per_block, QUERY_HEAD_COUNT * HEAD_SIZE)
    blocks = lax.map(jax.checkpoint(one_block), lax.iota(jnp.int32, row_len // rows_per_block))
    return blocks.reshape(row_len, QUERY_HEAD_COUNT * HEAD_SIZE)

def forward(tokens, gain_attn, query_weight, key_matrix, value_matrix, out_weight, gain_ffn, gate_weight, up_weight, down_weight, segment_ids, position):
    highest = lax.Precision.HIGHEST
    normed = lower_precision(rms_scale(tokens, gain_attn))
    query_lin = low_back(jnp.dot(normed, query_weight, precision=highest))
    key_linear = low_back(jnp.dot(normed, key_matrix, precision=highest))
    value_activation = lower_precision(low_back(jnp.dot(normed, value_matrix, precision=highest)))
    cosine_table, sine_table = turning(position.reshape(-1), HEAD_SIZE)
    query_rotated = lower_precision(apply_rotary(query_lin.reshape(-1, QUERY_HEAD_COUNT, HEAD_SIZE), cosine_table, sine_table))
    key_rotated = lower_precision(apply_rotary(key_linear.reshape(-1, KEY_VALUE_HEADS, HEAD_SIZE), cosine_table, sine_table))
    attended_values = lax.map(attend_packed_row, (query_rotated.reshape(N_DP, PACKED_ROW_TOKENS, QUERY_HEAD_COUNT, HEAD_SIZE), key_rotated.reshape(N_DP, PACKED_ROW_TOKENS, KEY_VALUE_HEADS, HEAD_SIZE), value_activation.reshape(N_DP, PACKED_ROW_TOKENS, KEY_VALUE_HEADS, HEAD_SIZE), segment_ids))
    attended_values = attended_values.reshape(-1, QUERY_HEAD_COUNT * HEAD_SIZE)
    branch = low_back(jnp.dot(attended_values, out_weight, precision=highest))
    middle = tokens + branch
    normed_two = lower_precision(rms_scale(middle, gain_ffn))
    gate_lin = low_back(jnp.dot(normed_two, gate_weight, precision=highest))
    up_lin = low_back(jnp.dot(normed_two, up_weight, precision=highest))
    hidden = lower_precision(jax.nn.silu(gate_lin) * up_lin)
    return middle + low_back(jnp.dot(hidden, down_weight, precision=highest))

def reference(tokens, seq_lengths, gain_attn, query_weight, key_matrix, value_matrix, out_weight, gain_ffn, gate_weight, up_weight, down_weight, out_grad):
    segment_ids, position = jax.vmap(lambda lengths: layout(lengths, PACKED_ROW_TOKENS))(seq_lengths)
    floats = (tokens.astype(jnp.float32), gain_attn.astype(jnp.float32), query_weight.astype(jnp.float32), key_matrix.astype(jnp.float32), value_matrix.astype(jnp.float32), out_weight.astype(jnp.float32), gain_ffn.astype(jnp.float32), gate_weight.astype(jnp.float32), up_weight.astype(jnp.float32), down_weight.astype(jnp.float32))

    def closed(*weights):
        return forward(*weights, segment_ids, position)
    mixed_out, pull_back = jax.vjp(closed, *floats)
    gradients = pull_back(out_grad.astype(jnp.float32))
    return (mixed_out.astype(jnp.bfloat16), gradients[0], gradients[1], gradients[2], gradients[3], gradients[4], gradients[5], gradients[6], gradients[7], gradients[8], gradients[9])
```

```python
import functools

import jax
import jax.numpy as jnp
import numpy as np
from jax import lax
from jax.experimental import pallas as pl
from jax.experimental.pallas import tpu as pltpu
from jax.sharding import PartitionSpec as P

HEAD = 96
LANES = 128
EPS = 1e-05
ROPE_BASE = 100000.0
LOG2E = 1.4426950408889634
LN2 = 0.6931471805599453
BF = jnp.bfloat16
F32 = jnp.float32
MESH = pl.DeviceIdType.MESH
rem, div = lax.rem, lax.div

NN = (((1,), (0,)), ((), ()))
NT = (((1,), (1,)), ((), ()))
TN = (((0,), (0,)), ((), ()))


def dot(a, b, dims):
    return lax.dot_general(a, b, dims, preferred_element_type=F32)


class Sizes:
    def __init__(self, n_dp, n_tensor, rows, width, q_cols, k_cols, hidden):
        self.N, self.T, self.R, self.D = n_dp, n_tensor, rows, width
        self.PZ = n_dp // 2
        self.H = n_tensor // 2
        self.L = rows * n_tensor
        self.S = width // n_dp
        self.F = hidden
        self.nq, self.nk = q_cols // HEAD, k_cols // HEAD
        self.G = self.nq // self.nk
        self.nh = self.nq + 2 * self.nk
        self.HA, self.PA = self.nh * HEAD, self.nh * LANES
        self.HQ, self.PQ = self.nq * HEAD, self.nq * LANES
        self.HO = -(-self.HQ // LANES) * LANES
        self.cols = (self.HA, self.HO, hidden, hidden, hidden)


def scratch_list(z):
    dma = pltpu.SemaphoreType.DMA
    items = [
        ("xv", pltpu.VMEM((z.R, z.D), BF)),
        ("normed", pltpu.VMEM((z.L, z.D), BF)),
        ("ogr", pltpu.VMEM((z.L, z.D), BF)),
        ("n2", pltpu.VMEM((z.L, z.D), BF)),
        ("part", pltpu.VMEM((z.L, z.D), BF)),
        ("rbuf_a", pltpu.VMEM((2, 2 * z.H - 1, z.R // 2, z.D), BF)),
        ("w0", pltpu.VMEM((z.D, z.cols[0]), BF)),
        ("w1", pltpu.VMEM((z.D, z.cols[1]), BF)),
        ("w2", pltpu.VMEM((z.D, z.cols[2]), BF)),
        ("w3", pltpu.VMEM((z.D, z.cols[3]), BF)),
        ("w4", pltpu.VMEM((z.D, z.cols[4]), BF)),
        ("perm", pltpu.VMEM((4 * HEAD, 4 * LANES), BF)),
        ("cos", pltpu.VMEM((z.L, LANES), F32)),
        ("sin", pltpu.VMEM((z.L, LANES), F32)),
        ("q4", pltpu.VMEM((z.nk, z.T, z.G * z.R, LANES), BF)),
        ("kk", pltpu.VMEM((z.nk, z.L, LANES), BF)),
        ("vv", pltpu.VMEM((z.nk, z.L, LANES), BF)),
        ("o4", pltpu.VMEM((z.nk, z.T, z.G * z.R, LANES), BF)),
        ("do4", pltpu.VMEM((z.nk, z.T, z.G * z.R, LANES), BF)),
        ("lse", pltpu.VMEM((z.nk, z.T, 8, z.G * z.R), F32)),
        ("dlt", pltpu.VMEM((z.nk, z.T, 8, z.G * z.R), F32)),
        ("middle", pltpu.VMEM((z.R, z.D), F32)),
        ("mgrad", pltpu.VMEM((z.R, z.D), F32)),
        ("gsum", pltpu.VMEM((2, z.D), F32)),
        ("gs", pltpu.VMEM((2, 8, z.D), F32)),
        ("gz", pltpu.VMEM((z.PZ, 8, z.D), F32)),
        ("gt", pltpu.VMEM((z.T, 8, z.D), F32)),
        ("s_loc", dma((16,))),
        ("s_agS", dma((4, 2, z.H + 1, 2))),
        ("s_agR", dma((4, 2, z.H + 1, 2))),
        ("s_rsS", dma((4, 2, z.H + 1, 2))),
        ("s_rsR", dma((4, 2, z.H + 1, 2))),
        ("s_zgS", dma((5, 2, z.PZ + 1))),
        ("s_zgR", dma((5, 2, z.PZ + 1))),
        ("s_sgS", dma((5, 2, z.PZ + 1))),
        ("s_sgR", dma((5, 2, z.PZ + 1))),
        ("s_zrS", dma((5, 2, z.PZ))),
        ("s_zrR", dma((5, 2, z.PZ))),
        ("s_srS", dma((5, z.PZ))),
        ("s_srR", dma((5, z.PZ))),
        ("s_free", pltpu.SemaphoreType.REGULAR((2,))),
        ("s_gS", dma((3, max(z.T, z.PZ)))),
        ("s_gR", dma((3, max(z.T, z.PZ)))),
    ]
    if z.T <= 4:
        items.append(("rbuf_b", pltpu.VMEM((2, 2 * z.H - 1, z.R // 2, z.D), BF)))
    for w in range(5):
        items.append((f"sib{w}", pltpu.VMEM((z.PZ, z.S, z.cols[w]), BF)))
        items.append((f"lin{w}", pltpu.VMEM((z.PZ + 1, z.S, z.cols[w]), BF)))
    return items


class Ring:
    def __init__(self, z):
        self.z = z
        self.dp = lax.axis_index("dp")
        t = lax.axis_index("tensor")
        self.t = t
        ycount = z.T // 2
        x, y = rem(t, 2), div(t, 2)
        self.r = y * (1 - x) + (z.T - 1 - y) * x
        self.ycount = ycount
        self.to = ((self.dp, self.index(1)), (self.dp, self.index(-1)))

    def index(self, step):
        z = self.z
        r = rem(self.r + step + z.T, z.T)
        far = div(r, self.ycount)
        return (1 - far) * 2 * r + far * (2 * (z.T - 1 - r) + 1)

    def off(self, step):
        return pl.multiple_of(self.index(step) * self.z.R, self.z.R)


class Gather:
    def __init__(self, ring, buf, s_send, s_recv):
        self.ring, self.buf, self.ss, self.rs = ring, buf, s_send, s_recv
        self.half = ring.z.R // 2

    def last(self, d, h):
        return self.ring.z.H if h == d else self.ring.z.H - 1

    def copy(self, d, k, h):
        sign = -1 if d == 0 else 1
        origin = self.ring.off(sign * (k - 1))
        piece = self.buf.at[pl.ds(pl.multiple_of(origin + h * self.half, self.half), self.half)]
        return pltpu.make_async_remote_copy(
            src_ref=piece, dst_ref=piece, send_sem=self.ss.at[d, k, h], recv_sem=self.rs.at[d, k, h],
            device_id=self.ring.to[d], device_id_type=MESH,
        )

    def start(self):
        for same in (True, False):
            for d in (0, 1):
                h = d if same else 1 - d
                if self.last(d, h) >= 1:
                    self.copy(d, 1, h).start()

    def step(self, k, same):
        for d in (0, 1):
            h = d if same else 1 - d
            if k <= self.last(d, h):
                self.copy(d, k, h).wait_recv()
                if k + 1 <= self.last(d, h):
                    self.copy(d, k + 1, h).start()

    def finish(self):
        for d in (0, 1):
            for h in (0, 1):
                for k in range(1, self.last(d, h) + 1):
                    self.copy(d, k, h).wait_send()


class Scatter:
    def __init__(self, ring, buf, rbuf, s_send, s_recv):
        self.ring, self.buf, self.rbuf, self.ss, self.rs = ring, buf, rbuf, s_send, s_recv
        self.half = ring.z.R // 2

    def piece(self, step, h):
        off = self.ring.off(step)
        return self.buf.at[pl.ds(pl.multiple_of(off + h * self.half, self.half), self.half)]

    def copy(self, d, k, h):
        dist = self.ring.z.H - k + 1
        return pltpu.make_async_remote_copy(
            src_ref=self.piece(dist if d == 0 else -dist, h), dst_ref=self.rbuf.at[d, self.slot(d, k, h)],
            send_sem=self.ss.at[d, k, h], recv_sem=self.rs.at[d, k, h],
            device_id=self.ring.to[d], device_id_type=MESH,
        )

    def first(self, d, h):
        return 1 if h == d else 2

    def slot(self, d, k, h):
        return k - 1 if h == d else self.ring.z.H + k - 2

    def send(self, k, same):
        for d in (0, 1):
            h = d if same else 1 - d
            if k < self.first(d, h):
                continue
            if k > self.first(d, h):
                self.copy(d, k - 1, h).wait_recv()
                dist = self.ring.z.H - k + 1
                piece = self.piece(dist if d == 0 else -dist, h)
                add_into(piece, self.rbuf.at[d, self.slot(d, k - 1, h)])
            self.copy(d, k, h).start()

    def arrive(self):
        for h in (0, 1):
            for d in (0, 1):
                if self.ring.z.H >= self.first(d, h):
                    self.copy(d, self.ring.z.H, h).wait_recv()

    def rows(self, lo, n):
        h = div(lo, self.half)
        last = self.ring.z.H - 1
        off = lo - h * self.half
        own = pl.ds(pl.multiple_of(self.ring.off(0) + lo, n), n)
        total = self.buf[own, :].astype(F32)
        for d in (0, 1):
            total = total + self.rbuf[d, last + last * (h if d == 0 else 1 - h), pl.ds(pl.multiple_of(off, n), n), :].astype(F32)
        return total

    def finish(self):
        for d in (0, 1):
            for h in (0, 1):
                for k in range(self.first(d, h), self.ring.z.H + 1):
                    self.copy(d, k, h).wait_send()


def add_into(dst, src):
    rows = dst.shape[0]
    step = 32

    def body(i, _):
        at = pl.ds(pl.multiple_of(i * step, step), step)
        dst[at, :] = (dst[at, :].astype(F32) + src[at, :].astype(F32)).astype(dst.dtype)
        return 0

    lax.fori_loop(0, rows // step, body, 0)


class Line:
    def __init__(self, z, s, ws):
        self.z, self.s, self.ws = z, s, ws
        dp, t = lax.axis_index("dp"), lax.axis_index("tensor")
        self.t = t
        self.p, self.c = div(dp, 2), rem(dp, 2)
        self.right = (dp + 2, t)
        self.left = (dp - 2, t)
        self.sibling = (dp + 1 - 2 * self.c, t)

    def shard(self, w, q, core):
        return self.ws[w].at[pl.ds(pl.multiple_of((2 * q + core) * self.z.S, self.z.S), self.z.S)]

    def ag_copy(self, w, side, h, where):
        q = self.p - h if side == 0 else self.p + h
        src = self.shard(w, q, self.c)
        s = self.s
        if where == "line":
            return pltpu.make_async_remote_copy(
                src_ref=src, dst_ref=src, send_sem=s.s_zgS.at[w, side, h], recv_sem=s.s_zgR.at[w, side, h + 1],
                device_id=self.right if side == 0 else self.left, device_id_type=MESH,
            )
        return pltpu.make_async_remote_copy(
            src_ref=src, dst_ref=src, send_sem=s.s_sgS.at[w, side, h], recv_sem=s.s_sgR.at[w, side, h],
            device_id=self.sibling, device_id_type=MESH,
        )

    def ag_has(self, side, h):
        return self.p >= h if side == 0 else self.p + h <= self.z.PZ - 1

    def ag_passes(self, side):
        return self.p < self.z.PZ - 1 if side == 0 else self.p > 0

    def ag_step(self, w, h):
        for side in (0, 1):
            @pl.when(self.ag_has(side, h))
            def _(side=side):
                if h > 0:
                    self.ag_arrival(w, side, h).wait_recv()

                @pl.when(self.ag_passes(side))
                def _():
                    self.ag_copy(w, side, h, "line").start()

                if h > 0 or side == 0:
                    self.ag_copy(w, side, h, "sib").start()

    def ag_arrival(self, w, side, h):
        src = self.shard(w, self.p, self.c)
        return pltpu.make_async_remote_copy(
            src_ref=src, dst_ref=src, send_sem=self.s.s_zgS.at[w, side, h], recv_sem=self.s.s_zgR.at[w, side, h],
            device_id=self.sibling, device_id_type=MESH,
        )

    def ag_drain(self, w):
        for h in range(self.z.PZ):
            for side in (0, 1):
                if h > 0 or side == 0:
                    @pl.when(self.ag_has(side, h))
                    def _(side=side, h=h):
                        self.ag_copy(w, side, h, "sib").wait_recv()

    def ag_finish(self, w):
        for h in range(self.z.PZ):
            for side in (0, 1):
                @pl.when(self.ag_has(side, h))
                def _(side=side, h=h):
                    @pl.when(self.ag_passes(side))
                    def _():
                        self.ag_copy(w, side, h, "line").wait_send()

                    if h > 0 or side == 0:
                        self.ag_copy(w, side, h, "sib").wait_send()

    def rs_sib_copy(self, w, q):
        return pltpu.make_async_remote_copy(
            src_ref=self.shard(w, q, 1 - self.c), dst_ref=getattr(self.s, f"sib{w}").at[q],
            send_sem=self.s.s_srS.at[w, q], recv_sem=self.s.s_srR.at[w, q],
            device_id=self.sibling, device_id_type=MESH,
        )

    def rs_sib_start(self, w):
        for q in range(self.z.PZ):
            self.rs_sib_copy(w, q).start()

    def rs_sib_sum(self, w):
        for q in range(self.z.PZ):
            self.rs_sib_copy(w, q).wait_recv()
            add_into(self.shard(w, q, self.c), getattr(self.s, f"sib{w}").at[q])

    def rs_copy(self, w, side, q):
        slot = q + 1 if side == 0 else q
        return pltpu.make_async_remote_copy(
            src_ref=self.shard(w, q, self.c), dst_ref=getattr(self.s, f"lin{w}").at[slot],
            send_sem=self.s.s_zrS.at[w, side, q], recv_sem=self.s.s_zrR.at[w, side, q],
            device_id=self.right if side == 0 else self.left, device_id_type=MESH,
        )

    def rs_step(self, w, k):
        p, last = self.p, self.z.PZ - 1
        lin = getattr(self.s, f"lin{w}")
        for side, q in ((0, last - k), (1, k)):
            inside = (p > 0) & (p < q) if side == 0 else (p < last) & (p > q)
            sends = p < q if side == 0 else p > q

            @pl.when(inside)
            def _(side=side, q=q):
                self.rs_copy(w, side, q).wait_recv()
                add_into(self.shard(w, q, self.c), lin.at[q + 1 if side == 0 else q])

            @pl.when(sends)
            def _(side=side, q=q):
                self.rs_copy(w, side, q).start()

    def rs_final(self, w, out_vmem):
        p, last = self.p, self.z.PZ - 1
        lin = getattr(self.s, f"lin{w}")
        own = self.shard(w, p, self.c)
        cols = self.z.cols[w]
        out = out_vmem.at[:, pl.ds(0, cols)]
        copy_f32(out, own)

        @pl.when(p > 0)
        def _():
            self.rs_copy(w, 0, p).wait_recv()
            add_into(out, lin.at[p + 1])

        @pl.when(p < last)
        def _():
            self.rs_copy(w, 1, p).wait_recv()
            add_into(out, lin.at[p])

    def rs_finish(self, w):
        p = self.p
        for q in range(self.z.PZ):
            self.rs_sib_copy(w, q).wait_send()
            if q > 0:
                @pl.when(p < q)
                def _(q=q):
                    self.rs_copy(w, 0, q).wait_send()
            if q < self.z.PZ - 1:
                @pl.when(p > q)
                def _(q=q):
                    self.rs_copy(w, 1, q).wait_send()


def copy_f32(dst, src):
    rows = dst.shape[0]
    step = 32

    def body(i, _):
        at = pl.ds(pl.multiple_of(i * step, step), step)
        dst[at, :] = src[at, :].astype(F32)
        return 0

    lax.fori_loop(0, rows // step, body, 0)


def kernel(z, names, *refs):
    (x_hbm, og_hbm, len_ref, ga_ref, gf_ref, freq_ref, *rest) = refs
    w_hbm, rest = rest[:5], rest[5:]
    mixed_hbm, tg_hbm, gain_out, *rest = rest
    o_hbm, rest = rest[:5], rest[5:]

    class Scratch:
        pass

    s = Scratch()
    for name, ref in zip(names, rest, strict=True):
        setattr(s, name, ref)
    ws = (s.w0, s.w1, s.w2, s.w3, s.w4)
    s.mid, s.dqkv = s.n2, s.ogr
    one_rbuf = not hasattr(s, "rbuf_b")
    if one_rbuf:
        s.rbuf_b = s.rbuf_a
    R, D, L, F, T = z.R, z.D, z.L, z.F, z.T
    ring = Ring(z)
    line = Line(z, s, ws)
    dp, t, p, c = ring.dp, ring.t, line.p, line.c
    own_off = pl.multiple_of(t * R, R)
    own_rows = pl.ds(own_off, R)

    loc = [pltpu.make_async_copy(x_hbm, s.xv, s.s_loc.at[0]),
           pltpu.make_async_copy(og_hbm, s.ogr.at[own_rows], s.s_loc.at[1])]
    for w in range(5):
        loc.append(pltpu.make_async_copy(w_hbm[w], line.shard(w, p, c), s.s_loc.at[2 + w]))
    for cp in loc:
        cp.start()

    bar = pltpu.get_barrier_semaphore()
    peers = [line.sibling]
    peers += [(rem(p + d, z.PZ) * 2 + c, t) for d in range(1, z.PZ)]
    peers += [(dp, rem(t + d, T)) for d in range(1, T)]
    for peer in peers:
        pl.semaphore_signal(bar, 1, device_id=peer, device_id_type=MESH)
    pl.semaphore_wait(bar, len(peers))

    loc[2].wait()
    line.ag_step(0, 0)

    loc[0].wait()
    NR = 32

    def norm_rows(i, _):
        at = pl.ds(pl.multiple_of(i * NR, NR), NR)
        x = s.xv[at, :].astype(F32)
        f = lax.rsqrt(jnp.mean(x * x, axis=-1, keepdims=True) + EPS)
        s.normed[pl.ds(pl.multiple_of(own_off + i * NR, NR), NR), :] = (x * f * ga_ref[...]).astype(BF)
        return 0

    lax.fori_loop(0, R // NR, norm_rows, 0)
    ag_x = Gather(ring, s.normed, s.s_agS.at[0], s.s_agR.at[0])
    ag_x.start()
    loc[3].wait()
    line.ag_step(1, 0)

    l0 = len_ref[0, 0]
    lane = lax.broadcasted_iota(jnp.int32, (R, LANES), 1)

    def table_rows(i, _):
        at = pl.ds(pl.multiple_of(i * R, R), R)
        place = lax.broadcasted_iota(jnp.int32, (R, LANES), 0) + i * R
        pos = place - jnp.where(place >= l0, l0, 0)
        ang = pos.astype(F32) * freq_ref[...]
        s.cos[at, :] = jnp.cos(ang)
        sn = jnp.sin(ang)
        s.sin[at, :] = jnp.where(lane < 64, -sn, sn)
        return 0

    lax.fori_loop(0, T, table_rows, 0)
    half = HEAD // 2
    rowi = lax.broadcasted_iota(jnp.int32, (4 * HEAD, LANES), 0)
    coli = lax.broadcasted_iota(jnp.int32, (4 * HEAD, LANES), 1)
    inside = (coli < half) | ((coli >= 64) & (coli < 64 + half))
    src = jnp.where(inside, jnp.where(coli < half, coli, coli - (64 - half)), -100 * HEAD)
    for h in range(4):
        s.perm[:, h * LANES:(h + 1) * LANES] = jnp.where(rowi == src + h * HEAD, 1.0, 0.0).astype(BF)

    line.ag_step(0, 1)
    ag_x.step(1, True)
    line.ag_step(1, 1)
    loc[4].wait()
    line.ag_step(2, 0)
    line.ag_step(0, 2) if z.PZ > 2 else None
    loc[1].wait()
    ag_og = Gather(ring, s.ogr, s.s_agS.at[1], s.s_agR.at[1])
    if z.H == 2:
        ag_og.start()
    ag_x.step(1, False)

    todo = []
    for tau in range(5 + z.PZ):
        for w in range(5):
            h = tau - w
            if 0 <= h < z.PZ:
                todo.append((w, h))
    for done in ((0, 0), (0, 1), (1, 0), (1, 1), (2, 0), (0, 2)):
        if done in todo:
            todo.remove(done)
    drained = [False] * 5

    def pump(n=1):
        for _ in range(n):
            if todo:
                w, h = todo.pop(0)
                if h == 0:
                    loc[2 + w].wait()
                line.ag_step(w, h)

    def drain(w):
        while any(a == w for a, _ in todo):
            pump()
        if not drained[w]:
            line.ag_drain(w)
            drained[w] = True

    drain(0)

    wp = s.part
    for quad in range(z.nh // 4):
        wp[quad * 4 * LANES:(quad + 1) * 4 * LANES, :] = dot(
            s.perm[...], s.w0[:, quad * 4 * HEAD:(quad + 1) * 4 * HEAD], (((0,), (1,)), ((), ()))
        ).astype(BF)
    qscale = HEAD ** -0.5 * LOG2E

    def qkv(step):
        off = ring.off(step)
        blk = ring.index(step)
        a = s.normed[pl.ds(off, R), :]
        cs, sn = s.cos[pl.ds(off, R), :], s.sin[pl.ds(off, R), :]
        for h in range(z.nh):
            if h % 2 == 0:
                y2 = dot(a, wp[h * LANES:(h + 2) * LANES, :], NT)
            y = y2[:, (h % 2) * LANES:(h % 2 + 1) * LANES]
            if h < z.nq:
                g, j = h // z.G, h % z.G
                rot = (y * cs + pltpu.roll(y, 64, 1) * sn) * qscale
                s.q4[g, blk, j * R:(j + 1) * R, :] = rot.astype(BF)
            elif h < z.nq + z.nk:
                rot = y * cs + pltpu.roll(y, 64, 1) * sn
                s.kk[h - z.nq, pl.ds(off, R), :] = rot.astype(BF)
            else:
                s.vv[h - z.nq - z.nk, pl.ds(off, R), :] = y.astype(BF)

    qkv(0)
    for k in range(1, z.H):
        if k > 1:
            ag_x.step(k, True)
            ag_x.step(k, False)
        qkv(k)
        qkv(-k)
        pump()
    ag_x.step(z.H, True)
    qkv(z.H)
    if z.H != 2:
        ag_og.start()

    def row_form(col):
        wide = jnp.broadcast_to(col, (col.shape[0], LANES))
        return jnp.transpose(wide)[0:8, :]

    def attend(qb):
        K = (qb + 1) * R
        rows = lax.broadcasted_iota(jnp.int32, (R, 1), 0) + qb * R
        begin = jnp.where(rows >= l0, l0, 0)

        def one(i, _):
            g, j = div(i, z.G), rem(i, z.G)
            at = pl.ds(pl.multiple_of(j * R, R), R)
            q = s.q4[g, qb, at, :]
            sc = dot(q, s.kk[g, 0:K, :], NT)
            keys = lax.broadcasted_iota(jnp.int32, (R, K), 1)
            sc = jnp.where((keys >= begin) & (keys <= rows), sc, -1e30)
            m = jnp.max(sc, axis=-1, keepdims=True)
            e = jnp.exp2(sc - m)
            tot = jnp.sum(e, axis=-1, keepdims=True)
            o = dot(e.astype(BF), s.vv[g, 0:K, :], NN) / tot
            s.o4[g, qb, at, :] = o.astype(BF)
            s.lse[g, qb, :, at] = row_form(m + jnp.log2(tot))
            return 0

        lax.fori_loop(0, z.nq, one, 0)

    hops = [(k, same) for k in range(1, z.H + 1) for same in (True, False)]
    for qb in range(T):
        attend(qb)
        pump(2)
        if hops and qb >= 1:
            ag_og.step(*hops.pop(0))

    drain(1)
    ag_x.finish()
    rs_o = Scatter(ring, s.part, s.rbuf_a, s.s_rsS.at[0], s.s_rsR.at[0])
    NB = 768

    def out_block(step):
        off, blk = ring.off(step), ring.index(step)
        pads = [s.o4[h // z.G, blk, (h % z.G) * R:(h % z.G + 1) * R, :] for h in range(z.nq)]
        a = dot(jnp.concatenate(pads, axis=1), s.perm[0:z.HQ, 0:z.PQ], NT).astype(BF)

        def cols(n, _):
            at = pl.ds(pl.multiple_of(n * NB, NB), NB)
            s.part[pl.ds(off, R), at] = dot(a, s.w1[at, 0:z.HQ], NT).astype(BF)
            return 0

        lax.fori_loop(0, D // NB, cols, 0)

    def scatter(rs, block, between=None):
        for k in range(1, z.H + 1):
            dist = z.H - k + 1
            block(dist)
            if k > 1:
                block(-dist)
                rs.send(k, False)
            rs.send(k, True)
            if between is not None:
                between(k)
        block(0)

    for hop in hops:
        ag_og.step(*hop)

    def between_o(k):
        pump(1)

    scatter(rs_o, out_block, between_o)
    rs_o.arrive()

    def middle_rows(i, _):
        lo = i * NR
        at = pl.ds(pl.multiple_of(lo, NR), NR)
        m = s.xv[at, :].astype(F32) + rs_o.rows(lo, NR)
        s.middle[at, :] = m
        f = lax.rsqrt(jnp.mean(m * m, axis=-1, keepdims=True) + EPS)
        s.n2[pl.ds(pl.multiple_of(own_off + lo, NR), NR), :] = (m * f * gf_ref[...]).astype(BF)
        return 0

    lax.fori_loop(0, R // NR, middle_rows, 0)
    ag_n2 = Gather(ring, s.n2, s.s_agS.at[2], s.s_agR.at[2])
    ag_n2.start()
    ag_og.finish()

    ag_m = Gather(ring, s.mid, s.s_agS.at[3], s.s_agR.at[3])
    rs_n = Scatter(ring, s.part, s.rbuf_a, s.s_rsS.at[1], s.s_rsR.at[1])
    rs_f = Scatter(ring, s.part, s.rbuf_b, s.s_rsS.at[2], s.s_rsR.at[2])
    FB = 512

    def free(i):
        for d in (0, 1):
            pl.semaphore_signal(s.s_free.at[i], 1, device_id=ring.to[d], device_id_type=MESH)

    def await_free(i):
        pl.semaphore_wait(s.s_free.at[i], 2)

    def ffn_phase(gl, ul, hid):
        def gate_up(step):
            rows = pl.ds(ring.off(step), R)

            def cols(n, _):
                at = pl.ds(pl.multiple_of(n * FB, FB), FB)
                a = s.n2[rows, :]
                g = dot(a, s.w2[:, at], NN)
                u = dot(a, s.w3[:, at], NN)
                gl[rows, at] = g.astype(BF)
                ul[rows, at] = u.astype(BF)
                hid[rows, at] = (g / (1.0 + jnp.exp(-g)) * u).astype(BF)
                return 0

            lax.fori_loop(0, F // FB, cols, 0)

        drain(2)
        ag_n2.step(1, True)
        drain(3)
        gate_up(0)
        pump(1)
        ag_n2.step(1, False)
        for k in range(1, z.H):
            if k > 1:
                ag_n2.step(k, True)
                ag_n2.step(k, False)
            gate_up(k)
            gate_up(-k)
        pump(1)
        ag_n2.step(z.H, True)
        gate_up(z.H)
        drain(4)
        rs_o.finish()

        def act_grads(step):
            rows = pl.ds(ring.off(step), R)

            def cols(n, _):
                at = pl.ds(pl.multiple_of(n * FB, FB), FB)
                hg = dot(s.ogr[rows, :], s.w4[:, at], NN)
                g = gl[rows, at].astype(F32)
                u = ul[rows, at].astype(F32)
                sg = 1.0 / (1.0 + jnp.exp(-g))
                silu = g * sg
                gl[rows, at] = (hg * u * (sg + silu * (1.0 - sg))).astype(BF)
                ul[rows, at] = (hg * silu).astype(BF)
                return 0

            lax.fori_loop(0, F // FB, cols, 0)

            def back(n, _):
                at = pl.ds(pl.multiple_of(n * NB, NB), NB)
                s.part[rows, at] = (
                    dot(gl[rows, :], s.w2[at, :], NT) + dot(ul[rows, :], s.w3[at, :], NT)
                ).astype(BF)
                return 0

            lax.fori_loop(0, D // NB, back, 0)

        scatter(rs_n, act_grads)

        def wgrad(w, rows_ref, act_ref):
            line.ag_finish(w)
            DB = 512

            def tile(i, _):
                at = pl.ds(pl.multiple_of(i * DB, DB), DB)
                ws[w][at, :] = dot(rows_ref[:, at], act_ref[...], TN).astype(BF)
                return 0

            lax.fori_loop(0, D // DB, tile, 0)
            line.rs_sib_start(w)

        wgrad(2, s.n2, gl)
        line.rs_sib_sum(2)
        line.rs_step(2, 0)
        wgrad(3, s.n2, ul)
        ag_n2.finish()
        free(0)
        line.rs_sib_sum(3)
        line.rs_step(2, 1) if z.PZ > 2 else None
        line.rs_step(3, 0)
        rs_n.arrive()

        s.gsum[...] = jnp.zeros_like(s.gsum)

        def norm_back(i, _):
            lo = i * NR
            at = pl.ds(pl.multiple_of(lo, NR), NR)
            ng = rs_n.rows(lo, NR)
            m = s.middle[at, :]
            f = lax.rsqrt(jnp.mean(m * m, axis=-1, keepdims=True) + EPS)
            zz = m * f
            s.gsum[0:1, :] += jnp.sum(ng * zz, axis=0, keepdims=True)
            dz = ng * gf_ref[...]
            own = pl.ds(pl.multiple_of(own_off + lo, NR), NR)
            mg = s.ogr[own, :].astype(F32) + f * (dz - zz * jnp.mean(dz * zz, axis=-1, keepdims=True))
            s.mgrad[at, :] = mg
            s.mid[own, :] = mg.astype(BF)
            return 0

        lax.fori_loop(0, R // NR, norm_back, 0)
        rs_n.finish()
        await_free(0)
        ag_m.start()

        def down_block(step):
            rows = pl.ds(ring.off(step), R)

            def cols(n, _):
                at = pl.ds(pl.multiple_of(n * NB, NB), NB)
                s.part[rows, at] = dot(hid[rows, :], s.w4[at, :], NT).astype(BF)
                return 0

            lax.fori_loop(0, D // NB, cols, 0)

        for k in range(1, z.H + 1):
            down_block(k)
            if k < z.H:
                down_block(-k)
        down_block(0)
        ag_m.step(1, True)
        line.rs_step(2, 2) if z.PZ > 3 else None
        line.rs_step(3, 1) if z.PZ > 2 else None
        wgrad(4, s.ogr, hid)
        line.rs_sib_sum(4)
        line.rs_step(4, 0)

    pl.run_scoped(ffn_phase, pltpu.VMEM((L, F), BF), pltpu.VMEM((L, F), BF), pltpu.VMEM((L, F), BF))

    done = {(2, 0), (2, 1), (2, 2), (3, 0), (3, 1), (4, 0)}
    left = [(w, k) for k in range(z.PZ - 1) for w in (2, 3, 4) if (w, k) not in done]
    left.sort(key=lambda e: (e[0] + 1.5 * e[1], e[1]))

    def rs_pump(n=1):
        for _ in range(n):
            if left:
                line.rs_step(*left.pop(0))

    def do_block(step):
        off, blk = ring.off(step), ring.index(step)
        a = dot(s.mid[pl.ds(off, R), :], s.w1[:, 0:z.HQ], NN).astype(BF)
        d = dot(a, s.perm[0:z.HQ, 0:z.PQ], NN)
        for h in range(z.nq):
            g, j = h // z.G, h % z.G
            dh = d[:, h * LANES:(h + 1) * LANES]
            at = pl.ds(j * R, R)
            s.do4[g, blk, at, :] = dh.astype(BF)
            dl = jnp.sum(dh * s.o4[g, blk, at, :].astype(F32), axis=-1, keepdims=True)
            s.dlt[g, blk, :, at] = row_form(dl)

    do_block(0)
    for k in range(1, z.H):
        if k > 1:
            ag_m.step(k, True)
        ag_m.step(k, False)
        do_block(k)
        do_block(-k)
    ag_m.step(z.H, True)
    do_block(z.H)

    rs_f.send(1, True)
    rs_f_steps = [(k, same) for k in range(2, z.H + 1) for same in (False, True)]

    def back_phase(dq, dk, dv, att):
        dk[...] = jnp.zeros_like(dk)
        dv[...] = jnp.zeros_like(dv)
        dq[...] = jnp.zeros_like(dq)
        GR = z.G * R

        def back_block(qb):
            def pair(i, _):
                g, kb = div(i, qb + 1), rem(i, qb + 1)
                at = pl.ds(pl.multiple_of(kb * R, R), R)
                q, do = s.q4[g, qb], s.do4[g, qb]
                kk, vv = s.kk[g, at, :], s.vv[g, at, :]
                st = dot(kk, q, NT)
                keys = lax.broadcasted_iota(jnp.int32, (R, GR), 0) + kb * R
                qs = rem(lax.broadcasted_iota(jnp.int32, (1, GR), 1), R) + qb * R
                begin = jnp.where(qs >= l0, l0, 0)
                e = jnp.exp2(st - s.lse[g, qb, 0:1, :])
                pt = jnp.where((keys >= begin) & (keys <= qs), e, 0.0)
                dpt = dot(vv, do, NT)
                ds = (pt * (dpt - s.dlt[g, qb, 0:1, :])).astype(BF)
                dv[g, at, :] += dot(pt.astype(BF), do, NN)
                dk[g, at, :] += dot(ds, q, NN)
                dq[g, qb] += dot(ds, kk, TN)
                return 0

            lax.fori_loop(0, z.nk * (qb + 1), pair, 0)

        for qb in range(T):
            back_block(qb)
            if qb >= 1:
                rs_pump(1)
            if rs_f_steps:
                rs_f.send(*rs_f_steps.pop(0))

        line.ag_finish(1)
        DB = 512

        def unpad(i, _):
            pads = [s.o4[h // z.G, i, (h % z.G) * R:(h % z.G + 1) * R, :] for h in range(z.nq)]
            att[pl.ds(pl.multiple_of(i * R, R), R), :] = dot(
                jnp.concatenate(pads, axis=1), s.perm[0:z.HQ, 0:z.PQ], NT
            ).astype(BF)
            return 0

        lax.fori_loop(0, T, unpad, 0)

        def tile(i, _):
            at = pl.ds(pl.multiple_of(i * DB, DB), DB)
            s.w1[at, 0:z.HQ] = dot(s.mid[:, at], att[...], TN).astype(BF)
            return 0

        lax.fori_loop(0, D // DB, tile, 0)
        line.rs_sib_start(1)

        def unrotate(i, _):
            rows = pl.ds(pl.multiple_of(i * R, R), R)
            cs, sn = s.cos[rows, :], s.sin[rows, :]
            heads = []
            for h in range(z.nh):
                if h < z.nq:
                    v = dq[h // z.G, i, (h % z.G) * R:(h % z.G + 1) * R, :] * (HEAD ** -0.5)
                    v = v * cs - pltpu.roll(v, 64, 1) * sn
                elif h < z.nq + z.nk:
                    v = dk[h - z.nq, rows, :] * LN2
                    v = v * cs - pltpu.roll(v, 64, 1) * sn
                else:
                    v = dv[h - z.nq - z.nk, rows, :]
                heads.append(v.astype(BF))
            for quad in range(z.nh // 4):
                four = jnp.concatenate(heads[4 * quad:4 * quad + 4], axis=1)
                s.dqkv[rows, quad * 4 * HEAD:(quad + 1) * 4 * HEAD] = dot(four, s.perm[...], NT).astype(BF)
            return 0

        lax.fori_loop(0, T, unrotate, 0)

    pl.run_scoped(
        back_phase,
        pltpu.VMEM((z.nk, T, z.G * R, LANES), F32),
        pltpu.VMEM((z.nk, L, LANES), F32),
        pltpu.VMEM((z.nk, L, LANES), F32),
        pltpu.VMEM((L, z.HQ), BF),
    )
    for step in rs_f_steps:
        rs_f.send(*step)
    rs_f.arrive()
    rs_pump(1)
    ag_m.finish()

    def mixed_rows(i, _):
        lo = i * NR
        at = pl.ds(pl.multiple_of(lo, NR), NR)
        s.mid[pl.ds(pl.multiple_of(own_off + lo, NR), NR), :] = (s.middle[at, :] + rs_f.rows(lo, NR)).astype(BF)
        return 0

    lax.fori_loop(0, R // NR, mixed_rows, 0)
    out_mixed = pltpu.make_async_copy(s.mid.at[own_rows], mixed_hbm, s.s_loc.at[7])
    out_mixed.start()
    rs_f.finish()
    if one_rbuf:
        free(1)
        await_free(1)

    rs_q = Scatter(ring, s.part, s.rbuf_a, s.s_rsS.at[3], s.s_rsR.at[3])

    def qkv_back(step):
        rows = pl.ds(ring.off(step), R)

        def cols(n, _):
            at = pl.ds(pl.multiple_of(n * NB, NB), NB)
            s.part[rows, at] = dot(s.dqkv[rows, 0:z.HA], s.w0[at, :], NT).astype(BF)
            return 0

        lax.fori_loop(0, D // NB, cols, 0)

    scatter(rs_q, qkv_back)
    line.ag_finish(0)

    def qkv_tile(i, _):
        at = pl.ds(pl.multiple_of(i * 256, 256), 256)
        g = dot(s.normed[:, at], s.dqkv[:, 0:z.HA], TN)
        part = jnp.sum(g * s.w0[at, :].astype(F32), axis=-1, keepdims=True)
        s.gs[c, :, at] = row_form(part)
        s.w0[at, :] = g.astype(BF)
        return 0

    lax.fori_loop(0, D // 256, qkv_tile, 0)
    line.rs_sib_start(0)
    s.gs[c, 0:1, :] = s.gs[c, 0:1, :] / ga_ref[...]
    s.gs[c, 1:2, :] = s.gsum[0:1, :]

    def g_copy(stage, d, ref, slot, to):
        return pltpu.make_async_remote_copy(
            src_ref=ref.at[slot], dst_ref=ref.at[slot], send_sem=s.s_gS.at[stage, d], recv_sem=s.s_gR.at[stage, d],
            device_id=to, device_id_type=MESH,
        )

    g0 = g_copy(0, 0, s.gs, c, line.sibling)
    g0.start()
    line.rs_sib_sum(1)
    line.rs_step(1, 0)
    line.rs_sib_sum(0)
    line.rs_step(0, 0)
    g0.wait_recv()
    s.gz[p] = s.gs[0] + s.gs[1]
    g1 = [g_copy(1, d, s.gz, p, (rem(p + d, z.PZ) * 2 + c, t)) for d in range(1, z.PZ)]
    for cp in g1:
        cp.start()
    rs_pump(100)
    for k in range(1, z.PZ - 1):
        line.rs_step(1, k)
        line.rs_step(0, k)
        if k == 1:
            for cp in g1:
                cp.wait_recv()
            tot = s.gz[0]
            for q in range(1, z.PZ):
                tot = tot + s.gz[q]
            s.gt[t] = tot
            g2 = [g_copy(2, d, s.gt, t, (dp, rem(t + d, T))) for d in range(1, T)]
            for cp in g2:
                cp.start()

    def outs(stage, sem):
        order = (2, 3, 4, 1, 0)
        pend = None
        for i, w in enumerate(order):
            slot = stage.at[i % 2]
            cp = pltpu.make_async_copy(slot.at[:, pl.ds(0, z.cols[w])], o_hbm[w], sem.at[8 + i % 2])
            if i >= 2:
                pend[i % 2].wait()
            else:
                pend = pend or {}
            if w == 0:
                rs_q.arrive()
                lax.fori_loop(0, R // NR, last_rows, 0)
                out_tg.start()
            line.rs_final(w, slot)
            cp.start()
            pend[i % 2] = cp
        for cp in pend.values():
            cp.wait()

    def last_rows(i, _):
        lo = i * NR
        at = pl.ds(pl.multiple_of(lo, NR), NR)
        ng = rs_q.rows(lo, NR)
        x = s.xv[at, :].astype(F32)
        f = lax.rsqrt(jnp.mean(x * x, axis=-1, keepdims=True) + EPS)
        zz = x * f
        dz = ng * ga_ref[...]
        s.mgrad[at, :] += f * (dz - zz * jnp.mean(dz * zz, axis=-1, keepdims=True))
        return 0

    out_tg = pltpu.make_async_copy(s.mgrad, tg_hbm, s.s_loc.at[10])
    pl.run_scoped(lambda stage: outs(stage, s.s_loc), pltpu.VMEM((2, z.S, max(z.cols)), F32))

    for cp in g2:
        cp.wait_recv()
    tot = s.gt[0]
    for q in range(1, T):
        tot = tot + s.gt[q]
    gain_out[...] = tot

    out_mixed.wait()
    out_tg.wait()
    rs_q.finish()
    g0.wait_send()
    for cp in g1 + g2:
        cp.wait_send()
    for w in range(5):
        line.rs_finish(w)


def body(tokens, seq_lengths, gain_attn, query_weight, key_matrix, value_matrix, out_weight,
         gain_ffn, gate_weight, up_weight, down_weight, out_grad):
    n_dp, n_tensor = lax.axis_size("dp"), lax.axis_size("tensor")
    z = Sizes(n_dp, n_tensor, tokens.shape[0], tokens.shape[1], query_weight.shape[1],
              key_matrix.shape[1], gate_weight.shape[1])
    shards = (
        jnp.concatenate([query_weight, key_matrix, value_matrix], axis=1),
        jnp.pad(out_weight.T, ((0, 0), (0, z.HO - z.HQ))), gate_weight, up_weight, down_weight.T,
    )
    j = np.arange(LANES) % 64
    freq = np.where(j < HEAD // 2, ROPE_BASE ** (-(2.0 * j) / HEAD), 0.0).astype(np.float32)[None, :]
    items = scratch_list(z)
    names = [name for name, _ in items]
    hbm = pl.BlockSpec(memory_space=pl.ANY)
    vmem = pl.BlockSpec(memory_space=pltpu.VMEM)
    flops = 2 * 3 * z.L * z.D * sum(z.cols)
    outs = pl.pallas_call(
        functools.partial(kernel, z, names),
        out_shape=(
            jax.ShapeDtypeStruct((z.R, z.D), BF),
            jax.ShapeDtypeStruct((z.R, z.D), F32),
            jax.ShapeDtypeStruct((8, z.D), F32),
        ) + tuple(jax.ShapeDtypeStruct((z.S, n), F32) for n in z.cols),
        in_specs=[hbm, hbm, pl.BlockSpec(memory_space=pltpu.SMEM), vmem, vmem, vmem] + [hbm] * 5,
        out_specs=[hbm, hbm, vmem] + [hbm] * 5,
        scratch_shapes=[shape for _, shape in items],
        compiler_params=pltpu.CompilerParams(
            collective_id=0, has_side_effects=True, vmem_limit_bytes=67_000_000
        ),
        cost_estimate=pl.CostEstimate(flops=flops, bytes_accessed=16_000_000, transcendentals=0),
        name="layer",
    )(tokens, out_grad, seq_lengths, gain_attn[None, :], gain_ffn[None, :], jnp.asarray(freq), *shards)
    mixed, tokens_grad, gains, qkv_g, out_g, gate_g, up_g, down_g = outs
    hq, hk = z.nq * HEAD, z.nk * HEAD
    return (
        mixed, tokens_grad, gains[0],
        qkv_g[:, :hq], qkv_g[:, hq:hq + hk], qkv_g[:, hq + hk:],
        out_g[:, :hq].T, gains[1], gate_g, up_g, down_g.T,
    )


def solution(mesh):
    rows = P(("dp", "tensor"), None)
    split, turned = P("dp", "tensor"), P("tensor", "dp")
    return jax.shard_map(
        body, mesh=mesh,
        in_specs=(rows, P("dp", None), P(), split, split, split, turned, P(), split, split, turned, rows),
        out_specs=(rows, rows, P(), split, split, split, turned, P(), split, split, turned),
        check_vma=False,
    )
```

```python
import functools

import jax
import jax.numpy as jnp
import numpy as np
from jax import lax
from jax.experimental import pallas as pl
from jax.experimental.pallas import tpu as pltpu
from jax.sharding import PartitionSpec as P

HEAD = 96
LANES = 128
EPS = 1e-05
ROPE_BASE = 100000.0
LOG2E = 1.4426950408889634
LN2 = 0.6931471805599453
BF = jnp.bfloat16
F32 = jnp.float32
MESH = pl.DeviceIdType.MESH
rem, div = lax.rem, lax.div

NN = (((1,), (0,)), ((), ()))
NT = (((1,), (1,)), ((), ()))
TN = (((0,), (0,)), ((), ()))


def dot(a, b, dims):
    return lax.dot_general(a, b, dims, preferred_element_type=F32)


class Sizes:
    def __init__(self, n_dp, n_tensor, rows, width, q_cols, k_cols, hidden):
        self.N, self.T, self.R, self.D = n_dp, n_tensor, rows, width
        self.PZ = n_dp // 2
        self.H = n_tensor // 2
        self.L = rows * n_tensor
        self.S = width // n_dp
        self.F = hidden
        self.nq, self.nk = q_cols // HEAD, k_cols // HEAD
        self.G = self.nq // self.nk
        self.nh = self.nq + 2 * self.nk
        self.HA, self.PA = self.nh * HEAD, self.nh * LANES
        self.HQ, self.PQ = self.nq * HEAD, self.nq * LANES
        self.HO = -(-self.HQ // LANES) * LANES
        self.HG, self.PG = (self.G + 2) * HEAD, (self.G + 2) * LANES
        self.cols = (self.HG,) * self.nk + (self.HO, hidden, hidden, hidden)
        self.NW = self.nk + 4
        self.WO, self.WG, self.WU, self.WD = range(self.nk, self.nk + 4)


def scratch_list(z):
    dma = pltpu.SemaphoreType.DMA
    items = [
        ("xv", pltpu.VMEM((z.R, z.D), BF)),
        ("normed", pltpu.VMEM((z.L, z.D), BF)),
        ("ogr", pltpu.VMEM((z.L, z.D), BF)),
        ("n2", pltpu.VMEM((z.L, z.D), BF)),
        ("part", pltpu.VMEM((z.L, z.D), BF)),
        ("rbuf_a", pltpu.VMEM((2, 2 * z.H - 1, z.R // 2, z.D), BF)),
        ("kin", pltpu.VMEM((z.S, z.nk * HEAD), BF)),
        ("vin", pltpu.VMEM((z.S, z.nk * HEAD), BF)),
        ("gain", pltpu.VMEM((8, z.D), F32)),
        ("dwd", pltpu.VMEM((z.D, z.F), BF)),
        ("perm", pltpu.VMEM((z.HG, z.PG), BF)),
        ("cos", pltpu.VMEM((z.L, LANES), F32)),
        ("sin", pltpu.VMEM((z.L, LANES), F32)),
        ("q4", pltpu.VMEM((z.nk, z.T, z.G * z.R, LANES), BF)),
        ("kk", pltpu.VMEM((z.nk, z.L, LANES), BF)),
        ("vv", pltpu.VMEM((z.nk, z.L, LANES), BF)),
        ("o4", pltpu.VMEM((z.nk, z.T, z.G * z.R, LANES), BF)),
        ("do4", pltpu.VMEM((z.nk, z.T, z.G * z.R, LANES), BF)),
        ("lse", pltpu.VMEM((z.nk, z.T, 1, z.G * z.R), F32)),
        ("dlt", pltpu.VMEM((z.nk, z.T, 1, z.G * z.R), F32)),
        ("middle", pltpu.VMEM((z.R, z.D), F32)),
        ("mgrad", pltpu.VMEM((z.R, z.D), F32)),
        ("gsum", pltpu.VMEM((1, z.D), F32)),
        ("gs", pltpu.VMEM((2, 2, z.D), F32)),
        ("gz", pltpu.VMEM((z.PZ, 2, z.D), F32)),
        ("gt", pltpu.VMEM((z.T, 2, z.D), F32)),
        ("s_loc", dma((16,))),
        ("s_agS", dma((4, 2, z.H + 1, 2))),
        ("s_agR", dma((4, 2, z.H + 1, 2))),
        ("s_rsS", dma((4, 2, z.H + 1, 2))),
        ("s_rsR", dma((4, 2, z.H + 1, 2))),
        ("s_zgS", dma((z.NW, z.PZ))),
        ("s_zgR", dma((z.NW, z.PZ))),
        ("s_sgS", dma((z.NW, z.PZ))),
        ("s_sgR", dma((z.NW, z.PZ))),
        ("s_zrS", dma((z.NW, z.PZ))),
        ("s_zrR", dma((z.NW, z.PZ))),
        ("s_srS", dma((z.NW, z.PZ))),
        ("s_srR", dma((z.NW, z.PZ))),
        ("s_free", pltpu.SemaphoreType.REGULAR((2,))),
        ("s_gS", dma((3, max(z.T, z.PZ)))),
        ("s_gR", dma((3, max(z.T, z.PZ)))),
    ]
    if z.HO != z.HQ:
        items.append(("qin", pltpu.VMEM((z.S, z.HQ), BF)))
    if z.T <= 4:
        items.append(("rbuf_b", pltpu.VMEM((2, 2 * z.H - 1, z.R // 2, z.D), BF)))
    for w in range(z.NW):
        items.append((f"w{w}", pltpu.VMEM((z.D, z.cols[w]), BF)))
        items.append((f"sib{w}", pltpu.VMEM((z.PZ, z.S, z.cols[w]), BF)))
        items.append((f"lin{w}", pltpu.VMEM((z.PZ, z.S, z.cols[w]), BF)))
    return items


class Ring:
    def __init__(self, z):
        self.z = z
        self.dp = lax.axis_index("dp")
        t = lax.axis_index("tensor")
        self.t = t
        ycount = z.T // 2
        x, y = rem(t, 2), div(t, 2)
        self.r = y * (1 - x) + (z.T - 1 - y) * x
        self.ycount = ycount
        self.to = ((self.dp, self.index(1)), (self.dp, self.index(-1)))

    def index(self, step):
        z = self.z
        r = rem(self.r + step + z.T, z.T)
        far = div(r, self.ycount)
        return (1 - far) * 2 * r + far * (2 * (z.T - 1 - r) + 1)

    def off(self, step):
        return pl.multiple_of(self.index(step) * self.z.R, self.z.R)


class Gather:
    def __init__(self, ring, buf, s_send, s_recv):
        self.ring, self.buf, self.ss, self.rs = ring, buf, s_send, s_recv
        self.half = ring.z.R // 2

    def last(self, d, h):
        return self.ring.z.H if h == d else self.ring.z.H - 1

    def copy(self, d, k, h):
        sign = -1 if d == 0 else 1
        origin = self.ring.off(sign * (k - 1))
        piece = self.buf.at[pl.ds(pl.multiple_of(origin + h * self.half, self.half), self.half)]
        return pltpu.make_async_remote_copy(
            src_ref=piece, dst_ref=piece, send_sem=self.ss.at[d, k, h], recv_sem=self.rs.at[d, k, h],
            device_id=self.ring.to[d], device_id_type=MESH,
        )

    def start(self):
        for same in (True, False):
            for d in (0, 1):
                h = d if same else 1 - d
                if self.last(d, h) >= 1:
                    self.copy(d, 1, h).start()

    def step(self, k, same):
        for d in (0, 1):
            h = d if same else 1 - d
            if k <= self.last(d, h):
                self.copy(d, k, h).wait_recv()
                if k + 1 <= self.last(d, h):
                    self.copy(d, k + 1, h).start()

    def finish(self):
        for d in (0, 1):
            for h in (0, 1):
                for k in range(1, self.last(d, h) + 1):
                    self.copy(d, k, h).wait_send()


class Scatter:
    def __init__(self, ring, buf, rbuf, s_send, s_recv):
        self.ring, self.buf, self.rbuf, self.ss, self.rs = ring, buf, rbuf, s_send, s_recv
        self.half = ring.z.R // 2

    def piece(self, step, h):
        off = self.ring.off(step)
        return self.buf.at[pl.ds(pl.multiple_of(off + h * self.half, self.half), self.half)]

    def copy(self, d, k, h):
        dist = self.ring.z.H - k + 1
        return pltpu.make_async_remote_copy(
            src_ref=self.piece(dist if d == 0 else -dist, h), dst_ref=self.rbuf.at[d, self.slot(d, k, h)],
            send_sem=self.ss.at[d, k, h], recv_sem=self.rs.at[d, k, h],
            device_id=self.ring.to[d], device_id_type=MESH,
        )

    def first(self, d, h):
        return 1 if h == d else 2

    def slot(self, d, k, h):
        return k - 1 if h == d else self.ring.z.H + k - 2

    def send(self, k, same, ways=(0, 1)):
        for d in ways:
            h = d if same else 1 - d
            if k < self.first(d, h):
                continue
            if k > self.first(d, h):
                self.copy(d, k - 1, h).wait_recv()
                dist = self.ring.z.H - k + 1
                piece = self.piece(dist if d == 0 else -dist, h)
                add_into(piece, self.rbuf.at[d, self.slot(d, k - 1, h)])
            self.copy(d, k, h).start()

    def arrive(self):
        for h in (0, 1):
            for d in (0, 1):
                if self.ring.z.H >= self.first(d, h):
                    self.copy(d, self.ring.z.H, h).wait_recv()

    def rows(self, lo, n):
        h = div(lo, self.half)
        last = self.ring.z.H - 1
        off = lo - h * self.half
        own = pl.ds(pl.multiple_of(self.ring.off(0) + lo, n), n)
        total = self.buf[own, :].astype(F32)
        for d in (0, 1):
            total = total + self.rbuf[d, last + last * (h if d == 0 else 1 - h), pl.ds(pl.multiple_of(off, n), n), :].astype(F32)
        return total

    def finish(self):
        for d in (0, 1):
            for h in (0, 1):
                for k in range(self.first(d, h), self.ring.z.H + 1):
                    self.copy(d, k, h).wait_send()


def add_into(dst, src):
    rows = dst.shape[0]
    step = 32

    def body(i, _):
        at = pl.ds(pl.multiple_of(i * step, step), step)
        dst[at, :] = (dst[at, :].astype(F32) + src[at, :].astype(F32)).astype(dst.dtype)
        return 0

    lax.fori_loop(0, rows // step, body, 0)


class Line:
    def __init__(self, z, s, ws, gs):
        self.z, self.s, self.ws, self.gs = z, s, ws, gs
        dp, t = lax.axis_index("dp"), lax.axis_index("tensor")
        self.t = t
        self.p, self.c = div(dp, 2), rem(dp, 2)
        self.sibling = (dp + 1 - 2 * self.c, t)

    def shard(self, w, q, core):
        return self.ws[w].at[pl.ds(pl.multiple_of((2 * q + core) * self.z.S, self.z.S), self.z.S)]

    def remote(self, src, dst, send, recv, to):
        return pltpu.make_async_remote_copy(
            src_ref=src, dst_ref=dst, send_sem=send, recv_sem=recv, device_id=to, device_id_type=MESH
        )

    def chip(self, q):
        return (2 * q + self.c, self.t)

    def others(self):
        return (2, 3, 1) if self.four else tuple(range(1, self.z.PZ))

    @property
    def four(self):
        return self.z.PZ == 4

    def only(self, d, chips, fn):
        if not self.four:
            fn()
        elif chips[d]:
            cond = self.p == chips[d][0]
            for q in chips[d][1:]:
                cond = cond | (self.p == q)
            pl.when(cond)(fn)

    def ag_copy(self, w, d):
        src = self.shard(w, self.p, self.c)
        to = self.chip(rem(self.p + d, self.z.PZ))
        return self.remote(src, src, self.s.s_zgS.at[w, d], self.s.s_zgR.at[w, self.p], to)

    def ag_relay_copy(self, w, q):
        src = self.shard(w, q, self.c)
        return self.remote(src, src, self.s.s_zgS.at[w, 0], self.s.s_zgR.at[w, q], self.chip(3 if q == 1 else 0))

    def ag_sib(self, w, q):
        src = self.shard(w, q, self.c)
        return self.remote(src, src, self.s.s_sgS.at[w, q], self.s.s_sgR.at[w, q], self.sibling)

    def ag_wait(self, w, q):
        src = self.shard(w, q, self.c)
        self.remote(src, src, self.s.s_zgS.at[w, 0], self.s.s_zgR.at[w, q], self.sibling).wait_recv()

    def ag_inner(self, w):
        if self.four:
            for d in (1, 3):
                self.only(d, {1: (1,), 3: (2,)}, lambda d=d: self.ag_copy(w, d).start())
        self.ag_sib(w, self.p).start()

    def ag_outer(self, w):
        for d in self.others():
            self.only(d, {1: (0, 2, 3), 2: (0, 3), 3: (0, 1, 3)}, lambda d=d: self.ag_copy(w, d).start())

    def ag_relay(self, w):
        if self.four:
            for q, via in ((1, 2), (2, 1)):
                @pl.when(self.p == via)
                def _(q=q):
                    self.ag_wait(w, q)
                    self.ag_relay_copy(w, q).start()
                    self.ag_sib(w, q).start()

    def ag_recv(self, w):
        order = (1, 2, 0, 3) if self.four else range(self.z.PZ)
        for q in order:
            here = self.p != q
            if self.four and q in (1, 2):
                here = here & (self.p != 3 - q)

            @pl.when(here)
            def _(q=q):
                self.ag_wait(w, q)
                self.ag_sib(w, q).start()

    def ag_drain(self, w):
        for q in range(self.z.PZ):
            self.ag_sib(w, q).wait_recv()

    def ag_finish(self, w):
        for d in self.others():
            self.only(d, {1: (0, 1, 2, 3), 2: (0, 3), 3: (0, 1, 2, 3)}, lambda d=d: self.ag_copy(w, d).wait_send())
        if self.four:
            for q, via in ((1, 2), (2, 1)):
                @pl.when(self.p == via)
                def _(q=q):
                    self.ag_relay_copy(w, q).wait_send()
        for q in range(self.z.PZ):
            self.ag_sib(w, q).wait_send()

    def gshard(self, w, q, core):
        return self.gs[w].at[pl.ds(pl.multiple_of((2 * q + core) * self.z.S, self.z.S), self.z.S)]

    def rs_sib_copy(self, w, q):
        return self.remote(
            self.gshard(w, q, 1 - self.c), getattr(self.s, f"sib{w}").at[q],
            self.s.s_srS.at[w, q], self.s.s_srR.at[w, q], self.sibling,
        )

    def rs_sib_start(self, w):
        for q in range(self.z.PZ):
            self.rs_sib_copy(w, q).start()

    def rs_sib_sum(self, w):
        for q in range(self.z.PZ):
            self.rs_sib_copy(w, q).wait_recv()
            add_into(self.gshard(w, q, self.c), getattr(self.s, f"sib{w}").at[q])

    def rs_copy(self, w, d):
        p = self.p
        q = rem(p + d, self.z.PZ)
        to, slot = q, p
        if self.four and d == 1:
            far = div(p, 3)
            to, slot = q + 2 * far, p - far
        if self.four and d == 3:
            far = 1 - div(p + 3, 4)
            to, slot = q - 2 * far, p + far
        return self.remote(
            self.gshard(w, q, self.c), getattr(self.s, f"lin{w}").at[slot],
            self.s.s_zrS.at[w, d], self.s.s_zrR.at[w, slot], self.chip(to),
        )

    def rs_wait(self, w, slot):
        lin = getattr(self.s, f"lin{w}")
        self.remote(
            lin.at[slot], lin.at[slot], self.s.s_zrS.at[w, 0], self.s.s_zrR.at[w, slot], self.sibling
        ).wait_recv()

    def rs_first(self, w):
        if self.four:
            for d in (3, 1):
                self.only(d, {3: (0,), 1: (3,)}, lambda d=d: self.rs_copy(w, d).start())

    def rs_rest(self, w):
        for d in self.others():
            self.only(d, {1: (0, 1, 2), 2: (0, 3), 3: (1, 2, 3)}, lambda d=d: self.rs_copy(w, d).start())
        self.rs_relay(w)

    def rs_relay(self, w):
        if not self.four:
            return
        lin = getattr(self.s, f"lin{w}")
        for via in (1, 2):
            @pl.when(self.p == via)
            def _(via=via):
                self.rs_wait(w, via)
                add_into(self.gshard(w, (via + 2) % 4, self.c), lin.at[via])
                self.rs_copy(w, 2).start()

    def rs_final(self, w, out_vmem):
        p = self.p
        lin = getattr(self.s, f"lin{w}")
        out = out_vmem.at[:, pl.ds(0, self.z.cols[w])]
        copy_f32(out, self.gshard(w, p, self.c))
        for q in range(self.z.PZ):
            here = p != q
            if self.four and q in (0, 3):
                here = here & (p != 3 - q)

            @pl.when(here)
            def _(q=q):
                self.rs_wait(w, q)
                add_into(out, lin.at[q])

    def rs_finish(self, w):
        for q in range(self.z.PZ):
            self.rs_sib_copy(w, q).wait_send()
        for d in self.others():
            self.rs_copy(w, d).wait_send()


def copy_f32(dst, src):
    rows = dst.shape[0]
    step = 32

    def body(i, _):
        at = pl.ds(pl.multiple_of(i * step, step), step)
        dst[at, :] = src[at, :].astype(F32)
        return 0

    lax.fori_loop(0, rows // step, body, 0)


def kernel(z, names, *refs):
    (x_hbm, og_hbm, len_ref, ga_in, gf_in, freq_ref, *rest) = refs
    qkv_hbm, rest = rest[:3], rest[3:]
    w_hbm, rest = rest[:4], rest[4:]
    mixed_hbm, tg_hbm, ga_out, gf_out, *rest = rest
    oqkv_hbm, rest = rest[:3], rest[3:]
    o_hbm, rest = rest[:4], rest[4:]

    class Scratch:
        pass

    s = Scratch()
    for name, ref in zip(names, rest, strict=True):
        setattr(s, name, ref)
    ws = [getattr(s, f"w{w}") for w in range(z.NW)]
    w_out, w_gate, w_up, w_down = ws[z.nk:]
    s.mid, s.dqkv = s.n2, s.n2
    if z.HO == z.HQ:
        s.qin = getattr(s, f"sib{z.WO}").at[0]
    one_rbuf = not hasattr(s, "rbuf_b")
    if one_rbuf:
        s.rbuf_b = s.rbuf_a
    R, D, L, F, T = z.R, z.D, z.L, z.F, z.T
    ring = Ring(z)
    line = Line(z, s, ws, [s.dwd.at[:, pl.ds(g * z.HG, z.HG)] for g in range(z.nk)] + ws[z.nk:z.WD] + [s.dwd])
    dp, t, p, c = ring.dp, ring.t, line.p, line.c
    own_off = pl.multiple_of(t * R, R)
    own_rows = pl.ds(own_off, R)

    loc = [pltpu.make_async_copy(x_hbm, s.xv, s.s_loc.at[0]),
           pltpu.make_async_copy(og_hbm, s.ogr.at[own_rows], s.s_loc.at[1])]
    for i, (src, dst) in enumerate(zip(qkv_hbm, (s.qin, s.kin, s.vin), strict=True)):
        loc.append(pltpu.make_async_copy(src, dst, s.s_loc.at[2 + i]))
    for i, w in enumerate((z.WO, z.WG, z.WU, z.WD)):
        loc.append(pltpu.make_async_copy(w_hbm[i], line.shard(w, p, c), s.s_loc.at[5 + i]))
    for i in (2, 3, 4, 0, 5, 6, 1, 7, 8):
        loc[i].start()
    for i, ref in enumerate((ga_in, gf_in)):
        s.gain[i:i + 1, :] = ref[...].reshape(1, D)
    ga_ref, gf_ref = s.gain.at[0:1], s.gain.at[1:2]

    bar = pltpu.get_barrier_semaphore()
    peers = [line.sibling]
    peers += [(rem(p + d, z.PZ) * 2 + c, t) for d in range(1, z.PZ)]
    peers += [(dp, rem(t + d, T)) for d in range(1, T)]
    for peer in peers:
        pl.semaphore_signal(bar, 1, device_id=peer, device_id_type=MESH)
    pl.semaphore_wait(bar, len(peers))

    for i in (2, 3, 4):
        loc[i].wait()
    gc = z.G * HEAD
    for g in range(z.nk):
        line.shard(g, p, c)[...] = jnp.concatenate([
            s.qin[:, g * gc:(g + 1) * gc], s.kin[:, g * HEAD:(g + 1) * HEAD], s.vin[:, g * HEAD:(g + 1) * HEAD],
        ], axis=1)
        line.ag_inner(g)
    line.ag_outer(0)

    loc[0].wait()
    NR = 32

    def norm_rows(i, _):
        at = pl.ds(pl.multiple_of(i * NR, NR), NR)
        x = s.xv[at, :].astype(F32)
        f = lax.rsqrt(jnp.mean(x * x, axis=-1, keepdims=True) + EPS)
        s.normed[pl.ds(pl.multiple_of(own_off + i * NR, NR), NR), :] = (x * f * ga_ref[...]).astype(BF)
        return 0

    lax.fori_loop(0, R // NR, norm_rows, 0)
    ag_x = Gather(ring, s.normed, s.s_agS.at[0], s.s_agR.at[0])
    ag_x.start()

    l0 = len_ref[0, 0]
    lane = lax.broadcasted_iota(jnp.int32, (R, LANES), 1)

    def table_rows(i, _):
        at = pl.ds(pl.multiple_of(i * R, R), R)
        place = lax.broadcasted_iota(jnp.int32, (R, LANES), 0) + i * R
        pos = place - jnp.where(place >= l0, l0, 0)
        ang = pos.astype(F32) * freq_ref[...]
        s.cos[at, :] = jnp.cos(ang)
        sn = jnp.sin(ang)
        s.sin[at, :] = jnp.where(lane < 64, -sn, sn)
        return 0

    lax.fori_loop(0, T, table_rows, 0)
    half = HEAD // 2
    rowi = lax.broadcasted_iota(jnp.int32, (z.HG, LANES), 0)
    coli = lax.broadcasted_iota(jnp.int32, (z.HG, LANES), 1)
    inside = (coli < half) | ((coli >= 64) & (coli < 64 + half))
    src = jnp.where(inside, jnp.where(coli < half, coli, coli - (64 - half)), -100 * HEAD)
    for h in range(z.G + 2):
        s.perm[:, h * LANES:(h + 1) * LANES] = jnp.where(rowi == src + h * HEAD, 1.0, 0.0).astype(BF)

    ag_x.step(1, True)
    line.ag_relay(0)
    for w in range(1, z.nk):
        line.ag_outer(w)
        line.ag_relay(w)
    loc[5].wait()
    line.ag_inner(z.WO)
    loc[1].wait()
    ag_og = Gather(ring, s.ogr, s.s_agS.at[1], s.s_agR.at[1])
    ag_x.step(1, False)
    line.ag_outer(z.WO)
    loc[6].wait()
    line.ag_inner(z.WG)
    line.ag_relay(z.WO)

    wp = s.part
    for g in range(z.nk):
        line.ag_recv(g)
    line.ag_outer(z.WG)
    for g in range(z.nk):
        line.ag_drain(g)
        wp[g * z.PG:(g + 1) * z.PG, :] = dot(s.perm[...], ws[g][...], (((0,), (1,)), ((), ()))).astype(BF)
    qscale = HEAD ** -0.5 * LOG2E

    def qkv(step):
        off = ring.off(step)
        blk = ring.index(step)
        a = s.normed[pl.ds(off, R), :]
        cs, sn = s.cos[pl.ds(off, R), :], s.sin[pl.ds(off, R), :]
        for g in range(z.nk):
            y = dot(a, wp[g * z.PG:(g + 1) * z.PG, :], NT)
            for j in range(z.G + 2):
                yj = y[:, j * LANES:(j + 1) * LANES]
                if j <= z.G:
                    rot = yj * cs + pltpu.roll(yj, 64, 1) * sn
                if j < z.G:
                    s.q4[g, blk, j * R:(j + 1) * R, :] = (rot * qscale).astype(BF)
                elif j == z.G:
                    s.kk[g, pl.ds(off, R), :] = rot.astype(BF)
                else:
                    s.vv[g, pl.ds(off, R), :] = yj.astype(BF)

    qkv(0)
    for k in range(1, z.H):
        if k > 1:
            ag_x.step(k, True)
            ag_x.step(k, False)
        qkv(k)
        qkv(-k)
    ag_x.step(z.H, True)
    qkv(z.H)
    ag_og.start()

    line.ag_recv(z.WO)

    def row_form(col):
        wide = jnp.broadcast_to(col, (col.shape[0], LANES))
        return jnp.transpose(wide)[0:1, :]

    GR = z.G * R

    def allowed(qb, kb, diagonal, heads=z.G):
        qs = rem(lax.broadcasted_iota(jnp.int32, (1, heads * R), 1), R) + qb * R
        keys = lax.broadcasted_iota(jnp.int32, (R, heads * R), 0) + kb * R
        ok = keys >= jnp.where(qs >= l0, l0, 0)
        return ok & (keys <= qs) if diagonal else ok

    HP = 1

    def attend(qb):
        def one(i, _):
            g, j = div(i, z.G // HP), rem(i, z.G // HP)
            at = pl.ds(pl.multiple_of(j * HP * R, R), HP * R)
            q = s.q4[g, qb, at, :]
            scores = []
            for kb in range(qb + 1):
                st = dot(s.kk[g, kb * R:(kb + 1) * R, :], q, NT)
                scores.append(jnp.where(allowed(qb, kb, kb == qb, HP), st, -1e30))
            peak = jnp.max(scores[0], axis=0, keepdims=True)
            for st in scores[1:]:
                peak = jnp.maximum(peak, jnp.max(st, axis=0, keepdims=True))
            total, out = 0.0, 0.0
            for kb in range(qb + 1):
                e = jnp.exp2(scores[kb] - peak)
                total = total + jnp.sum(e, axis=0, keepdims=True)
                out = out + dot(s.vv[g, kb * R:(kb + 1) * R, :], e.astype(BF), TN)
            s.o4[g, qb, at, :] = jnp.transpose(out / total).astype(BF)
            s.lse[g, qb, :, at] = peak + jnp.log2(total)
            return 0

        lax.fori_loop(0, z.nk * z.G // HP, one, 0)

    hops = [(k, same) for k in range(1, z.H + 1) for same in (True, False)]
    for qb in range(T):
        attend(qb)
        if qb == 0:
            ag_og.step(*hops.pop(0))
            line.ag_relay(z.WG)
            loc[7].wait()
            line.ag_inner(z.WU)

    ag_x.finish()
    rs_o = Scatter(ring, s.part, s.rbuf_a, s.s_rsS.at[0], s.s_rsR.at[0])
    NB = 768

    qperm = s.perm[0:z.G * HEAD, 0:z.G * LANES]

    def unpadded(blk):
        out = []
        for g in range(z.nk):
            pads = [s.o4[g, blk, j * R:(j + 1) * R, :] for j in range(z.G)]
            out.append(dot(jnp.concatenate(pads, axis=1), qperm, NT).astype(BF))
        return jnp.concatenate(out, axis=1) if z.nk > 1 else out[0]

    def out_block(step):
        off, blk = ring.off(step), ring.index(step)
        a = unpadded(blk)

        def cols(n, _):
            at = pl.ds(pl.multiple_of(n * NB, NB), NB)
            s.part[pl.ds(off, R), at] = dot(a, w_out[at, 0:z.HQ], NT).astype(BF)
            return 0

        lax.fori_loop(0, D // NB, cols, 0)

    def scatter(rs, block, between=None):
        for k in range(1, z.H + 1):
            dist = z.H - k + 1
            block(dist)
            if k > 1:
                rs.send(k, False, (0,))
                block(-dist)
                rs.send(k, False, (1,))
            rs.send(k, True)
            if between is not None:
                between(k)
        block(0)

    line.ag_drain(z.WO)

    def between_o(k):
        if k == 1:
            ag_og.step(*hops.pop(0))
            line.ag_outer(z.WU)
        if k == z.H:
            for hop in hops:
                ag_og.step(*hop)
            line.ag_relay(z.WU)
            loc[8].wait()
            line.ag_inner(z.WD)
            line.ag_recv(z.WG)
            line.ag_outer(z.WD)

    scatter(rs_o, out_block, between_o)
    rs_o.arrive()

    def middle_rows(i, _):
        lo = i * NR
        at = pl.ds(pl.multiple_of(lo, NR), NR)
        m = s.xv[at, :].astype(F32) + rs_o.rows(lo, NR)
        s.middle[at, :] = m
        f = lax.rsqrt(jnp.mean(m * m, axis=-1, keepdims=True) + EPS)
        s.n2[pl.ds(pl.multiple_of(own_off + lo, NR), NR), :] = (m * f * gf_ref[...]).astype(BF)
        return 0

    lax.fori_loop(0, R // NR, middle_rows, 0)
    ag_n2 = Gather(ring, s.n2, s.s_agS.at[2], s.s_agR.at[2])
    ag_n2.start()
    ag_og.finish()

    ag_m = Gather(ring, s.mid, s.s_agS.at[3], s.s_agR.at[3])
    rs_n = Scatter(ring, s.part, s.rbuf_a, s.s_rsS.at[1], s.s_rsR.at[1])
    rs_f = Scatter(ring, s.ogr, s.rbuf_b, s.s_rsS.at[2], s.s_rsR.at[2])
    FB = 512

    def free(i):
        for d in (0, 1):
            pl.semaphore_signal(s.s_free.at[i], 1, device_id=ring.to[d], device_id_type=MESH)

    def await_free(i):
        pl.semaphore_wait(s.s_free.at[i], 2)

    def ffn_phase(gl, ul, hid):
        def wgrad(w, rows_ref, act_ref):
            if w != z.WD:
                line.ag_finish(w)
            DB = 512

            def tile(i, _):
                at = pl.ds(pl.multiple_of(i * DB, DB), DB)
                line.gs[w][at, :] = dot(rows_ref[:, at], act_ref[...], TN).astype(BF)
                return 0

            lax.fori_loop(0, D // DB, tile, 0)
            line.rs_sib_start(w)

        def gate_up(step):
            rows = pl.ds(ring.off(step), R)

            def cols(n, _):
                at = pl.ds(pl.multiple_of(n * FB, FB), FB)
                a = s.n2[rows, :]
                g = dot(a, w_gate[:, at], NN)
                u = dot(a, w_up[:, at], NN)
                gl[rows, at] = g.astype(BF)
                ul[rows, at] = u.astype(BF)
                hid[rows, at] = (g / (1.0 + jnp.exp(-g)) * u).astype(BF)
                return 0

            lax.fori_loop(0, F // FB, cols, 0)

        line.ag_drain(z.WG)
        ag_n2.step(1, True)
        line.ag_relay(z.WD)
        line.ag_recv(z.WU)
        line.ag_drain(z.WU)
        gate_up(0)
        ag_n2.step(1, False)
        for k in range(1, z.H):
            if k > 1:
                ag_n2.step(k, True)
                ag_n2.step(k, False)
            gate_up(k)
            gate_up(-k)
        ag_n2.step(z.H, True)
        gate_up(z.H)
        wgrad(z.WD, s.ogr, hid)
        rs_o.finish()
        line.ag_recv(z.WD)
        line.rs_sib_sum(z.WD)
        line.rs_first(z.WD)
        line.ag_drain(z.WD)

        def act_grads(step):
            rows = pl.ds(ring.off(step), R)

            def cols(n, _):
                at = pl.ds(pl.multiple_of(n * FB, FB), FB)
                hg = dot(s.ogr[rows, :], w_down[:, at], NN)
                g = gl[rows, at].astype(F32)
                u = ul[rows, at].astype(F32)
                sg = 1.0 / (1.0 + jnp.exp(-g))
                silu = g * sg
                gl[rows, at] = (hg * u * (sg + silu * (1.0 - sg))).astype(BF)
                ul[rows, at] = (hg * silu).astype(BF)
                return 0

            lax.fori_loop(0, F // FB, cols, 0)

            def back(n, _):
                at = pl.ds(pl.multiple_of(n * NB, NB), NB)
                s.part[rows, at] = (
                    dot(gl[rows, :], w_gate[at, :], NT) + dot(ul[rows, :], w_up[at, :], NT)
                ).astype(BF)
                return 0

            lax.fori_loop(0, D // NB, back, 0)

        scatter(rs_n, act_grads, lambda k: line.rs_rest(z.WD) if k == z.H else None)

        wgrad(z.WG, s.n2, gl)
        wgrad(z.WU, s.n2, ul)
        ag_n2.finish()
        free(0)
        line.rs_sib_sum(z.WG)
        line.rs_first(z.WG)
        line.rs_sib_sum(z.WU)
        rs_n.arrive()

        s.gsum[...] = jnp.zeros_like(s.gsum)

        def norm_back(i, _):
            lo = i * NR
            at = pl.ds(pl.multiple_of(lo, NR), NR)
            ng = rs_n.rows(lo, NR)
            m = s.middle[at, :]
            f = lax.rsqrt(jnp.mean(m * m, axis=-1, keepdims=True) + EPS)
            zz = m * f
            s.gsum[0:1, :] += jnp.sum(ng * zz, axis=0, keepdims=True)
            dz = ng * gf_ref[...]
            own = pl.ds(pl.multiple_of(own_off + lo, NR), NR)
            mg = s.ogr[own, :].astype(F32) + f * (dz - zz * jnp.mean(dz * zz, axis=-1, keepdims=True))
            s.mgrad[at, :] = mg
            s.mid[own, :] = mg.astype(BF)
            return 0

        lax.fori_loop(0, R // NR, norm_back, 0)
        rs_n.finish()
        await_free(0)
        ag_m.start()

        def down_block(step):
            rows = pl.ds(ring.off(step), R)

            def cols(n, _):
                at = pl.ds(pl.multiple_of(n * NB, NB), NB)
                s.ogr[rows, at] = dot(hid[rows, :], w_down[at, :], NT).astype(BF)
                return 0

            lax.fori_loop(0, D // NB, cols, 0)

        for k in range(1, z.H + 1):
            down_block(k)
            if k < z.H:
                down_block(-k)
        down_block(0)
        ag_m.step(1, True)
        line.rs_rest(z.WG)
        line.rs_first(z.WU)

    pl.run_scoped(ffn_phase, pltpu.VMEM((L, F), BF), pltpu.VMEM((L, F), BF), pltpu.VMEM((L, F), BF))

    def do_block(step):
        off, blk = ring.off(step), ring.index(step)
        a = dot(s.mid[pl.ds(off, R), :], w_out[:, 0:z.HQ], NN).astype(BF)
        for h in range(z.nq):
            g, j = h // z.G, h % z.G
            if j == 0:
                d = dot(a[:, g * z.G * HEAD:(g + 1) * z.G * HEAD], qperm, NN)
            dh = d[:, j * LANES:(j + 1) * LANES]
            at = pl.ds(j * R, R)
            s.do4[g, blk, at, :] = dh.astype(BF)
            dl = jnp.sum(dh * s.o4[g, blk, at, :].astype(F32), axis=-1, keepdims=True)
            s.dlt[g, blk, :, at] = row_form(dl)

    do_block(0)
    for k in range(1, z.H):
        if k > 1:
            ag_m.step(k, True)
        ag_m.step(k, False)
        do_block(k)
        do_block(-k)
    ag_m.step(z.H, True)
    do_block(z.H)

    rs_f.send(1, True)
    rs_f_steps = [(k, same) for k in range(2, z.H + 1) for same in (False, True)]

    def back_phase(dq, dk, dv, att):
        dk[...] = jnp.zeros_like(dk)
        dv[...] = jnp.zeros_like(dv)

        def back_block(qb):
            def pair(kb, diagonal):
                for g in range(z.nk):
                    at = pl.ds(kb * R, R) if diagonal else pl.ds(pl.multiple_of(kb * R, R), R)
                    q, do = s.q4[g, qb], s.do4[g, qb]
                    kk, vv = s.kk[g, at, :], s.vv[g, at, :]
                    e = jnp.exp2(dot(kk, q, NT) - s.lse[g, qb, 0:1, :])
                    pt = jnp.where(allowed(qb, kb, diagonal), e, 0.0)
                    dpt = dot(vv, do, NT)
                    ds = (pt * (dpt - s.dlt[g, qb, 0:1, :])).astype(BF)
                    dv[g, at, :] += dot(pt.astype(BF), do, NN)
                    dk[g, at, :] += dot(ds, q, NN)
                    if diagonal:
                        dq[g, qb] = dot(ds, kk, TN)
                    else:
                        dq[g, qb] += dot(ds, kk, TN)

            def off_diagonal(kb, _):
                pair(kb, False)
                return 0

            pair(qb, True)
            if qb > 0:
                lax.fori_loop(0, qb, off_diagonal, 0)

        for qb in range(T):
            back_block(qb)
            if qb == 0:
                line.rs_rest(z.WU)
            if rs_f_steps:
                rs_f.send(*rs_f_steps.pop(0))

        line.ag_finish(z.WO)
        DB = 512

        def unpad(i, _):
            att[pl.ds(pl.multiple_of(i * R, R), R), :] = unpadded(i)
            return 0

        lax.fori_loop(0, T, unpad, 0)

        def tile(i, _):
            at = pl.ds(pl.multiple_of(i * DB, DB), DB)
            w_out[at, 0:z.HQ] = dot(s.mid[:, at], att[...], TN).astype(BF)
            return 0

        lax.fori_loop(0, D // DB, tile, 0)
        line.rs_sib_start(z.WO)
        ag_m.finish()

        def unrotate(i, _):
            rows = pl.ds(pl.multiple_of(i * R, R), R)
            cs, sn = s.cos[rows, :], s.sin[rows, :]
            for g in range(z.nk):
                heads = []
                for j in range(z.G + 2):
                    if j < z.G:
                        v = dq[g, i, j * R:(j + 1) * R, :] * (HEAD ** -0.5)
                    elif j == z.G:
                        v = dk[g, rows, :] * LN2
                    else:
                        v = dv[g, rows, :]
                    if j <= z.G:
                        v = v * cs - pltpu.roll(v, 64, 1) * sn
                    heads.append(v.astype(BF))
                four = jnp.concatenate(heads, axis=1)
                s.dqkv[rows, g * z.HG:(g + 1) * z.HG] = dot(four, s.perm[...], NT).astype(BF)
            return 0

        lax.fori_loop(0, T, unrotate, 0)

    pl.run_scoped(
        back_phase,
        pltpu.VMEM((z.nk, T, z.G * R, LANES), F32),
        pltpu.VMEM((z.nk, L, LANES), F32),
        pltpu.VMEM((z.nk, L, LANES), F32),
        pltpu.VMEM((L, z.HQ), BF),
    )
    for step in rs_f_steps:
        rs_f.send(*step)

    def mixed_rows(i, _):
        lo = i * NR
        at = pl.ds(pl.multiple_of(lo, NR), NR)
        s.ogr[pl.ds(pl.multiple_of(own_off + lo, NR), NR), :] = (s.middle[at, :] + rs_f.rows(lo, NR)).astype(BF)
        return 0

    out_mixed = pltpu.make_async_copy(s.ogr.at[own_rows], mixed_hbm, s.s_loc.at[14])

    def outputs(chunks):
        def run(stage):
            copies = []
            for i, w in enumerate(chunks):
                slot = stage.at[i % 2]
                if i >= 2:
                    copies[i - 2].wait()
                line.rs_final(w, slot)
                cp = pltpu.make_async_copy(slot.at[:, pl.ds(0, z.cols[w])], o_hbm[w - z.nk], s.s_loc.at[9 + i % 2])
                cp.start()
                copies.append(cp)
            for cp in copies[-2:]:
                cp.wait()

        pl.run_scoped(run, pltpu.VMEM((2, z.S, max(z.cols)), F32))

    def qkv_outputs(stage, q_out, k_out, v_out):
        for g in range(z.nk):
            line.rs_final(g, stage.at[g])
        cuts = (0, gc, gc + HEAD, gc + 2 * HEAD)
        copies = []
        for i, out in enumerate((q_out, k_out, v_out)):
            parts = [stage[g, :, cuts[i]:cuts[i + 1]] for g in range(z.nk)]
            out[...] = jnp.concatenate(parts, axis=1) if z.nk > 1 else parts[0]
            copies.append(pltpu.make_async_copy(out, oqkv_hbm[i], s.s_loc.at[11 + i]))
            copies[-1].start()
        last()
        for cp in copies:
            cp.wait()

    def ffn_out():
        rs_f.arrive()
        lax.fori_loop(0, R // NR, mixed_rows, 0)
        out_mixed.start()

    if one_rbuf:
        ffn_out()
        free(1)
        await_free(1)

    rs_q = Scatter(ring, s.part, s.rbuf_a, s.s_rsS.at[3], s.s_rsR.at[3])

    def qkv_back(step):
        rows = pl.ds(ring.off(step), R)

        def cols(n, _):
            at = pl.ds(pl.multiple_of(n * NB, NB), NB)
            tot = dot(s.dqkv[rows, 0:z.HG], ws[0][at, :], NT)
            for g in range(1, z.nk):
                tot = tot + dot(s.dqkv[rows, g * z.HG:(g + 1) * z.HG], ws[g][at, :], NT)
            s.part[rows, at] = tot.astype(BF)
            return 0

        lax.fori_loop(0, D // NB, cols, 0)

    s.gs[c] = jnp.zeros_like(s.gs[c])

    def qkv_grads(k):
        if k == z.H:
            if not one_rbuf:
                ffn_out()
            line.rs_rest(z.WO)
            for g in range(z.nk):
                line.rs_sib_sum(g)
                line.rs_first(g)
        if k > 1:
            return
        outputs([z.WD])
        line.rs_finish(z.WD)
        line.rs_sib_sum(z.WO)
        line.rs_first(z.WO)
        for g in range(z.nk):
            def qkv_tile(i, _, g=g):
                at = pl.ds(pl.multiple_of(i * 512, 512), 512)
                grad = dot(s.normed[:, at], s.dqkv[:, g * z.HG:(g + 1) * z.HG], TN)
                part = jnp.sum(grad * ws[g][at, :].astype(F32), axis=-1, keepdims=True)
                s.gs[c, 0:1, at] += row_form(part)
                s.dwd[at, g * z.HG:(g + 1) * z.HG] = grad.astype(BF)
                return 0

            lax.fori_loop(0, D // 512, qkv_tile, 0)
            line.rs_sib_start(g)

    scatter(rs_q, qkv_back, qkv_grads)
    for g in range(z.nk):
        line.rs_rest(g)
    s.gs[c, 0:1, :] = s.gs[c, 0:1, :] / ga_ref[...]
    s.gs[c, 1:2, :] = s.gsum[0:1, :]

    def g_copy(stage, d, ref, slot, to):
        return pltpu.make_async_remote_copy(
            src_ref=ref.at[slot], dst_ref=ref.at[slot], send_sem=s.s_gS.at[stage, d], recv_sem=s.s_gR.at[stage, d],
            device_id=to, device_id_type=MESH,
        )

    g0 = g_copy(0, 0, s.gs, c, line.sibling)
    g0.start()
    g0.wait_recv()
    s.gz[p] = s.gs[0] + s.gs[1]
    g1 = [g_copy(1, d, s.gz, p, (rem(p + d, z.PZ) * 2 + c, t)) for d in range(1, z.PZ)]
    for cp in g1:
        cp.start()
    for cp in g1:
        cp.wait_recv()
    tot = s.gz[0]
    for q in range(1, z.PZ):
        tot = tot + s.gz[q]
    s.gt[t] = tot
    g2 = [g_copy(2, d, s.gt, t, (dp, rem(t + d, T))) for d in range(1, T)]
    for cp in g2:
        cp.start()
    def last_rows(i, _):
        lo = i * NR
        at = pl.ds(pl.multiple_of(lo, NR), NR)
        ng = rs_q.rows(lo, NR)
        x = s.xv[at, :].astype(F32)
        f = lax.rsqrt(jnp.mean(x * x, axis=-1, keepdims=True) + EPS)
        zz = x * f
        dz = ng * ga_ref[...]
        s.mgrad[at, :] += f * (dz - zz * jnp.mean(dz * zz, axis=-1, keepdims=True))
        return 0

    out_tg = pltpu.make_async_copy(s.mgrad, tg_hbm, s.s_loc.at[15])

    def last():
        rs_q.arrive()
        lax.fori_loop(0, R // NR, last_rows, 0)
        out_tg.start()

    outputs([z.WG, z.WU, z.WO])
    pl.run_scoped(
        qkv_outputs, pltpu.VMEM((z.nk, z.S, z.HG), F32), pltpu.VMEM((z.S, z.HQ), F32),
        pltpu.VMEM((z.S, z.nk * HEAD), F32), pltpu.VMEM((z.S, z.nk * HEAD), F32),
    )

    for cp in g2:
        cp.wait_recv()
    tot = s.gt[0]
    for q in range(1, T):
        tot = tot + s.gt[q]
    ga_out[...] = tot[0:1, :].reshape(D)
    gf_out[...] = tot[1:2, :].reshape(D)

    out_mixed.wait()
    rs_f.finish()
    out_tg.wait()
    rs_q.finish()
    g0.wait_send()
    for cp in g1 + g2:
        cp.wait_send()
    for w in list(range(z.nk)) + [z.WD]:
        line.ag_finish(w)
    for w in range(z.NW):
        if w != z.WD:
            line.rs_finish(w)


def body(tokens, seq_lengths, gain_attn, query_weight, key_matrix, value_matrix, out_weight,
         gain_ffn, gate_weight, up_weight, down_weight, out_grad):
    n_dp, n_tensor = lax.axis_size("dp"), lax.axis_size("tensor")
    z = Sizes(n_dp, n_tensor, tokens.shape[0], tokens.shape[1], query_weight.shape[1],
              key_matrix.shape[1], gate_weight.shape[1])
    shards = [
        query_weight, key_matrix, value_matrix,
        jnp.pad(out_weight.T, ((0, 0), (0, z.HO - z.HQ))), gate_weight, up_weight, down_weight.T,
    ]
    grads = [jax.ShapeDtypeStruct((z.S, n), F32) for n in (z.HQ, z.nk * HEAD, z.nk * HEAD) + z.cols[z.nk:]]
    j = np.arange(LANES) % 64
    freq = np.where(j < HEAD // 2, ROPE_BASE ** (-(2.0 * j) / HEAD), 0.0).astype(np.float32)[None, :]
    items = scratch_list(z)
    names = [name for name, _ in items]
    hbm = pl.BlockSpec(memory_space=pl.ANY)
    vmem = pl.BlockSpec(memory_space=pltpu.VMEM)
    flops = 2 * 3 * z.L * z.D * sum(z.cols)
    outs = pl.pallas_call(
        functools.partial(kernel, z, names),
        out_shape=(
            jax.ShapeDtypeStruct((z.R, z.D), BF),
            jax.ShapeDtypeStruct((z.R, z.D), F32),
            jax.ShapeDtypeStruct((z.D,), F32),
            jax.ShapeDtypeStruct((z.D,), F32),
            *grads,
        ),
        in_specs=[hbm, hbm, pl.BlockSpec(memory_space=pltpu.SMEM), vmem, vmem, vmem] + [hbm] * 7,
        out_specs=[hbm, hbm, vmem, vmem] + [hbm] * 7,
        scratch_shapes=[shape for _, shape in items],
        compiler_params=pltpu.CompilerParams(
            collective_id=0, has_side_effects=True, vmem_limit_bytes=67_000_000
        ),
        cost_estimate=pl.CostEstimate(flops=flops, bytes_accessed=16_000_000, transcendentals=0),
        name="layer",
    )(tokens, out_grad, seq_lengths, gain_attn, gain_ffn, jnp.asarray(freq), *shards)
    mixed, tokens_grad, ga_grad, gf_grad, q_g, k_g, v_g, out_g, gate_g, up_g, down_g = outs
    return (
        mixed, tokens_grad, ga_grad, q_g, k_g, v_g, out_g[:, :z.HQ].T, gf_grad, gate_g, up_g, down_g.T,
    )


def solution(mesh):
    rows = P(("dp", "tensor"), None)
    split, turned = P("dp", "tensor"), P("tensor", "dp")
    return jax.shard_map(
        body, mesh=mesh,
        in_specs=(rows, P("dp", None), P(), split, split, split, turned, P(), split, split, turned, rows),
        out_specs=(rows, rows, P(), split, split, split, turned, P(), split, split, turned),
        check_vma=False,
    )
```

```python
import functools

import jax
import jax.numpy as jnp
import numpy as np
from jax import lax
from jax.experimental import pallas as pl
from jax.experimental.pallas import tpu as pltpu
from jax.sharding import PartitionSpec as P

HEAD = 96
LANES = 128
EPS = 1e-05
ROPE_BASE = 100000.0
LOG2E = 1.4426950408889634
LN2 = 0.6931471805599453
BF = jnp.bfloat16
F32 = jnp.float32
MESH = pl.DeviceIdType.MESH
rem, div = lax.rem, lax.div

NN = (((1,), (0,)), ((), ()))
NT = (((1,), (1,)), ((), ()))
TN = (((0,), (0,)), ((), ()))


def dot(a, b, dims):
    return lax.dot_general(a, b, dims, preferred_element_type=F32)


class Sizes:
    def __init__(self, n_dp, n_tensor, rows, width, q_cols, k_cols, hidden):
        self.N, self.T, self.R, self.D = n_dp, n_tensor, rows, width
        self.PZ = n_dp // 2
        self.H = n_tensor // 2
        self.L = rows * n_tensor
        self.S = width // n_dp
        self.F = hidden
        self.nq, self.nk = q_cols // HEAD, k_cols // HEAD
        self.G = self.nq // self.nk
        self.nh = self.nq + 2 * self.nk
        self.HA, self.PA = self.nh * HEAD, self.nh * LANES
        self.HQ, self.PQ = self.nq * HEAD, self.nq * LANES
        self.HO = -(-self.HQ // LANES) * LANES
        self.HG, self.PG = (self.G + 2) * HEAD, (self.G + 2) * LANES
        self.cols = (self.HG,) * self.nk + (self.HO, hidden, hidden, hidden)
        self.NW = self.nk + 4
        self.WO, self.WG, self.WU, self.WD = range(self.nk, self.nk + 4)


def scratch_list(z):
    dma = pltpu.SemaphoreType.DMA
    items = [
        ("xv", pltpu.VMEM((z.R, z.D), BF)),
        ("normed", pltpu.VMEM((z.L, z.D), BF)),
        ("ogr", pltpu.VMEM((z.L, z.D), BF)),
        ("n2", pltpu.VMEM((z.L, z.D), BF)),
        ("part", pltpu.VMEM((z.L, z.D), BF)),
        ("rbuf_a", pltpu.VMEM((2, 2 * z.H - 1, z.R // 2, z.D), BF)),
        ("kin", pltpu.VMEM((z.S, z.nk * HEAD), BF)),
        ("vin", pltpu.VMEM((z.S, z.nk * HEAD), BF)),
        ("gain", pltpu.VMEM((8, z.D), F32)),
        ("dwd", pltpu.VMEM((z.D, z.F), BF)),
        ("perm", pltpu.VMEM((z.HG, z.PG), BF)),
        ("cos", pltpu.VMEM((z.L, LANES), F32)),
        ("sin", pltpu.VMEM((z.L, LANES), F32)),
        ("q4", pltpu.VMEM((z.nk, z.T, z.G * z.R, LANES), BF)),
        ("kk", pltpu.VMEM((z.nk, z.L, LANES), BF)),
        ("vv", pltpu.VMEM((z.nk, z.L, LANES), BF)),
        ("o4", pltpu.VMEM((z.nk, z.T, z.G * z.R, LANES), BF)),
        ("do4", pltpu.VMEM((z.nk, z.T, z.G * z.R, LANES), BF)),
        ("lse", pltpu.VMEM((z.nk, z.T, 1, z.G * z.R), F32)),
        ("dlt", pltpu.VMEM((z.nk, z.T, 1, z.G * z.R), F32)),
        ("middle", pltpu.VMEM((z.R, z.D), F32)),
        ("mgrad", pltpu.VMEM((z.R, z.D), F32)),
        ("gsum", pltpu.VMEM((1, z.D), F32)),
        ("gs", pltpu.VMEM((2, 2, z.D), F32)),
        ("gz", pltpu.VMEM((z.PZ, 2, z.D), F32)),
        ("gt", pltpu.VMEM((z.T, 2, z.D), F32)),
        ("s_loc", dma((16,))),
        ("s_agS", dma((4, 2, z.H + 1, 2))),
        ("s_agR", dma((4, 2, z.H + 1, 2))),
        ("s_rsS", dma((4, 2, z.H + 1, 2))),
        ("s_rsR", dma((4, 2, z.H + 1, 2))),
        ("s_zgS", dma((z.NW, z.PZ))),
        ("s_zgR", dma((z.NW, z.PZ))),
        ("s_sgS", dma((z.NW, z.PZ))),
        ("s_sgR", dma((z.NW, z.PZ))),
        ("s_zrS", dma((z.NW, z.PZ))),
        ("s_zrR", dma((z.NW, z.PZ))),
        ("s_srS", dma((z.NW, z.PZ))),
        ("s_srR", dma((z.NW, z.PZ))),
        ("s_free", pltpu.SemaphoreType.REGULAR((2,))),
        ("s_gS", dma((3, max(z.T, z.PZ)))),
        ("s_gR", dma((3, max(z.T, z.PZ)))),
    ]
    if z.HO != z.HQ:
        items.append(("qin", pltpu.VMEM((z.S, z.HQ), BF)))
    if z.T <= 4:
        items.append(("rbuf_b", pltpu.VMEM((2, 2 * z.H - 1, z.R // 2, z.D), BF)))
    for w in range(z.NW):
        items.append((f"w{w}", pltpu.VMEM((z.D, z.cols[w]), BF)))
        items.append((f"sib{w}", pltpu.VMEM((z.PZ, z.S, z.cols[w]), BF)))
        items.append((f"lin{w}", pltpu.VMEM((z.PZ, z.S, z.cols[w]), BF)))
    return items


class Ring:
    def __init__(self, z):
        self.z = z
        self.dp = lax.axis_index("dp")
        t = lax.axis_index("tensor")
        self.t = t
        ycount = z.T // 2
        x, y = rem(t, 2), div(t, 2)
        self.r = y * (1 - x) + (z.T - 1 - y) * x
        self.ycount = ycount
        self.to = ((self.dp, self.index(1)), (self.dp, self.index(-1)))

    def index(self, step):
        z = self.z
        r = rem(self.r + step + z.T, z.T)
        far = div(r, self.ycount)
        return (1 - far) * 2 * r + far * (2 * (z.T - 1 - r) + 1)

    def off(self, step):
        return pl.multiple_of(self.index(step) * self.z.R, self.z.R)


class Gather:
    def __init__(self, ring, buf, s_send, s_recv):
        self.ring, self.buf, self.ss, self.rs = ring, buf, s_send, s_recv
        self.half = ring.z.R // 2

    def last(self, d, h):
        return self.ring.z.H if h == d else self.ring.z.H - 1

    def copy(self, d, k, h):
        sign = -1 if d == 0 else 1
        origin = self.ring.off(sign * (k - 1))
        piece = self.buf.at[pl.ds(pl.multiple_of(origin + h * self.half, self.half), self.half)]
        return pltpu.make_async_remote_copy(
            src_ref=piece, dst_ref=piece, send_sem=self.ss.at[d, k, h], recv_sem=self.rs.at[d, k, h],
            device_id=self.ring.to[d], device_id_type=MESH,
        )

    def start(self):
        for same in (True, False):
            for d in (0, 1):
                h = d if same else 1 - d
                if self.last(d, h) >= 1:
                    self.copy(d, 1, h).start()

    def step(self, k, same):
        for d in (0, 1):
            h = d if same else 1 - d
            if k <= self.last(d, h):
                self.copy(d, k, h).wait_recv()
                if k + 1 <= self.last(d, h):
                    self.copy(d, k + 1, h).start()

    def finish(self):
        for d in (0, 1):
            for h in (0, 1):
                for k in range(1, self.last(d, h) + 1):
                    self.copy(d, k, h).wait_send()


class Scatter:
    def __init__(self, ring, buf, rbuf, s_send, s_recv):
        self.ring, self.buf, self.rbuf, self.ss, self.rs = ring, buf, rbuf, s_send, s_recv
        self.half = ring.z.R // 2

    def piece(self, step, h):
        off = self.ring.off(step)
        return self.buf.at[pl.ds(pl.multiple_of(off + h * self.half, self.half), self.half)]

    def copy(self, d, k, h):
        dist = self.ring.z.H - k + 1
        return pltpu.make_async_remote_copy(
            src_ref=self.piece(dist if d == 0 else -dist, h), dst_ref=self.rbuf.at[d, self.slot(d, k, h)],
            send_sem=self.ss.at[d, k, h], recv_sem=self.rs.at[d, k, h],
            device_id=self.ring.to[d], device_id_type=MESH,
        )

    def first(self, d, h):
        return 1 if h == d else 2

    def slot(self, d, k, h):
        return k - 1 if h == d else self.ring.z.H + k - 2

    def send(self, k, same, ways=(0, 1)):
        for d in ways:
            h = d if same else 1 - d
            if k < self.first(d, h):
                continue
            if k > self.first(d, h):
                self.copy(d, k - 1, h).wait_recv()
                dist = self.ring.z.H - k + 1
                piece = self.piece(dist if d == 0 else -dist, h)
                add_into(piece, self.rbuf.at[d, self.slot(d, k - 1, h)])
            self.copy(d, k, h).start()

    def arrive(self):
        for h in (0, 1):
            for d in (0, 1):
                if self.ring.z.H >= self.first(d, h):
                    self.copy(d, self.ring.z.H, h).wait_recv()

    def rows(self, lo, n):
        h = div(lo, self.half)
        last = self.ring.z.H - 1
        off = lo - h * self.half
        own = pl.ds(pl.multiple_of(self.ring.off(0) + lo, n), n)
        total = self.buf[own, :].astype(F32)
        for d in (0, 1):
            total = total + self.rbuf[d, last + last * (h if d == 0 else 1 - h), pl.ds(pl.multiple_of(off, n), n), :].astype(F32)
        return total

    def finish(self):
        for d in (0, 1):
            for h in (0, 1):
                for k in range(self.first(d, h), self.ring.z.H + 1):
                    self.copy(d, k, h).wait_send()


def add_into(dst, src):
    rows = dst.shape[0]
    step = 32

    def body(i, _):
        at = pl.ds(pl.multiple_of(i * step, step), step)
        dst[at, :] = (dst[at, :].astype(F32) + src[at, :].astype(F32)).astype(dst.dtype)
        return 0

    lax.fori_loop(0, rows // step, body, 0)


class Line:
    def __init__(self, z, s, ws, gs):
        self.z, self.s, self.ws, self.gs = z, s, ws, gs
        dp, t = lax.axis_index("dp"), lax.axis_index("tensor")
        self.t = t
        self.p, self.c = div(dp, 2), rem(dp, 2)
        self.sibling = (dp + 1 - 2 * self.c, t)

    def shard(self, w, q, core):
        return self.ws[w].at[pl.ds(pl.multiple_of((2 * q + core) * self.z.S, self.z.S), self.z.S)]

    def remote(self, src, dst, send, recv, to):
        return pltpu.make_async_remote_copy(
            src_ref=src, dst_ref=dst, send_sem=send, recv_sem=recv, device_id=to, device_id_type=MESH
        )

    def chip(self, q):
        return (2 * q + self.c, self.t)

    def others(self):
        return (2, 3, 1) if self.four else tuple(range(1, self.z.PZ))

    @property
    def four(self):
        return self.z.PZ == 4

    def only(self, d, chips, fn):
        if not self.four:
            fn()
        elif chips[d]:
            cond = self.p == chips[d][0]
            for q in chips[d][1:]:
                cond = cond | (self.p == q)
            pl.when(cond)(fn)

    def ag_copy(self, w, d):
        src = self.shard(w, self.p, self.c)
        to = self.chip(rem(self.p + d, self.z.PZ))
        return self.remote(src, src, self.s.s_zgS.at[w, d], self.s.s_zgR.at[w, self.p], to)

    def ag_relay_copy(self, w, q):
        src = self.shard(w, q, self.c)
        return self.remote(src, src, self.s.s_zgS.at[w, 0], self.s.s_zgR.at[w, q], self.chip(3 if q == 1 else 0))

    def ag_sib(self, w, q):
        src = self.shard(w, q, self.c)
        return self.remote(src, src, self.s.s_sgS.at[w, q], self.s.s_sgR.at[w, q], self.sibling)

    def ag_wait(self, w, q):
        src = self.shard(w, q, self.c)
        self.remote(src, src, self.s.s_zgS.at[w, 0], self.s.s_zgR.at[w, q], self.sibling).wait_recv()

    def ag_near(self, w):
        for d in (1, 3) if self.four else self.others():
            self.only(d, {1: (0, 1, 2), 3: (1, 2, 3)}, lambda d=d: self.ag_copy(w, d).start())
        self.ag_sib(w, self.p).start()

    def ag_far(self, w):
        if self.four:
            self.ag_relay(w)
            for d in (2, 3, 1):
                self.only(d, {1: (3,), 2: (0, 3), 3: (0,)}, lambda d=d: self.ag_copy(w, d).start())

    def ag_relay(self, w):
        for q, via in ((1, 2), (2, 1)):
            @pl.when(self.p == via)
            def _(q=q):
                self.ag_wait(w, q)
                self.ag_relay_copy(w, q).start()
                self.ag_sib(w, q).start()

    def ag_recv(self, w):
        order = (1, 2, 0, 3) if self.four else range(self.z.PZ)
        for q in order:
            here = self.p != q
            if self.four and q in (1, 2):
                here = here & (self.p != 3 - q)

            @pl.when(here)
            def _(q=q):
                self.ag_wait(w, q)
                self.ag_sib(w, q).start()

    def ag_drain(self, w):
        for q in range(self.z.PZ):
            self.ag_sib(w, q).wait_recv()

    def ag_finish(self, w):
        for d in self.others():
            self.only(d, {1: (0, 1, 2, 3), 2: (0, 3), 3: (0, 1, 2, 3)}, lambda d=d: self.ag_copy(w, d).wait_send())
        if self.four:
            for q, via in ((1, 2), (2, 1)):
                @pl.when(self.p == via)
                def _(q=q):
                    self.ag_relay_copy(w, q).wait_send()
        for q in range(self.z.PZ):
            self.ag_sib(w, q).wait_send()

    def gshard(self, w, q, core):
        return self.gs[w].at[pl.ds(pl.multiple_of((2 * q + core) * self.z.S, self.z.S), self.z.S)]

    def rs_sib_copy(self, w, q):
        return self.remote(
            self.gshard(w, q, 1 - self.c), getattr(self.s, f"sib{w}").at[q],
            self.s.s_srS.at[w, q], self.s.s_srR.at[w, q], self.sibling,
        )

    def rs_sib_start(self, w):
        for q in range(self.z.PZ):
            self.rs_sib_copy(w, q).start()

    def rs_sib_sum(self, w):
        for q in range(self.z.PZ):
            self.rs_sib_copy(w, q).wait_recv()
            add_into(self.gshard(w, q, self.c), getattr(self.s, f"sib{w}").at[q])

    def rs_copy(self, w, d):
        p = self.p
        q = rem(p + d, self.z.PZ)
        to, slot = q, p
        if self.four and d == 1:
            far = div(p, 3)
            to, slot = q + 2 * far, p - far
        if self.four and d == 3:
            far = 1 - div(p + 3, 4)
            to, slot = q - 2 * far, p + far
        return self.remote(
            self.gshard(w, q, self.c), getattr(self.s, f"lin{w}").at[slot],
            self.s.s_zrS.at[w, d], self.s.s_zrR.at[w, slot], self.chip(to),
        )

    def rs_wait(self, w, slot):
        lin = getattr(self.s, f"lin{w}")
        self.remote(
            lin.at[slot], lin.at[slot], self.s.s_zrS.at[w, 0], self.s.s_zrR.at[w, slot], self.sibling
        ).wait_recv()

    def rs_first(self, w):
        for d in (3, 1) if self.four else self.others():
            self.only(d, {3: (0, 1, 2), 1: (1, 2, 3)}, lambda d=d: self.rs_copy(w, d).start())

    def rs_rest(self, w):
        if self.four:
            for d in (2, 1, 3):
                self.only(d, {1: (0,), 2: (0, 3), 3: (3,)}, lambda d=d: self.rs_copy(w, d).start())
            self.rs_relay(w)

    def rs_relay(self, w):
        lin = getattr(self.s, f"lin{w}")
        for via in (1, 2):
            @pl.when(self.p == via)
            def _(via=via):
                self.rs_wait(w, via)
                add_into(self.gshard(w, (via + 2) % 4, self.c), lin.at[via])
                self.rs_copy(w, 2).start()

    def rs_final(self, w, out_vmem):
        p = self.p
        lin = getattr(self.s, f"lin{w}")
        out = out_vmem.at[:, pl.ds(0, self.z.cols[w])]
        copy_f32(out, self.gshard(w, p, self.c))
        for q in range(self.z.PZ):
            here = p != q
            if self.four and q in (0, 3):
                here = here & (p != 3 - q)

            @pl.when(here)
            def _(q=q):
                self.rs_wait(w, q)
                add_into(out, lin.at[q])

    def rs_finish(self, w):
        for q in range(self.z.PZ):
            self.rs_sib_copy(w, q).wait_send()
        for d in self.others():
            self.rs_copy(w, d).wait_send()


def copy_f32(dst, src):
    rows = dst.shape[0]
    step = 32

    def body(i, _):
        at = pl.ds(pl.multiple_of(i * step, step), step)
        dst[at, :] = src[at, :].astype(F32)
        return 0

    lax.fori_loop(0, rows // step, body, 0)


def kernel(z, names, *refs):
    (x_hbm, og_hbm, len_ref, ga_in, gf_in, freq_ref, *rest) = refs
    qkv_hbm, rest = rest[:3], rest[3:]
    w_hbm, rest = rest[:4], rest[4:]
    mixed_hbm, tg_hbm, ga_out, gf_out, *rest = rest
    oqkv_hbm, rest = rest[:3], rest[3:]
    o_hbm, rest = rest[:4], rest[4:]

    class Scratch:
        pass

    s = Scratch()
    for name, ref in zip(names, rest, strict=True):
        setattr(s, name, ref)
    ws = [getattr(s, f"w{w}") for w in range(z.NW)]
    w_out, w_gate, w_up, w_down = ws[z.nk:]
    s.mid, s.dqkv = s.n2, s.n2
    if z.HO == z.HQ:
        s.qin = getattr(s, f"sib{z.WO}").at[0]
    one_rbuf = not hasattr(s, "rbuf_b")
    if one_rbuf:
        s.rbuf_b = s.rbuf_a
    R, D, L, F, T = z.R, z.D, z.L, z.F, z.T
    ring = Ring(z)
    line = Line(z, s, ws, [s.dwd.at[:, pl.ds(g * z.HG, z.HG)] for g in range(z.nk)] + ws[z.nk:z.WD] + [s.dwd])
    dp, t, p, c = ring.dp, ring.t, line.p, line.c
    own_off = pl.multiple_of(t * R, R)
    own_rows = pl.ds(own_off, R)

    loc = [pltpu.make_async_copy(x_hbm, s.xv, s.s_loc.at[0]),
           pltpu.make_async_copy(og_hbm, s.ogr.at[own_rows], s.s_loc.at[1])]
    for i, (src, dst) in enumerate(zip(qkv_hbm, (s.qin, s.kin, s.vin), strict=True)):
        loc.append(pltpu.make_async_copy(src, dst, s.s_loc.at[2 + i]))
    for i, w in enumerate((z.WO, z.WG, z.WU, z.WD)):
        loc.append(pltpu.make_async_copy(w_hbm[i], line.shard(w, p, c), s.s_loc.at[5 + i]))
    for i in (2, 3, 4, 0, 5, 6, 1, 7, 8):
        loc[i].start()
    for i, ref in enumerate((ga_in, gf_in)):
        s.gain[i:i + 1, :] = ref[...].reshape(1, D)
    ga_ref, gf_ref = s.gain.at[0:1], s.gain.at[1:2]

    bar = pltpu.get_barrier_semaphore()
    peers = [line.sibling]
    peers += [(rem(p + d, z.PZ) * 2 + c, t) for d in range(1, z.PZ)]
    peers += [(dp, rem(t + d, T)) for d in range(1, T)]
    for peer in peers:
        pl.semaphore_signal(bar, 1, device_id=peer, device_id_type=MESH)
    pl.semaphore_wait(bar, len(peers))

    for i in (2, 3, 4):
        loc[i].wait()
    gc = z.G * HEAD
    for g in range(z.nk):
        line.shard(g, p, c)[...] = jnp.concatenate([
            s.qin[:, g * gc:(g + 1) * gc], s.kin[:, g * HEAD:(g + 1) * HEAD], s.vin[:, g * HEAD:(g + 1) * HEAD],
        ], axis=1)
        line.ag_near(g)

    loc[0].wait()
    NR = 32

    def norm_rows(i, _):
        at = pl.ds(pl.multiple_of(i * NR, NR), NR)
        x = s.xv[at, :].astype(F32)
        f = lax.rsqrt(jnp.mean(x * x, axis=-1, keepdims=True) + EPS)
        s.normed[pl.ds(pl.multiple_of(own_off + i * NR, NR), NR), :] = (x * f * ga_ref[...]).astype(BF)
        return 0

    lax.fori_loop(0, R // NR, norm_rows, 0)
    ag_x = Gather(ring, s.normed, s.s_agS.at[0], s.s_agR.at[0])
    ag_x.start()

    l0 = len_ref[0, 0]
    lane = lax.broadcasted_iota(jnp.int32, (R, LANES), 1)

    def table_rows(i, _):
        at = pl.ds(pl.multiple_of(i * R, R), R)
        place = lax.broadcasted_iota(jnp.int32, (R, LANES), 0) + i * R
        pos = place - jnp.where(place >= l0, l0, 0)
        ang = pos.astype(F32) * freq_ref[...]
        s.cos[at, :] = jnp.cos(ang)
        sn = jnp.sin(ang)
        s.sin[at, :] = jnp.where(lane < 64, -sn, sn)
        return 0

    lax.fori_loop(0, T, table_rows, 0)
    half = HEAD // 2
    rowi = lax.broadcasted_iota(jnp.int32, (z.HG, LANES), 0)
    coli = lax.broadcasted_iota(jnp.int32, (z.HG, LANES), 1)
    inside = (coli < half) | ((coli >= 64) & (coli < 64 + half))
    src = jnp.where(inside, jnp.where(coli < half, coli, coli - (64 - half)), -100 * HEAD)
    for h in range(z.G + 2):
        s.perm[:, h * LANES:(h + 1) * LANES] = jnp.where(rowi == src + h * HEAD, 1.0, 0.0).astype(BF)

    for g in range(z.nk):
        line.ag_far(g)
    ag_x.step(1, True)
    loc[1].wait()
    ag_og = Gather(ring, s.ogr, s.s_agS.at[1], s.s_agR.at[1])
    ag_x.step(1, False)
    loc[5].wait()
    line.ag_near(z.WO)

    wp = s.part
    for g in range(z.nk):
        line.ag_recv(g)
    line.ag_far(z.WO)
    loc[6].wait()
    line.ag_near(z.WG)
    for g in range(z.nk):
        line.ag_drain(g)
        wp[g * z.PG:(g + 1) * z.PG, :] = dot(s.perm[...], ws[g][...], (((0,), (1,)), ((), ()))).astype(BF)
    qscale = HEAD ** -0.5 * LOG2E

    def qkv(step):
        off = ring.off(step)
        blk = ring.index(step)
        a = s.normed[pl.ds(off, R), :]
        cs, sn = s.cos[pl.ds(off, R), :], s.sin[pl.ds(off, R), :]
        for g in range(z.nk):
            y = dot(a, wp[g * z.PG:(g + 1) * z.PG, :], NT)
            for j in range(z.G + 2):
                yj = y[:, j * LANES:(j + 1) * LANES]
                if j <= z.G:
                    rot = yj * cs + pltpu.roll(yj, 64, 1) * sn
                if j < z.G:
                    s.q4[g, blk, j * R:(j + 1) * R, :] = (rot * qscale).astype(BF)
                elif j == z.G:
                    s.kk[g, pl.ds(off, R), :] = rot.astype(BF)
                else:
                    s.vv[g, pl.ds(off, R), :] = yj.astype(BF)

    qkv(0)
    for k in range(1, z.H):
        if k > 1:
            ag_x.step(k, True)
            ag_x.step(k, False)
        qkv(k)
        qkv(-k)
    ag_x.step(z.H, True)
    qkv(z.H)
    ag_og.start()

    line.ag_recv(z.WO)
    line.ag_far(z.WG)
    loc[7].wait()
    line.ag_near(z.WU)

    def row_form(col):
        wide = jnp.broadcast_to(col, (col.shape[0], LANES))
        return jnp.transpose(wide)[0:1, :]

    GR = z.G * R

    def allowed(qb, kb, diagonal, heads=z.G):
        qs = rem(lax.broadcasted_iota(jnp.int32, (1, heads * R), 1), R) + qb * R
        keys = lax.broadcasted_iota(jnp.int32, (R, heads * R), 0) + kb * R
        ok = keys >= jnp.where(qs >= l0, l0, 0)
        return ok & (keys <= qs) if diagonal else ok

    HP = 1

    def attend(qb):
        def one(i, _):
            g, j = div(i, z.G // HP), rem(i, z.G // HP)
            at = pl.ds(pl.multiple_of(j * HP * R, R), HP * R)
            q = s.q4[g, qb, at, :]
            scores = []
            for kb in range(qb + 1):
                st = dot(s.kk[g, kb * R:(kb + 1) * R, :], q, NT)
                scores.append(jnp.where(allowed(qb, kb, kb == qb, HP), st, -1e30))
            peak = jnp.max(scores[0], axis=0, keepdims=True)
            for st in scores[1:]:
                peak = jnp.maximum(peak, jnp.max(st, axis=0, keepdims=True))
            total, out = 0.0, 0.0
            for kb in range(qb + 1):
                e = jnp.exp2(scores[kb] - peak)
                total = total + jnp.sum(e, axis=0, keepdims=True)
                out = out + dot(s.vv[g, kb * R:(kb + 1) * R, :], e.astype(BF), TN)
            s.o4[g, qb, at, :] = jnp.transpose(out / total).astype(BF)
            s.lse[g, qb, :, at] = peak + jnp.log2(total)
            return 0

        lax.fori_loop(0, z.nk * z.G // HP, one, 0)

    hops = [(k, same) for k in range(1, z.H + 1) for same in (True, False)]
    for qb in range(T):
        attend(qb)
        if qb == 0:
            ag_og.step(*hops.pop(0))

    ag_x.finish()
    rs_o = Scatter(ring, s.part, s.rbuf_a, s.s_rsS.at[0], s.s_rsR.at[0])
    NB = 768 if T <= 4 else 512

    qperm = s.perm[0:z.G * HEAD, 0:z.G * LANES]

    def unpadded(blk):
        out = []
        for g in range(z.nk):
            pads = [s.o4[g, blk, j * R:(j + 1) * R, :] for j in range(z.G)]
            out.append(dot(jnp.concatenate(pads, axis=1), qperm, NT).astype(BF))
        return jnp.concatenate(out, axis=1) if z.nk > 1 else out[0]

    def out_block(step):
        off, blk = ring.off(step), ring.index(step)
        a = unpadded(blk)

        def cols(n, _):
            at = pl.ds(pl.multiple_of(n * NB, NB), NB)
            s.part[pl.ds(off, R), at] = dot(a, w_out[at, 0:z.HQ], NT).astype(BF)
            return 0

        lax.fori_loop(0, D // NB, cols, 0)

    def scatter(rs, block, between=None):
        for k in range(1, z.H + 1):
            dist = z.H - k + 1
            block(dist)
            if k > 1:
                rs.send(k, False, (0,))
                block(-dist)
                rs.send(k, False, (1,))
            rs.send(k, True)
            if between is not None:
                between(k)
        block(0)

    line.ag_drain(z.WO)

    def between_o(k):
        if k == z.H:
            for hop in hops:
                ag_og.step(*hop)
            line.ag_recv(z.WG)
            line.ag_far(z.WU)
            loc[8].wait()
            line.ag_near(z.WD)

    scatter(rs_o, out_block, between_o)
    rs_o.arrive()

    def middle_rows(i, _):
        lo = i * NR
        at = pl.ds(pl.multiple_of(lo, NR), NR)
        m = s.xv[at, :].astype(F32) + rs_o.rows(lo, NR)
        s.middle[at, :] = m
        f = lax.rsqrt(jnp.mean(m * m, axis=-1, keepdims=True) + EPS)
        s.n2[pl.ds(pl.multiple_of(own_off + lo, NR), NR), :] = (m * f * gf_ref[...]).astype(BF)
        return 0

    lax.fori_loop(0, R // NR, middle_rows, 0)
    ag_n2 = Gather(ring, s.n2, s.s_agS.at[2], s.s_agR.at[2])
    ag_n2.start()
    ag_og.finish()

    ag_m = Gather(ring, s.mid, s.s_agS.at[3], s.s_agR.at[3])
    rs_n = Scatter(ring, s.part, s.rbuf_a, s.s_rsS.at[1], s.s_rsR.at[1])
    rs_f = Scatter(ring, s.ogr, s.rbuf_b, s.s_rsS.at[2], s.s_rsR.at[2])
    FB = 512 if T <= 4 else 256

    def free(i):
        for d in (0, 1):
            pl.semaphore_signal(s.s_free.at[i], 1, device_id=ring.to[d], device_id_type=MESH)

    def await_free(i):
        pl.semaphore_wait(s.s_free.at[i], 2)

    def ffn_phase(gl, ul, hid):
        def wgrad(w, rows_ref, act_ref):
            if w != z.WD:
                line.ag_finish(w)
            DB = 512

            def tile(i, _):
                at = pl.ds(pl.multiple_of(i * DB, DB), DB)
                line.gs[w][at, :] = dot(rows_ref[:, at], act_ref[...], TN).astype(BF)
                return 0

            lax.fori_loop(0, D // DB, tile, 0)
            line.rs_sib_start(w)

        def gate_up(step):
            rows = pl.ds(ring.off(step), R)

            def cols(n, _):
                at = pl.ds(pl.multiple_of(n * FB, FB), FB)
                a = s.n2[rows, :]
                g = dot(a, w_gate[:, at], NN)
                u = dot(a, w_up[:, at], NN)
                gl[rows, at] = g.astype(BF)
                ul[rows, at] = u.astype(BF)
                hid[rows, at] = (g / (1.0 + jnp.exp(-g)) * u).astype(BF)
                return 0

            lax.fori_loop(0, F // FB, cols, 0)

        line.ag_drain(z.WG)
        ag_n2.step(1, True)
        line.ag_far(z.WD)
        ag_n2.step(1, False)
        line.ag_recv(z.WU)
        line.ag_drain(z.WU)
        gate_up(0)
        for k in range(1, z.H):
            if k > 1:
                ag_n2.step(k, True)
                ag_n2.step(k, False)
            gate_up(k)
            gate_up(-k)
        ag_n2.step(z.H, True)
        gate_up(z.H)
        wgrad(z.WD, s.ogr, hid)
        rs_o.finish()
        line.ag_recv(z.WD)
        line.rs_sib_sum(z.WD)
        line.rs_first(z.WD)
        line.ag_drain(z.WD)

        def act_grads(step):
            rows = pl.ds(ring.off(step), R)

            def cols(n, _):
                at = pl.ds(pl.multiple_of(n * FB, FB), FB)
                hg = dot(s.ogr[rows, :], w_down[:, at], NN)
                g = gl[rows, at].astype(F32)
                u = ul[rows, at].astype(F32)
                sg = 1.0 / (1.0 + jnp.exp(-g))
                silu = g * sg
                gl[rows, at] = (hg * u * (sg + silu * (1.0 - sg))).astype(BF)
                ul[rows, at] = (hg * silu).astype(BF)
                return 0

            lax.fori_loop(0, F // FB, cols, 0)

            def back(n, _):
                at = pl.ds(pl.multiple_of(n * NB, NB), NB)
                s.part[rows, at] = (
                    dot(gl[rows, :], w_gate[at, :], NT) + dot(ul[rows, :], w_up[at, :], NT)
                ).astype(BF)
                return 0

            lax.fori_loop(0, D // NB, back, 0)

        scatter(rs_n, act_grads, lambda k: line.rs_rest(z.WD) if k == z.H else None)

        wgrad(z.WG, s.n2, gl)
        wgrad(z.WU, s.n2, ul)
        ag_n2.finish()
        free(0)
        line.rs_sib_sum(z.WG)
        line.rs_first(z.WG)
        line.rs_sib_sum(z.WU)
        line.rs_first(z.WU)
        rs_n.arrive()

        s.gsum[...] = jnp.zeros_like(s.gsum)

        def norm_back(i, _):
            lo = i * NR
            at = pl.ds(pl.multiple_of(lo, NR), NR)
            ng = rs_n.rows(lo, NR)
            m = s.middle[at, :]
            f = lax.rsqrt(jnp.mean(m * m, axis=-1, keepdims=True) + EPS)
            zz = m * f
            s.gsum[0:1, :] += jnp.sum(ng * zz, axis=0, keepdims=True)
            dz = ng * gf_ref[...]
            own = pl.ds(pl.multiple_of(own_off + lo, NR), NR)
            mg = s.ogr[own, :].astype(F32) + f * (dz - zz * jnp.mean(dz * zz, axis=-1, keepdims=True))
            s.mgrad[at, :] = mg
            s.mid[own, :] = mg.astype(BF)
            return 0

        lax.fori_loop(0, R // NR, norm_back, 0)
        rs_n.finish()
        await_free(0)
        ag_m.start()

        def down_block(step):
            rows = pl.ds(ring.off(step), R)

            def cols(n, _):
                at = pl.ds(pl.multiple_of(n * NB, NB), NB)
                s.ogr[rows, at] = dot(hid[rows, :], w_down[at, :], NT).astype(BF)
                return 0

            lax.fori_loop(0, D // NB, cols, 0)

        for k in range(1, z.H + 1):
            down_block(k)
            if k < z.H:
                down_block(-k)
        down_block(0)
        ag_m.step(1, True)
        line.rs_rest(z.WG)

    pl.run_scoped(ffn_phase, pltpu.VMEM((L, F), BF), pltpu.VMEM((L, F), BF), pltpu.VMEM((L, F), BF))

    def do_block(step):
        off, blk = ring.off(step), ring.index(step)
        a = dot(s.mid[pl.ds(off, R), :], w_out[:, 0:z.HQ], NN).astype(BF)
        for h in range(z.nq):
            g, j = h // z.G, h % z.G
            if j == 0:
                d = dot(a[:, g * z.G * HEAD:(g + 1) * z.G * HEAD], qperm, NN)
            dh = d[:, j * LANES:(j + 1) * LANES]
            at = pl.ds(j * R, R)
            s.do4[g, blk, at, :] = dh.astype(BF)
            dl = jnp.sum(dh * s.o4[g, blk, at, :].astype(F32), axis=-1, keepdims=True)
            s.dlt[g, blk, :, at] = row_form(dl)

    do_block(0)
    for k in range(1, z.H):
        if k > 1:
            ag_m.step(k, True)
        ag_m.step(k, False)
        do_block(k)
        do_block(-k)
    ag_m.step(z.H, True)
    do_block(z.H)

    rs_f.send(1, True)
    rs_f_steps = [(k, same) for k in range(2, z.H + 1) for same in (False, True)]

    def outputs(chunks):
        def run(stage):
            copies = []
            for i, w in enumerate(chunks):
                slot = stage.at[i % 2]
                if i >= 2:
                    copies[i - 2].wait()
                line.rs_final(w, slot)
                cp = pltpu.make_async_copy(slot.at[:, pl.ds(0, z.cols[w])], o_hbm[w - z.nk], s.s_loc.at[9 + i % 2])
                cp.start()
                copies.append(cp)
            for cp in copies[-2:]:
                cp.wait()

        pl.run_scoped(run, pltpu.VMEM((2, z.S, max(z.cols)), F32))

    def back_phase(dq, dk, dv, att):
        dk[...] = jnp.zeros_like(dk)
        dv[...] = jnp.zeros_like(dv)

        def back_block(qb):
            def pair(kb, diagonal):
                for g in range(z.nk):
                    at = pl.ds(kb * R, R) if diagonal else pl.ds(pl.multiple_of(kb * R, R), R)
                    q, do = s.q4[g, qb], s.do4[g, qb]
                    kk, vv = s.kk[g, at, :], s.vv[g, at, :]
                    e = jnp.exp2(dot(kk, q, NT) - s.lse[g, qb, 0:1, :])
                    pt = jnp.where(allowed(qb, kb, diagonal), e, 0.0)
                    dpt = dot(vv, do, NT)
                    ds = (pt * (dpt - s.dlt[g, qb, 0:1, :])).astype(BF)
                    dv[g, at, :] += dot(pt.astype(BF), do, NN)
                    dk[g, at, :] += dot(ds, q, NN)
                    if diagonal:
                        dq[g, qb] = dot(ds, kk, TN)
                    else:
                        dq[g, qb] += dot(ds, kk, TN)

            def off_diagonal(kb, _):
                pair(kb, False)
                return 0

            pair(qb, True)
            if qb > 0:
                lax.fori_loop(0, qb, off_diagonal, 0)

        line.ag_finish(z.WO)
        DB = 512

        def unpad(i, _):
            att[pl.ds(pl.multiple_of(i * R, R), R), :] = unpadded(i)
            return 0

        lax.fori_loop(0, T, unpad, 0)

        def tile(i, _):
            at = pl.ds(pl.multiple_of(i * DB, DB), DB)
            w_out[at, 0:z.HQ] = dot(s.mid[:, at], att[...], TN).astype(BF)
            return 0

        lax.fori_loop(0, D // DB, tile, 0)
        line.rs_sib_start(z.WO)
        line.rs_rest(z.WU)
        for qb in range(T):
            back_block(qb)
            if qb == min(1, T - 1):
                line.rs_sib_sum(z.WO)
                line.rs_first(z.WO)
            if qb == T - 1:
                line.rs_rest(z.WO)
            if rs_f_steps:
                rs_f.send(*rs_f_steps.pop(0))

        ag_m.finish()

        def unrotate(i, _):
            rows = pl.ds(pl.multiple_of(i * R, R), R)
            cs, sn = s.cos[rows, :], s.sin[rows, :]
            for g in range(z.nk):
                heads = []
                for j in range(z.G + 2):
                    if j < z.G:
                        v = dq[g, i, j * R:(j + 1) * R, :] * (HEAD ** -0.5)
                    elif j == z.G:
                        v = dk[g, rows, :] * LN2
                    else:
                        v = dv[g, rows, :]
                    if j <= z.G:
                        v = v * cs - pltpu.roll(v, 64, 1) * sn
                    heads.append(v.astype(BF))
                four = jnp.concatenate(heads, axis=1)
                s.dqkv[rows, g * z.HG:(g + 1) * z.HG] = dot(four, s.perm[...], NT).astype(BF)
            return 0

        lax.fori_loop(0, T, unrotate, 0)

    pl.run_scoped(
        back_phase,
        pltpu.VMEM((z.nk, T, z.G * R, LANES), F32),
        pltpu.VMEM((z.nk, L, LANES), F32),
        pltpu.VMEM((z.nk, L, LANES), F32),
        pltpu.VMEM((L, z.HQ), BF),
    )
    for step in rs_f_steps:
        rs_f.send(*step)

    def mixed_rows(i, _):
        lo = i * NR
        at = pl.ds(pl.multiple_of(lo, NR), NR)
        s.ogr[pl.ds(pl.multiple_of(own_off + lo, NR), NR), :] = (s.middle[at, :] + rs_f.rows(lo, NR)).astype(BF)
        return 0

    out_mixed = pltpu.make_async_copy(s.ogr.at[own_rows], mixed_hbm, s.s_loc.at[14])

    def qkv_outputs(stage, q_out, k_out, v_out):
        for g in range(z.nk):
            line.rs_final(g, stage.at[g])
        cuts = (0, gc, gc + HEAD, gc + 2 * HEAD)
        copies = []
        for i, out in enumerate((q_out, k_out, v_out)):
            parts = [stage[g, :, cuts[i]:cuts[i + 1]] for g in range(z.nk)]
            out[...] = jnp.concatenate(parts, axis=1) if z.nk > 1 else parts[0]
            copies.append(pltpu.make_async_copy(out, oqkv_hbm[i], s.s_loc.at[11 + i]))
            copies[-1].start()
        last()
        for cp in copies:
            cp.wait()

    def ffn_out():
        rs_f.arrive()
        lax.fori_loop(0, R // NR, mixed_rows, 0)
        out_mixed.start()

    if one_rbuf:
        ffn_out()
        free(1)
        await_free(1)

    rs_q = Scatter(ring, s.part, s.rbuf_a, s.s_rsS.at[3], s.s_rsR.at[3])

    def qkv_back(step):
        rows = pl.ds(ring.off(step), R)

        def cols(n, _):
            at = pl.ds(pl.multiple_of(n * NB, NB), NB)
            tot = dot(s.dqkv[rows, 0:z.HG], ws[0][at, :], NT)
            for g in range(1, z.nk):
                tot = tot + dot(s.dqkv[rows, g * z.HG:(g + 1) * z.HG], ws[g][at, :], NT)
            s.part[rows, at] = tot.astype(BF)
            return 0

        lax.fori_loop(0, D // NB, cols, 0)

    s.gs[c] = jnp.zeros_like(s.gs[c])

    def qkv_grads(k):
        if k == z.H:
            line.rs_sib_sum(z.nk - 1)
            line.rs_first(z.nk - 1)
            if not one_rbuf:
                ffn_out()
            for g in range(z.nk - 1):
                line.rs_rest(g)
            outputs([z.WG, z.WU])
        if k > 1:
            return
        outputs([z.WD])
        line.rs_finish(z.WD)
        for g in range(z.nk):
            def qkv_tile(i, _, g=g):
                at = pl.ds(pl.multiple_of(i * 512, 512), 512)
                grad = dot(s.normed[:, at], s.dqkv[:, g * z.HG:(g + 1) * z.HG], TN)
                part = jnp.sum(grad * ws[g][at, :].astype(F32), axis=-1, keepdims=True)
                s.gs[c, 0:1, at] += row_form(part)
                s.dwd[at, g * z.HG:(g + 1) * z.HG] = grad.astype(BF)
                return 0

            lax.fori_loop(0, D // 512, qkv_tile, 0)
            line.rs_sib_start(g)
            if g > 0:
                line.rs_sib_sum(g - 1)
                line.rs_first(g - 1)

    scatter(rs_q, qkv_back, qkv_grads)
    line.rs_rest(z.nk - 1)
    s.gs[c, 0:1, :] = s.gs[c, 0:1, :] / ga_ref[...]
    s.gs[c, 1:2, :] = s.gsum[0:1, :]

    def g_copy(stage, d, ref, slot, to):
        return pltpu.make_async_remote_copy(
            src_ref=ref.at[slot], dst_ref=ref.at[slot], send_sem=s.s_gS.at[stage, d], recv_sem=s.s_gR.at[stage, d],
            device_id=to, device_id_type=MESH,
        )

    g0 = g_copy(0, 0, s.gs, c, line.sibling)
    g0.start()
    g0.wait_recv()
    s.gz[p] = s.gs[0] + s.gs[1]
    g1 = [g_copy(1, d, s.gz, p, (rem(p + d, z.PZ) * 2 + c, t)) for d in range(1, z.PZ)]
    for cp in g1:
        cp.start()
    for cp in g1:
        cp.wait_recv()
    tot = s.gz[0]
    for q in range(1, z.PZ):
        tot = tot + s.gz[q]
    s.gt[t] = tot
    g2 = [g_copy(2, d, s.gt, t, (dp, rem(t + d, T))) for d in range(1, T)]
    for cp in g2:
        cp.start()
    def last_rows(i, _):
        lo = i * NR
        at = pl.ds(pl.multiple_of(lo, NR), NR)
        ng = rs_q.rows(lo, NR)
        x = s.xv[at, :].astype(F32)
        f = lax.rsqrt(jnp.mean(x * x, axis=-1, keepdims=True) + EPS)
        zz = x * f
        dz = ng * ga_ref[...]
        s.mgrad[at, :] += f * (dz - zz * jnp.mean(dz * zz, axis=-1, keepdims=True))
        return 0

    out_tg = pltpu.make_async_copy(s.mgrad, tg_hbm, s.s_loc.at[15])

    def last():
        rs_q.arrive()
        lax.fori_loop(0, R // NR, last_rows, 0)
        out_tg.start()

    outputs([z.WO])
    pl.run_scoped(
        qkv_outputs, pltpu.VMEM((z.nk, z.S, z.HG), F32), pltpu.VMEM((z.S, z.HQ), F32),
        pltpu.VMEM((z.S, z.nk * HEAD), F32), pltpu.VMEM((z.S, z.nk * HEAD), F32),
    )

    for cp in g2:
        cp.wait_recv()
    tot = s.gt[0]
    for q in range(1, T):
        tot = tot + s.gt[q]
    ga_out[...] = tot[0:1, :].reshape(D)
    gf_out[...] = tot[1:2, :].reshape(D)

    out_mixed.wait()
    rs_f.finish()
    out_tg.wait()
    rs_q.finish()
    g0.wait_send()
    for cp in g1 + g2:
        cp.wait_send()
    for w in list(range(z.nk)) + [z.WD]:
        line.ag_finish(w)
    for w in range(z.NW):
        if w != z.WD:
            line.rs_finish(w)


def body(tokens, seq_lengths, gain_attn, query_weight, key_matrix, value_matrix, out_weight,
         gain_ffn, gate_weight, up_weight, down_weight, out_grad):
    n_dp, n_tensor = lax.axis_size("dp"), lax.axis_size("tensor")
    z = Sizes(n_dp, n_tensor, tokens.shape[0], tokens.shape[1], query_weight.shape[1],
              key_matrix.shape[1], gate_weight.shape[1])
    shards = [
        query_weight, key_matrix, value_matrix,
        jnp.pad(out_weight.T, ((0, 0), (0, z.HO - z.HQ))), gate_weight, up_weight, down_weight.T,
    ]
    grads = [jax.ShapeDtypeStruct((z.S, n), F32) for n in (z.HQ, z.nk * HEAD, z.nk * HEAD) + z.cols[z.nk:]]
    j = np.arange(LANES) % 64
    freq = np.where(j < HEAD // 2, ROPE_BASE ** (-(2.0 * j) / HEAD), 0.0).astype(np.float32)[None, :]
    items = scratch_list(z)
    names = [name for name, _ in items]
    hbm = pl.BlockSpec(memory_space=pl.ANY)
    vmem = pl.BlockSpec(memory_space=pltpu.VMEM)
    flops = 2 * 3 * z.L * z.D * sum(z.cols)
    outs = pl.pallas_call(
        functools.partial(kernel, z, names),
        out_shape=(
            jax.ShapeDtypeStruct((z.R, z.D), BF),
            jax.ShapeDtypeStruct((z.R, z.D), F32),
            jax.ShapeDtypeStruct((z.D,), F32),
            jax.ShapeDtypeStruct((z.D,), F32),
            *grads,
        ),
        in_specs=[hbm, hbm, pl.BlockSpec(memory_space=pltpu.SMEM), vmem, vmem, vmem] + [hbm] * 7,
        out_specs=[hbm, hbm, vmem, vmem] + [hbm] * 7,
        scratch_shapes=[shape for _, shape in items],
        compiler_params=pltpu.CompilerParams(
            collective_id=0, has_side_effects=True, vmem_limit_bytes=67_000_000
        ),
        cost_estimate=pl.CostEstimate(flops=flops, bytes_accessed=16_000_000, transcendentals=0),
        name="layer",
    )(tokens, out_grad, seq_lengths, gain_attn, gain_ffn, jnp.asarray(freq), *shards)
    mixed, tokens_grad, ga_grad, gf_grad, q_g, k_g, v_g, out_g, gate_g, up_g, down_g = outs
    return (
        mixed, tokens_grad, ga_grad, q_g, k_g, v_g, out_g[:, :z.HQ].T, gf_grad, gate_g, up_g, down_g.T,
    )


def solution(mesh):
    rows = P(("dp", "tensor"), None)
    split, turned = P("dp", "tensor"), P("tensor", "dp")
    return jax.shard_map(
        body, mesh=mesh,
        in_specs=(rows, P("dp", None), P(), split, split, split, turned, P(), split, split, turned, rows),
        out_specs=(rows, rows, P(), split, split, split, turned, P(), split, split, turned),
        check_vma=False,
    )
```

```python
import functools

import jax
import jax.numpy as jnp
import numpy as np
from jax import lax
from jax.experimental import pallas as pl
from jax.experimental.pallas import tpu as pltpu
from jax.sharding import PartitionSpec as P

HEAD = 96
LANES = 128
EPS = 1e-05
ROPE_BASE = 100000.0
LOG2E = 1.4426950408889634
LN2 = 0.6931471805599453
BF = jnp.bfloat16
F32 = jnp.float32
MESH = pl.DeviceIdType.MESH
rem, div = lax.rem, lax.div

NN = (((1,), (0,)), ((), ()))
NT = (((1,), (1,)), ((), ()))
TN = (((0,), (0,)), ((), ()))


def dot(a, b, dims):
    return lax.dot_general(a, b, dims, preferred_element_type=F32)


class Sizes:
    def __init__(self, n_dp, n_tensor, rows, width, q_cols, k_cols, hidden):
        self.N, self.T, self.R, self.D = n_dp, n_tensor, rows, width
        self.PZ = n_dp // 2
        self.H = n_tensor // 2
        self.L = rows * n_tensor
        self.S = width // n_dp
        self.F = hidden
        self.nq, self.nk = q_cols // HEAD, k_cols // HEAD
        self.G = self.nq // self.nk
        self.nh = self.nq + 2 * self.nk
        self.HA, self.PA = self.nh * HEAD, self.nh * LANES
        self.HQ, self.PQ = self.nq * HEAD, self.nq * LANES
        self.HO = -(-self.HQ // LANES) * LANES
        self.HG, self.PG = (self.G + 2) * HEAD, (self.G + 2) * LANES
        self.cols = (self.HG,) * self.nk + (self.HO, hidden, hidden, hidden)
        self.NW = self.nk + 4
        self.WO, self.WG, self.WU, self.WD = range(self.nk, self.nk + 4)


def scratch_list(z):
    dma = pltpu.SemaphoreType.DMA
    items = [
        ("xv", pltpu.VMEM((z.R, z.D), BF)),
        ("normed", pltpu.VMEM((z.L, z.D), BF)),
        ("ogr", pltpu.VMEM((z.L, z.D), BF)),
        ("n2", pltpu.VMEM((z.L, z.D), BF)),
        ("part", pltpu.VMEM((z.L, z.D), BF)),
        ("rbuf_a", pltpu.VMEM((2, 2 * z.H - 1, z.R // 2, z.D), BF)),
        ("kin", pltpu.VMEM((z.S, z.nk * HEAD), BF)),
        ("vin", pltpu.VMEM((z.S, z.nk * HEAD), BF)),
        ("gain", pltpu.VMEM((8, z.D), F32)),
        ("dwd", pltpu.VMEM((z.D, z.F), BF)),
        ("perm", pltpu.VMEM((z.HG, z.PG), BF)),
        ("cos", pltpu.VMEM((z.L, LANES), F32)),
        ("sin", pltpu.VMEM((z.L, LANES), F32)),
        ("q4", pltpu.VMEM((z.nk, z.T, z.G * z.R, LANES), BF)),
        ("kk", pltpu.VMEM((z.nk, z.L, LANES), BF)),
        ("vv", pltpu.VMEM((z.nk, z.L, LANES), BF)),
        ("o4", pltpu.VMEM((z.nk, z.T, z.G * z.R, LANES), BF)),
        ("do4", pltpu.VMEM((z.nk, z.T, z.G * z.R, LANES), BF)),
        ("lse", pltpu.VMEM((z.nk, z.T, 1, z.G * z.R), F32)),
        ("dlt", pltpu.VMEM((z.nk, z.T, 1, z.G * z.R), F32)),
        ("middle", pltpu.VMEM((z.R, z.D), F32)),
        ("mgrad", pltpu.VMEM((z.R, z.D), F32)),
        ("gsum", pltpu.VMEM((1, z.D), F32)),
        ("gs", pltpu.VMEM((2, 2, z.D), F32)),
        ("gz", pltpu.VMEM((z.PZ, 2, z.D), F32)),
        ("gt", pltpu.VMEM((z.T, 2, z.D), F32)),
        ("s_loc", dma((16,))),
        ("s_agS", dma((4, 2, z.H + 1, 2))),
        ("s_agR", dma((4, 2, z.H + 1, 2))),
        ("s_rsS", dma((4, 2, z.H + 1, 2))),
        ("s_rsR", dma((4, 2, z.H + 1, 2))),
        ("s_zgS", dma((z.NW, z.PZ))),
        ("s_zgR", dma((z.NW, z.PZ))),
        ("s_sgS", dma((z.NW, z.PZ))),
        ("s_sgR", dma((z.NW, z.PZ))),
        ("s_zrS", dma((z.NW, z.PZ))),
        ("s_zrR", dma((z.NW, z.PZ))),
        ("s_srS", dma((z.NW, z.PZ))),
        ("s_srR", dma((z.NW, z.PZ))),
        ("s_free", pltpu.SemaphoreType.REGULAR((2,))),
        ("s_gS", dma((3, max(z.T, z.PZ)))),
        ("s_gR", dma((3, max(z.T, z.PZ)))),
    ]
    if z.HO != z.HQ:
        items.append(("qin", pltpu.VMEM((z.S, z.HQ), BF)))
    if z.T <= 4:
        items.append(("rbuf_b", pltpu.VMEM((2, 2 * z.H - 1, z.R // 2, z.D), BF)))
    for w in range(z.NW):
        items.append((f"w{w}", pltpu.VMEM((z.D, z.cols[w]), BF)))
        items.append((f"sib{w}", pltpu.VMEM((z.PZ, z.S, z.cols[w]), BF)))
        items.append((f"lin{w}", pltpu.VMEM((z.PZ, z.S, z.cols[w]), BF)))
    return items


class Ring:
    def __init__(self, z):
        self.z = z
        self.dp = lax.axis_index("dp")
        t = lax.axis_index("tensor")
        self.t = t
        ycount = z.T // 2
        x, y = rem(t, 2), div(t, 2)
        self.r = y * (1 - x) + (z.T - 1 - y) * x
        self.ycount = ycount
        self.to = ((self.dp, self.index(1)), (self.dp, self.index(-1)))

    def index(self, step):
        z = self.z
        r = rem(self.r + step + z.T, z.T)
        far = div(r, self.ycount)
        return (1 - far) * 2 * r + far * (2 * (z.T - 1 - r) + 1)

    def off(self, step):
        return pl.multiple_of(self.index(step) * self.z.R, self.z.R)


class Gather:
    def __init__(self, ring, buf, s_send, s_recv):
        self.ring, self.buf, self.ss, self.rs = ring, buf, s_send, s_recv
        self.half = ring.z.R // 2

    def last(self, d, h):
        return self.ring.z.H if h == d else self.ring.z.H - 1

    def copy(self, d, k, h):
        sign = -1 if d == 0 else 1
        origin = self.ring.off(sign * (k - 1))
        piece = self.buf.at[pl.ds(pl.multiple_of(origin + h * self.half, self.half), self.half)]
        return pltpu.make_async_remote_copy(
            src_ref=piece, dst_ref=piece, send_sem=self.ss.at[d, k, h], recv_sem=self.rs.at[d, k, h],
            device_id=self.ring.to[d], device_id_type=MESH,
        )

    def start(self):
        for same in (True, False):
            for d in (0, 1):
                h = d if same else 1 - d
                if self.last(d, h) >= 1:
                    self.copy(d, 1, h).start()

    def step(self, k, same):
        for d in (0, 1):
            h = d if same else 1 - d
            if k <= self.last(d, h):
                self.copy(d, k, h).wait_recv()
                if k + 1 <= self.last(d, h):
                    self.copy(d, k + 1, h).start()

    def finish(self):
        for d in (0, 1):
            for h in (0, 1):
                for k in range(1, self.last(d, h) + 1):
                    self.copy(d, k, h).wait_send()


class Scatter:
    def __init__(self, ring, buf, rbuf, s_send, s_recv):
        self.ring, self.buf, self.rbuf, self.ss, self.rs = ring, buf, rbuf, s_send, s_recv
        self.half = ring.z.R // 2

    def piece(self, step, h):
        off = self.ring.off(step)
        return self.buf.at[pl.ds(pl.multiple_of(off + h * self.half, self.half), self.half)]

    def copy(self, d, k, h):
        dist = self.ring.z.H - k + 1
        return pltpu.make_async_remote_copy(
            src_ref=self.piece(dist if d == 0 else -dist, h), dst_ref=self.rbuf.at[d, self.slot(d, k, h)],
            send_sem=self.ss.at[d, k, h], recv_sem=self.rs.at[d, k, h],
            device_id=self.ring.to[d], device_id_type=MESH,
        )

    def first(self, d, h):
        return 1 if h == d else 2

    def slot(self, d, k, h):
        return k - 1 if h == d else self.ring.z.H + k - 2

    def send(self, k, same, ways=(0, 1)):
        for d in ways:
            h = d if same else 1 - d
            if k < self.first(d, h):
                continue
            if k > self.first(d, h):
                self.copy(d, k - 1, h).wait_recv()
                dist = self.ring.z.H - k + 1
                piece = self.piece(dist if d == 0 else -dist, h)
                add_into(piece, self.rbuf.at[d, self.slot(d, k - 1, h)])
            self.copy(d, k, h).start()

    def arrive(self):
        for h in (0, 1):
            for d in (0, 1):
                if self.ring.z.H >= self.first(d, h):
                    self.copy(d, self.ring.z.H, h).wait_recv()

    def rows(self, lo, n):
        h = div(lo, self.half)
        last = self.ring.z.H - 1
        off = lo - h * self.half
        own = pl.ds(pl.multiple_of(self.ring.off(0) + lo, n), n)
        total = self.buf[own, :].astype(F32)
        for d in (0, 1):
            total = total + self.rbuf[d, last + last * (h if d == 0 else 1 - h), pl.ds(pl.multiple_of(off, n), n), :].astype(F32)
        return total

    def finish(self):
        for d in (0, 1):
            for h in (0, 1):
                for k in range(self.first(d, h), self.ring.z.H + 1):
                    self.copy(d, k, h).wait_send()


def add_into(dst, src):
    rows = dst.shape[0]
    step = 32

    def body(i, _):
        at = pl.ds(pl.multiple_of(i * step, step), step)
        dst[at, :] = (dst[at, :].astype(F32) + src[at, :].astype(F32)).astype(dst.dtype)
        return 0

    lax.fori_loop(0, rows // step, body, 0)


class Line:
    def __init__(self, z, s, ws, gs):
        self.z, self.s, self.ws, self.gs = z, s, ws, gs
        dp, t = lax.axis_index("dp"), lax.axis_index("tensor")
        self.t = t
        self.p, self.c = div(dp, 2), rem(dp, 2)
        self.sibling = (dp + 1 - 2 * self.c, t)

    def shard(self, w, q, core):
        return self.ws[w].at[pl.ds(pl.multiple_of((2 * q + core) * self.z.S, self.z.S), self.z.S)]

    def remote(self, src, dst, send, recv, to):
        return pltpu.make_async_remote_copy(
            src_ref=src, dst_ref=dst, send_sem=send, recv_sem=recv, device_id=to, device_id_type=MESH
        )

    def chip(self, q):
        return (2 * q + self.c, self.t)

    def others(self):
        return (2, 3, 1) if self.four else tuple(range(1, self.z.PZ))

    @property
    def four(self):
        return self.z.PZ == 4

    def only(self, d, chips, fn):
        if not self.four:
            fn()
        elif chips[d]:
            cond = self.p == chips[d][0]
            for q in chips[d][1:]:
                cond = cond | (self.p == q)
            pl.when(cond)(fn)

    def ag_copy(self, w, d):
        src = self.shard(w, self.p, self.c)
        to = self.chip(rem(self.p + d, self.z.PZ))
        return self.remote(src, src, self.s.s_zgS.at[w, d], self.s.s_zgR.at[w, self.p], to)

    def ag_relay_copy(self, w, q):
        src = self.shard(w, q, self.c)
        return self.remote(src, src, self.s.s_zgS.at[w, 0], self.s.s_zgR.at[w, q], self.chip(3 if q == 1 else 0))

    def ag_sib(self, w, q):
        src = self.shard(w, q, self.c)
        return self.remote(src, src, self.s.s_sgS.at[w, q], self.s.s_sgR.at[w, q], self.sibling)

    def ag_wait(self, w, q):
        src = self.shard(w, q, self.c)
        self.remote(src, src, self.s.s_zgS.at[w, 0], self.s.s_zgR.at[w, q], self.sibling).wait_recv()

    def ag_near(self, w):
        for d in (1, 3) if self.four else self.others():
            self.only(d, {1: (0, 1, 2), 3: (1, 2, 3)}, lambda d=d: self.ag_copy(w, d).start())
        self.ag_sib(w, self.p).start()

    def ag_far(self, w):
        if self.four:
            self.ag_relay(w)
            for d in (2, 3, 1):
                self.only(d, {1: (3,), 2: (0, 3), 3: (0,)}, lambda d=d: self.ag_copy(w, d).start())

    def ag_relay(self, w):
        for q, via in ((1, 2), (2, 1)):
            @pl.when(self.p == via)
            def _(q=q):
                self.ag_wait(w, q)
                self.ag_relay_copy(w, q).start()
                self.ag_sib(w, q).start()

    def ag_recv(self, w):
        order = (1, 2, 0, 3) if self.four else range(self.z.PZ)
        for q in order:
            here = self.p != q
            if self.four and q in (1, 2):
                here = here & (self.p != 3 - q)

            @pl.when(here)
            def _(q=q):
                self.ag_wait(w, q)
                self.ag_sib(w, q).start()

    def ag_drain(self, w):
        for q in range(self.z.PZ):
            self.ag_sib(w, q).wait_recv()

    def ag_finish(self, w):
        for d in self.others():
            self.only(d, {1: (0, 1, 2, 3), 2: (0, 3), 3: (0, 1, 2, 3)}, lambda d=d: self.ag_copy(w, d).wait_send())
        if self.four:
            for q, via in ((1, 2), (2, 1)):
                @pl.when(self.p == via)
                def _(q=q):
                    self.ag_relay_copy(w, q).wait_send()
        for q in range(self.z.PZ):
            self.ag_sib(w, q).wait_send()

    def gshard(self, w, q, core):
        return self.gs[w].at[pl.ds(pl.multiple_of((2 * q + core) * self.z.S, self.z.S), self.z.S)]

    def rs_sib_copy(self, w, q):
        return self.remote(
            self.gshard(w, q, 1 - self.c), getattr(self.s, f"sib{w}").at[q],
            self.s.s_srS.at[w, q], self.s.s_srR.at[w, q], self.sibling,
        )

    def rs_sib_start(self, w):
        for q in range(self.z.PZ):
            self.rs_sib_copy(w, q).start()

    def rs_sib_sum(self, w):
        for q in range(self.z.PZ):
            self.rs_sib_copy(w, q).wait_recv()
            add_into(self.gshard(w, q, self.c), getattr(self.s, f"sib{w}").at[q])

    def rs_copy(self, w, d):
        p = self.p
        q = rem(p + d, self.z.PZ)
        to, slot = q, p
        if self.four and d == 1:
            far = div(p, 3)
            to, slot = q + 2 * far, p - far
        if self.four and d == 3:
            far = 1 - div(p + 3, 4)
            to, slot = q - 2 * far, p + far
        return self.remote(
            self.gshard(w, q, self.c), getattr(self.s, f"lin{w}").at[slot],
            self.s.s_zrS.at[w, d], self.s.s_zrR.at[w, slot], self.chip(to),
        )

    def rs_wait(self, w, slot):
        lin = getattr(self.s, f"lin{w}")
        self.remote(
            lin.at[slot], lin.at[slot], self.s.s_zrS.at[w, 0], self.s.s_zrR.at[w, slot], self.sibling
        ).wait_recv()

    def rs_first(self, w):
        for d in (3, 1) if self.four else self.others():
            self.only(d, {3: (0, 1, 2), 1: (1, 2, 3)}, lambda d=d: self.rs_copy(w, d).start())

    def rs_rest(self, w):
        if self.four:
            for d in (2, 1, 3):
                self.only(d, {1: (0,), 2: (0, 3), 3: (3,)}, lambda d=d: self.rs_copy(w, d).start())
            self.rs_relay(w)

    def rs_relay(self, w):
        lin = getattr(self.s, f"lin{w}")
        for via in (1, 2):
            @pl.when(self.p == via)
            def _(via=via):
                self.rs_wait(w, via)
                add_into(self.gshard(w, (via + 2) % 4, self.c), lin.at[via])
                self.rs_copy(w, 2).start()

    def rs_final(self, w, out_vmem):
        p = self.p
        lin = getattr(self.s, f"lin{w}")
        out = out_vmem.at[:, pl.ds(0, self.z.cols[w])]
        copy_f32(out, self.gshard(w, p, self.c))
        for q in range(self.z.PZ):
            here = p != q
            if self.four and q in (0, 3):
                here = here & (p != 3 - q)

            @pl.when(here)
            def _(q=q):
                self.rs_wait(w, q)
                add_into(out, lin.at[q])

    def rs_finish(self, w):
        for q in range(self.z.PZ):
            self.rs_sib_copy(w, q).wait_send()
        for d in self.others():
            self.rs_copy(w, d).wait_send()


def copy_f32(dst, src):
    rows = dst.shape[0]
    step = 32

    def body(i, _):
        at = pl.ds(pl.multiple_of(i * step, step), step)
        dst[at, :] = src[at, :].astype(F32)
        return 0

    lax.fori_loop(0, rows // step, body, 0)


def kernel(z, names, *refs):
    (x_hbm, og_hbm, len_ref, ga_in, gf_in, freq_ref, *rest) = refs
    qkv_hbm, rest = rest[:3], rest[3:]
    w_hbm, rest = rest[:4], rest[4:]
    mixed_hbm, tg_hbm, ga_out, gf_out, *rest = rest
    oqkv_hbm, rest = rest[:3], rest[3:]
    o_hbm, rest = rest[:4], rest[4:]

    class Scratch:
        pass

    s = Scratch()
    for name, ref in zip(names, rest, strict=True):
        setattr(s, name, ref)
    ws = [getattr(s, f"w{w}") for w in range(z.NW)]
    w_out, w_gate, w_up, w_down = ws[z.nk:]
    s.mid, s.dqkv = s.n2, s.n2
    if z.HO == z.HQ:
        s.qin = getattr(s, f"sib{z.WO}").at[0]
    one_rbuf = not hasattr(s, "rbuf_b")
    if one_rbuf:
        s.rbuf_b = s.rbuf_a
    R, D, L, F, T = z.R, z.D, z.L, z.F, z.T
    ring = Ring(z)
    line = Line(z, s, ws, [s.dwd.at[:, pl.ds(g * z.HG, z.HG)] for g in range(z.nk)] + ws[z.nk:z.WD] + [s.dwd])
    dp, t, p, c = ring.dp, ring.t, line.p, line.c
    own_off = pl.multiple_of(t * R, R)
    own_rows = pl.ds(own_off, R)

    loc = [pltpu.make_async_copy(x_hbm, s.xv, s.s_loc.at[0]),
           pltpu.make_async_copy(og_hbm, s.ogr.at[own_rows], s.s_loc.at[1])]
    for i, (src, dst) in enumerate(zip(qkv_hbm, (s.qin, s.kin, s.vin), strict=True)):
        loc.append(pltpu.make_async_copy(src, dst, s.s_loc.at[2 + i]))
    for i, w in enumerate((z.WO, z.WG, z.WU, z.WD)):
        loc.append(pltpu.make_async_copy(w_hbm[i], line.shard(w, p, c), s.s_loc.at[5 + i]))
    for i in (2, 3, 4, 0, 5, 6, 1, 7, 8):
        loc[i].start()
    for i, ref in enumerate((ga_in, gf_in)):
        s.gain[i:i + 1, :] = ref[...].reshape(1, D)
    ga_ref, gf_ref = s.gain.at[0:1], s.gain.at[1:2]

    bar = pltpu.get_barrier_semaphore()
    peers = [line.sibling]
    peers += [(rem(p + d, z.PZ) * 2 + c, t) for d in range(1, z.PZ)]
    peers += [(dp, rem(t + d, T)) for d in range(1, T)]
    for peer in peers:
        pl.semaphore_signal(bar, 1, device_id=peer, device_id_type=MESH)
    pl.semaphore_wait(bar, len(peers))

    for i in (2, 3, 4):
        loc[i].wait()
    gc = z.G * HEAD
    for g in range(z.nk):
        line.shard(g, p, c)[...] = jnp.concatenate([
            s.qin[:, g * gc:(g + 1) * gc], s.kin[:, g * HEAD:(g + 1) * HEAD], s.vin[:, g * HEAD:(g + 1) * HEAD],
        ], axis=1)
        line.ag_near(g)

    loc[0].wait()
    NR = 32

    def norm_rows(i, _):
        at = pl.ds(pl.multiple_of(i * NR, NR), NR)
        x = s.xv[at, :].astype(F32)
        f = lax.rsqrt(jnp.mean(x * x, axis=-1, keepdims=True) + EPS)
        s.normed[pl.ds(pl.multiple_of(own_off + i * NR, NR), NR), :] = (x * f * ga_ref[...]).astype(BF)
        return 0

    lax.fori_loop(0, R // NR, norm_rows, 0)
    ag_x = Gather(ring, s.normed, s.s_agS.at[0], s.s_agR.at[0])
    ag_x.start()

    l0 = len_ref[0, 0]
    lane = lax.broadcasted_iota(jnp.int32, (R, LANES), 1)

    def table_rows(i, _):
        at = pl.ds(pl.multiple_of(i * R, R), R)
        place = lax.broadcasted_iota(jnp.int32, (R, LANES), 0) + i * R
        pos = place - jnp.where(place >= l0, l0, 0)
        ang = pos.astype(F32) * freq_ref[...]
        s.cos[at, :] = jnp.cos(ang)
        sn = jnp.sin(ang)
        s.sin[at, :] = jnp.where(lane < 64, -sn, sn)
        return 0

    lax.fori_loop(0, T, table_rows, 0)
    half = HEAD // 2
    rowi = lax.broadcasted_iota(jnp.int32, (z.HG, LANES), 0)
    coli = lax.broadcasted_iota(jnp.int32, (z.HG, LANES), 1)
    inside = (coli < half) | ((coli >= 64) & (coli < 64 + half))
    src = jnp.where(inside, jnp.where(coli < half, coli, coli - (64 - half)), -100 * HEAD)
    for h in range(z.G + 2):
        s.perm[:, h * LANES:(h + 1) * LANES] = jnp.where(rowi == src + h * HEAD, 1.0, 0.0).astype(BF)

    for g in range(z.nk):
        line.ag_far(g)
    ag_x.step(1, True)
    loc[1].wait()
    ag_og = Gather(ring, s.ogr, s.s_agS.at[1], s.s_agR.at[1])
    ag_x.step(1, False)
    loc[5].wait()
    line.ag_near(z.WO)

    wp = s.part
    for g in range(z.nk):
        line.ag_recv(g)
    line.ag_far(z.WO)
    loc[6].wait()
    line.ag_near(z.WG)
    for g in range(z.nk):
        line.ag_drain(g)
        wp[g * z.PG:(g + 1) * z.PG, :] = dot(s.perm[...], ws[g][...], (((0,), (1,)), ((), ()))).astype(BF)
    qscale = HEAD ** -0.5 * LOG2E

    def qkv(step):
        off = ring.off(step)
        blk = ring.index(step)
        a = s.normed[pl.ds(off, R), :]
        cs, sn = s.cos[pl.ds(off, R), :], s.sin[pl.ds(off, R), :]
        for g in range(z.nk):
            y = dot(a, wp[g * z.PG:(g + 1) * z.PG, :], NT)
            for j in range(z.G + 2):
                yj = y[:, j * LANES:(j + 1) * LANES]
                if j <= z.G:
                    rot = yj * cs + pltpu.roll(yj, 64, 1) * sn
                if j < z.G:
                    s.q4[g, blk, j * R:(j + 1) * R, :] = (rot * qscale).astype(BF)
                elif j == z.G:
                    s.kk[g, pl.ds(off, R), :] = rot.astype(BF)
                else:
                    s.vv[g, pl.ds(off, R), :] = yj.astype(BF)

    qkv(0)
    for k in range(1, z.H):
        if k > 1:
            ag_x.step(k, True)
            ag_x.step(k, False)
        qkv(k)
        qkv(-k)
    ag_x.step(z.H, True)
    qkv(z.H)
    ag_og.start()

    line.ag_recv(z.WO)
    line.ag_far(z.WG)
    loc[7].wait()
    line.ag_near(z.WU)

    def row_form(col):
        wide = jnp.broadcast_to(col, (col.shape[0], LANES))
        return jnp.transpose(wide)[0:1, :]

    GR = z.G * R

    def allowed(qb, kb, diagonal, heads=z.G):
        qs = rem(lax.broadcasted_iota(jnp.int32, (1, heads * R), 1), R) + qb * R
        keys = lax.broadcasted_iota(jnp.int32, (R, heads * R), 0) + kb * R
        ok = keys >= jnp.where(qs >= l0, l0, 0)
        return ok & (keys <= qs) if diagonal else ok

    HP = 1

    def attend(qb):
        def one(i, _):
            g, j = div(i, z.G // HP), rem(i, z.G // HP)
            at = pl.ds(pl.multiple_of(j * HP * R, R), HP * R)
            q = s.q4[g, qb, at, :]
            scores = []
            for kb in range(qb + 1):
                st = dot(s.kk[g, kb * R:(kb + 1) * R, :], q, NT)
                scores.append(jnp.where(allowed(qb, kb, kb == qb, HP), st, -1e30))
            peak = jnp.max(scores[0], axis=0, keepdims=True)
            for st in scores[1:]:
                peak = jnp.maximum(peak, jnp.max(st, axis=0, keepdims=True))
            total, out = 0.0, 0.0
            for kb in range(qb + 1):
                e = jnp.exp2(scores[kb] - peak)
                total = total + jnp.sum(e, axis=0, keepdims=True)
                out = out + dot(s.vv[g, kb * R:(kb + 1) * R, :], e.astype(BF), TN)
            s.o4[g, qb, at, :] = jnp.transpose(out / total).astype(BF)
            s.lse[g, qb, :, at] = peak + jnp.log2(total)
            return 0

        lax.fori_loop(0, z.nk * z.G // HP, one, 0)

    hops = [(k, same) for k in range(1, z.H + 1) for same in (True, False)]
    for qb in range(T):
        attend(qb)
        if qb == 0:
            ag_og.step(*hops.pop(0))

    ag_x.finish()
    rs_o = Scatter(ring, s.part, s.rbuf_a, s.s_rsS.at[0], s.s_rsR.at[0])
    NB = 768 if T <= 4 else 512

    qperm = s.perm[0:z.G * HEAD, 0:z.G * LANES]

    def unpadded(blk):
        out = []
        for g in range(z.nk):
            pads = [s.o4[g, blk, j * R:(j + 1) * R, :] for j in range(z.G)]
            out.append(dot(jnp.concatenate(pads, axis=1), qperm, NT).astype(BF))
        return jnp.concatenate(out, axis=1) if z.nk > 1 else out[0]

    def out_block(step):
        off, blk = ring.off(step), ring.index(step)
        a = unpadded(blk)

        def cols(n, _):
            at = pl.ds(pl.multiple_of(n * NB, NB), NB)
            s.part[pl.ds(off, R), at] = dot(a, w_out[at, 0:z.HQ], NT).astype(BF)
            return 0

        lax.fori_loop(0, D // NB, cols, 0)

    def scatter(rs, block, between=None):
        for k in range(1, z.H + 1):
            dist = z.H - k + 1
            block(dist)
            if k > 1:
                rs.send(k, False, (0,))
                block(-dist)
                rs.send(k, False, (1,))
            rs.send(k, True)
            if between is not None:
                between(k)
        block(0)

    line.ag_drain(z.WO)

    def between_o(k):
        if k == z.H:
            for hop in hops:
                ag_og.step(*hop)
            line.ag_recv(z.WG)
            line.ag_far(z.WU)
            loc[8].wait()
            line.ag_near(z.WD)

    scatter(rs_o, out_block, between_o)
    rs_o.arrive()

    def middle_rows(i, _):
        lo = i * NR
        at = pl.ds(pl.multiple_of(lo, NR), NR)
        m = s.xv[at, :].astype(F32) + rs_o.rows(lo, NR)
        s.middle[at, :] = m
        f = lax.rsqrt(jnp.mean(m * m, axis=-1, keepdims=True) + EPS)
        s.n2[pl.ds(pl.multiple_of(own_off + lo, NR), NR), :] = (m * f * gf_ref[...]).astype(BF)
        return 0

    lax.fori_loop(0, R // NR, middle_rows, 0)
    ag_n2 = Gather(ring, s.n2, s.s_agS.at[2], s.s_agR.at[2])
    ag_n2.start()
    ag_og.finish()

    ag_m = Gather(ring, s.mid, s.s_agS.at[3], s.s_agR.at[3])
    rs_n = Scatter(ring, s.part, s.rbuf_a, s.s_rsS.at[1], s.s_rsR.at[1])
    rs_f = Scatter(ring, s.ogr, s.rbuf_b, s.s_rsS.at[2], s.s_rsR.at[2])
    FB = 512 if T <= 4 else 256

    def free(i):
        for d in (0, 1):
            pl.semaphore_signal(s.s_free.at[i], 1, device_id=ring.to[d], device_id_type=MESH)

    def await_free(i):
        pl.semaphore_wait(s.s_free.at[i], 2)

    def ffn_phase(gl, ul, hid):
        def wgrad(w, rows_ref, act_ref):
            if w != z.WD:
                line.ag_finish(w)
            DB = 512

            def tile(i, _):
                at = pl.ds(pl.multiple_of(i * DB, DB), DB)
                line.gs[w][at, :] = dot(rows_ref[:, at], act_ref[...], TN).astype(BF)
                return 0

            lax.fori_loop(0, D // DB, tile, 0)
            line.rs_sib_start(w)

        def gate_up(step):
            rows = pl.ds(ring.off(step), R)

            def cols(n, _):
                at = pl.ds(pl.multiple_of(n * FB, FB), FB)
                a = s.n2[rows, :]
                g = dot(a, w_gate[:, at], NN)
                u = dot(a, w_up[:, at], NN)
                gl[rows, at] = g.astype(BF)
                ul[rows, at] = u.astype(BF)
                hid[rows, at] = (g / (1.0 + jnp.exp(-g)) * u).astype(BF)
                return 0

            lax.fori_loop(0, F // FB, cols, 0)

        line.ag_drain(z.WG)
        ag_n2.step(1, True)
        line.ag_far(z.WD)
        ag_n2.step(1, False)
        line.ag_recv(z.WU)
        line.ag_drain(z.WU)
        gate_up(0)
        for k in range(1, z.H):
            if k > 1:
                ag_n2.step(k, True)
                ag_n2.step(k, False)
            gate_up(k)
            gate_up(-k)
        ag_n2.step(z.H, True)
        gate_up(z.H)
        wgrad(z.WD, s.ogr, hid)
        rs_o.finish()
        line.ag_recv(z.WD)
        line.ag_drain(z.WD)

        def act_grads(step):
            rows = pl.ds(ring.off(step), R)

            def cols(n, _):
                at = pl.ds(pl.multiple_of(n * FB, FB), FB)
                hg = dot(s.ogr[rows, :], w_down[:, at], NN)
                g = gl[rows, at].astype(F32)
                u = ul[rows, at].astype(F32)
                sg = 1.0 / (1.0 + jnp.exp(-g))
                silu = g * sg
                gl[rows, at] = (hg * u * (sg + silu * (1.0 - sg))).astype(BF)
                ul[rows, at] = (hg * silu).astype(BF)
                return 0

            lax.fori_loop(0, F // FB, cols, 0)

            def back(n, _):
                at = pl.ds(pl.multiple_of(n * NB, NB), NB)
                s.part[rows, at] = (
                    dot(gl[rows, :], w_gate[at, :], NT) + dot(ul[rows, :], w_up[at, :], NT)
                ).astype(BF)
                return 0

            lax.fori_loop(0, D // NB, back, 0)

        def between_n(k):
            if k == 1:
                line.rs_sib_sum(z.WD)
                line.rs_first(z.WD)
            if k == z.H:
                line.rs_rest(z.WD)

        scatter(rs_n, act_grads, between_n)

        wgrad(z.WG, s.n2, gl)
        wgrad(z.WU, s.n2, ul)
        ag_n2.finish()
        free(0)
        line.rs_sib_sum(z.WG)
        line.rs_first(z.WG)
        rs_n.arrive()

        s.gsum[...] = jnp.zeros_like(s.gsum)

        def norm_back(i, _):
            lo = i * NR
            at = pl.ds(pl.multiple_of(lo, NR), NR)
            ng = rs_n.rows(lo, NR)
            m = s.middle[at, :]
            f = lax.rsqrt(jnp.mean(m * m, axis=-1, keepdims=True) + EPS)
            zz = m * f
            s.gsum[0:1, :] += jnp.sum(ng * zz, axis=0, keepdims=True)
            dz = ng * gf_ref[...]
            own = pl.ds(pl.multiple_of(own_off + lo, NR), NR)
            mg = s.ogr[own, :].astype(F32) + f * (dz - zz * jnp.mean(dz * zz, axis=-1, keepdims=True))
            s.mgrad[at, :] = mg
            s.mid[own, :] = mg.astype(BF)
            return 0

        lax.fori_loop(0, R // NR, norm_back, 0)
        rs_n.finish()
        await_free(0)
        ag_m.start()
        line.rs_sib_sum(z.WU)
        line.rs_first(z.WU)

        def down_block(step):
            rows = pl.ds(ring.off(step), R)

            def cols(n, _):
                at = pl.ds(pl.multiple_of(n * NB, NB), NB)
                s.ogr[rows, at] = dot(hid[rows, :], w_down[at, :], NT).astype(BF)
                return 0

            lax.fori_loop(0, D // NB, cols, 0)

        for k in range(1, z.H + 1):
            down_block(k)
            if k < z.H:
                down_block(-k)
        down_block(0)
        ag_m.step(1, True)
        line.rs_rest(z.WG)

    pl.run_scoped(ffn_phase, pltpu.VMEM((L, F), BF), pltpu.VMEM((L, F), BF), pltpu.VMEM((L, F), BF))

    def do_block(step):
        off, blk = ring.off(step), ring.index(step)
        a = dot(s.mid[pl.ds(off, R), :], w_out[:, 0:z.HQ], NN).astype(BF)
        for h in range(z.nq):
            g, j = h // z.G, h % z.G
            if j == 0:
                d = dot(a[:, g * z.G * HEAD:(g + 1) * z.G * HEAD], qperm, NN)
            dh = d[:, j * LANES:(j + 1) * LANES]
            at = pl.ds(j * R, R)
            s.do4[g, blk, at, :] = dh.astype(BF)
            dl = jnp.sum(dh * s.o4[g, blk, at, :].astype(F32), axis=-1, keepdims=True)
            s.dlt[g, blk, :, at] = row_form(dl)

    do_block(0)
    for k in range(1, z.H):
        if k > 1:
            ag_m.step(k, True)
        ag_m.step(k, False)
        do_block(k)
        do_block(-k)
    ag_m.step(z.H, True)
    do_block(z.H)

    rs_f.send(1, True)
    rs_f_steps = [(k, same) for k in range(2, z.H + 1) for same in (False, True)]

    def outputs(chunks):
        def run(stage):
            copies = []
            for i, w in enumerate(chunks):
                slot = stage.at[i % 2]
                if i >= 2:
                    copies[i - 2].wait()
                line.rs_final(w, slot)
                cp = pltpu.make_async_copy(slot.at[:, pl.ds(0, z.cols[w])], o_hbm[w - z.nk], s.s_loc.at[9 + i % 2])
                cp.start()
                copies.append(cp)
            for cp in copies[-2:]:
                cp.wait()

        pl.run_scoped(run, pltpu.VMEM((2, z.S, max(z.cols)), F32))

    def back_phase(dq, dk, dv, att):
        dk[...] = jnp.zeros_like(dk)
        dv[...] = jnp.zeros_like(dv)

        def back_block(qb):
            def pair(kb, diagonal):
                for g in range(z.nk):
                    at = pl.ds(kb * R, R) if diagonal else pl.ds(pl.multiple_of(kb * R, R), R)
                    q, do = s.q4[g, qb], s.do4[g, qb]
                    kk, vv = s.kk[g, at, :], s.vv[g, at, :]
                    e = jnp.exp2(dot(kk, q, NT) - s.lse[g, qb, 0:1, :])
                    pt = jnp.where(allowed(qb, kb, diagonal), e, 0.0)
                    dpt = dot(vv, do, NT)
                    ds = (pt * (dpt - s.dlt[g, qb, 0:1, :])).astype(BF)
                    dv[g, at, :] += dot(pt.astype(BF), do, NN)
                    dk[g, at, :] += dot(ds, q, NN)
                    if diagonal:
                        dq[g, qb] = dot(ds, kk, TN)
                    else:
                        dq[g, qb] += dot(ds, kk, TN)

            def off_diagonal(kb, _):
                pair(kb, False)
                return 0

            pair(qb, True)
            if qb > 0:
                lax.fori_loop(0, qb, off_diagonal, 0)

        line.ag_finish(z.WO)
        DB = 512

        def unpad(i, _):
            att[pl.ds(pl.multiple_of(i * R, R), R), :] = unpadded(i)
            return 0

        lax.fori_loop(0, T, unpad, 0)

        def tile(i, _):
            at = pl.ds(pl.multiple_of(i * DB, DB), DB)
            w_out[at, 0:z.HQ] = dot(s.mid[:, at], att[...], TN).astype(BF)
            return 0

        lax.fori_loop(0, D // DB, tile, 0)
        line.rs_sib_start(z.WO)
        line.rs_rest(z.WU)
        for qb in range(T):
            back_block(qb)
            if qb == min(1, T - 1):
                line.rs_sib_sum(z.WO)
                line.rs_first(z.WO)
            if qb == T - 1:
                line.rs_rest(z.WO)
            if rs_f_steps:
                rs_f.send(*rs_f_steps.pop(0))

        ag_m.finish()

        def unrotate(i, _):
            rows = pl.ds(pl.multiple_of(i * R, R), R)
            cs, sn = s.cos[rows, :], s.sin[rows, :]
            for g in range(z.nk):
                heads = []
                for j in range(z.G + 2):
                    if j < z.G:
                        v = dq[g, i, j * R:(j + 1) * R, :] * (HEAD ** -0.5)
                    elif j == z.G:
                        v = dk[g, rows, :] * LN2
                    else:
                        v = dv[g, rows, :]
                    if j <= z.G:
                        v = v * cs - pltpu.roll(v, 64, 1) * sn
                    heads.append(v.astype(BF))
                four = jnp.concatenate(heads, axis=1)
                s.dqkv[rows, g * z.HG:(g + 1) * z.HG] = dot(four, s.perm[...], NT).astype(BF)
            return 0

        lax.fori_loop(0, T, unrotate, 0)

    pl.run_scoped(
        back_phase,
        pltpu.VMEM((z.nk, T, z.G * R, LANES), F32),
        pltpu.VMEM((z.nk, L, LANES), F32),
        pltpu.VMEM((z.nk, L, LANES), F32),
        pltpu.VMEM((L, z.HQ), BF),
    )
    for step in rs_f_steps:
        rs_f.send(*step)

    def mixed_rows(i, _):
        lo = i * NR
        at = pl.ds(pl.multiple_of(lo, NR), NR)
        s.ogr[pl.ds(pl.multiple_of(own_off + lo, NR), NR), :] = (s.middle[at, :] + rs_f.rows(lo, NR)).astype(BF)
        return 0

    out_mixed = pltpu.make_async_copy(s.ogr.at[own_rows], mixed_hbm, s.s_loc.at[14])

    def qkv_outputs(stage, q_out, k_out, v_out):
        last()
        for g in range(z.nk):
            line.rs_final(g, stage.at[g])
        cuts = (0, gc, gc + HEAD, gc + 2 * HEAD)
        copies = []
        for i, out in enumerate((q_out, k_out, v_out)):
            parts = [stage[g, :, cuts[i]:cuts[i + 1]] for g in range(z.nk)]
            out[...] = jnp.concatenate(parts, axis=1) if z.nk > 1 else parts[0]
            copies.append(pltpu.make_async_copy(out, oqkv_hbm[i], s.s_loc.at[11 + i]))
            copies[-1].start()
        for cp in copies:
            cp.wait()

    def ffn_out():
        rs_f.arrive()
        lax.fori_loop(0, R // NR, mixed_rows, 0)
        out_mixed.start()

    if one_rbuf:
        ffn_out()
        free(1)
        await_free(1)

    rs_q = Scatter(ring, s.part, s.rbuf_a, s.s_rsS.at[3], s.s_rsR.at[3])

    def qkv_back(step):
        rows = pl.ds(ring.off(step), R)

        def cols(n, _):
            at = pl.ds(pl.multiple_of(n * NB, NB), NB)
            tot = dot(s.dqkv[rows, 0:z.HG], ws[0][at, :], NT)
            for g in range(1, z.nk):
                tot = tot + dot(s.dqkv[rows, g * z.HG:(g + 1) * z.HG], ws[g][at, :], NT)
            s.part[rows, at] = tot.astype(BF)
            return 0

        lax.fori_loop(0, D // NB, cols, 0)

    s.gs[c] = jnp.zeros_like(s.gs[c])

    def qkv_grads(k):
        if k == z.H:
            line.rs_sib_sum(z.nk - 1)
            line.rs_first(z.nk - 1)
            for g in range(z.nk - 1):
                line.rs_rest(g)
            if not one_rbuf:
                ffn_out()
        if k > 1:
            return
        outputs([z.WD])
        line.rs_finish(z.WD)
        for g in range(z.nk):
            def qkv_tile(i, _, g=g):
                at = pl.ds(pl.multiple_of(i * 512, 512), 512)
                grad = dot(s.normed[:, at], s.dqkv[:, g * z.HG:(g + 1) * z.HG], TN)
                part = jnp.sum(grad * ws[g][at, :].astype(F32), axis=-1, keepdims=True)
                s.gs[c, 0:1, at] += row_form(part)
                s.dwd[at, g * z.HG:(g + 1) * z.HG] = grad.astype(BF)
                return 0

            lax.fori_loop(0, D // 512, qkv_tile, 0)
            line.rs_sib_start(g)
            if g > 0:
                line.rs_sib_sum(g - 1)
                line.rs_first(g - 1)

    scatter(rs_q, qkv_back, qkv_grads)
    line.rs_rest(z.nk - 1)
    s.gs[c, 0:1, :] = s.gs[c, 0:1, :] / ga_ref[...]
    s.gs[c, 1:2, :] = s.gsum[0:1, :]

    def g_copy(stage, d, ref, slot, to):
        return pltpu.make_async_remote_copy(
            src_ref=ref.at[slot], dst_ref=ref.at[slot], send_sem=s.s_gS.at[stage, d], recv_sem=s.s_gR.at[stage, d],
            device_id=to, device_id_type=MESH,
        )

    g0 = g_copy(0, 0, s.gs, c, line.sibling)
    g0.start()
    g0.wait_recv()
    s.gz[p] = s.gs[0] + s.gs[1]
    g1 = [g_copy(1, d, s.gz, p, (rem(p + d, z.PZ) * 2 + c, t)) for d in range(1, z.PZ)]
    for cp in g1:
        cp.start()
    for cp in g1:
        cp.wait_recv()
    tot = s.gz[0]
    for q in range(1, z.PZ):
        tot = tot + s.gz[q]
    s.gt[t] = tot
    g2 = [g_copy(2, d, s.gt, t, (dp, rem(t + d, T))) for d in range(1, T)]
    for cp in g2:
        cp.start()
    def last_rows(i, _):
        lo = i * NR
        at = pl.ds(pl.multiple_of(lo, NR), NR)
        ng = rs_q.rows(lo, NR)
        x = s.xv[at, :].astype(F32)
        f = lax.rsqrt(jnp.mean(x * x, axis=-1, keepdims=True) + EPS)
        zz = x * f
        dz = ng * ga_ref[...]
        s.mgrad[at, :] += f * (dz - zz * jnp.mean(dz * zz, axis=-1, keepdims=True))
        return 0

    out_tg = pltpu.make_async_copy(s.mgrad, tg_hbm, s.s_loc.at[15])

    def last():
        rs_q.arrive()
        lax.fori_loop(0, R // NR, last_rows, 0)
        out_tg.start()

    outputs([z.WG, z.WU, z.WO])
    pl.run_scoped(
        qkv_outputs, pltpu.VMEM((z.nk, z.S, z.HG), F32), pltpu.VMEM((z.S, z.HQ), F32),
        pltpu.VMEM((z.S, z.nk * HEAD), F32), pltpu.VMEM((z.S, z.nk * HEAD), F32),
    )

    for cp in g2:
        cp.wait_recv()
    tot = s.gt[0]
    for q in range(1, T):
        tot = tot + s.gt[q]
    ga_out[...] = tot[0:1, :].reshape(D)
    gf_out[...] = tot[1:2, :].reshape(D)

    out_mixed.wait()
    rs_f.finish()
    out_tg.wait()
    rs_q.finish()
    g0.wait_send()
    for cp in g1 + g2:
        cp.wait_send()
    for w in list(range(z.nk)) + [z.WD]:
        line.ag_finish(w)
    for w in range(z.NW):
        if w != z.WD:
            line.rs_finish(w)


def hand_out(count, *refs):
    src, dst, sem, held = refs[:count], refs[count:2 * count], refs[2 * count], refs[2 * count + 1:]
    first = [pltpu.make_async_copy(a, v, sem.at[0, i]) for i, (a, v) in enumerate(zip(src, held, strict=True))]
    second = [pltpu.make_async_copy(v, b, sem.at[1, i]) for i, (b, v) in enumerate(zip(dst, held, strict=True))]
    for cp in first:
        cp.start()
    for cp, onward in zip(first, second, strict=True):
        cp.wait()
        onward.start()
    for cp in second:
        cp.wait()


def body(tokens, seq_lengths, gain_attn, query_weight, key_matrix, value_matrix, out_weight,
         gain_ffn, gate_weight, up_weight, down_weight, out_grad):
    n_dp, n_tensor = lax.axis_size("dp"), lax.axis_size("tensor")
    z = Sizes(n_dp, n_tensor, tokens.shape[0], tokens.shape[1], query_weight.shape[1],
              key_matrix.shape[1], gate_weight.shape[1])
    shards = [
        query_weight, key_matrix, value_matrix,
        jnp.pad(out_weight.T, ((0, 0), (0, z.HO - z.HQ))), gate_weight, up_weight, down_weight.T,
    ]
    grads = [jax.ShapeDtypeStruct((z.S, n), F32) for n in (z.HQ, z.nk * HEAD, z.nk * HEAD) + z.cols[z.nk:]]
    j = np.arange(LANES) % 64
    freq = np.where(j < HEAD // 2, ROPE_BASE ** (-(2.0 * j) / HEAD), 0.0).astype(np.float32)[None, :]
    items = scratch_list(z)
    names = [name for name, _ in items]
    hbm = pl.BlockSpec(memory_space=pl.ANY)
    vmem = pl.BlockSpec(memory_space=pltpu.VMEM)
    flops = 2 * 3 * z.L * z.D * sum(z.cols)
    outs = pl.pallas_call(
        functools.partial(kernel, z, names),
        out_shape=(
            jax.ShapeDtypeStruct((z.R, z.D), BF),
            jax.ShapeDtypeStruct((z.R, z.D), F32),
            jax.ShapeDtypeStruct((z.D,), F32),
            jax.ShapeDtypeStruct((z.D,), F32),
            *grads,
        ),
        in_specs=[hbm, hbm, pl.BlockSpec(memory_space=pltpu.SMEM), vmem, vmem, vmem] + [hbm] * 7,
        out_specs=[hbm, hbm, vmem, vmem] + [hbm] * 7,
        scratch_shapes=[shape for _, shape in items],
        compiler_params=pltpu.CompilerParams(
            collective_id=0, has_side_effects=True, vmem_limit_bytes=67_000_000
        ),
        cost_estimate=pl.CostEstimate(flops=flops, bytes_accessed=16_000_000, transcendentals=0),
        name="layer",
    )(tokens, out_grad, seq_lengths, gain_attn, gain_ffn, jnp.asarray(freq), *shards)
    count = len(outs)
    shapes = [jax.ShapeDtypeStruct(a.shape, a.dtype) for a in outs]
    outs = pl.pallas_call(
        functools.partial(hand_out, count),
        out_shape=tuple(shapes),
        in_specs=[hbm] * count, out_specs=[hbm] * count,
        scratch_shapes=[pltpu.SemaphoreType.DMA((2, count))] + [pltpu.VMEM(a.shape, a.dtype) for a in shapes],
        compiler_params=pltpu.CompilerParams(vmem_limit_bytes=67_000_000),
        name="hand_out",
    )(*outs)
    mixed, tokens_grad, ga_grad, gf_grad, q_g, k_g, v_g, out_g, gate_g, up_g, down_g = outs
    return (
        mixed, tokens_grad, ga_grad, q_g, k_g, v_g, out_g[:, :z.HQ].T, gf_grad, gate_g, up_g, down_g.T,
    )


def solution(mesh):
    rows = P(("dp", "tensor"), None)
    split, turned = P("dp", "tensor"), P("tensor", "dp")
    return jax.shard_map(
        body, mesh=mesh,
        in_specs=(rows, P("dp", None), P(), split, split, split, turned, P(), split, split, turned, rows),
        out_specs=(rows, rows, P(), split, split, split, turned, P(), split, split, turned),
        check_vma=False,
    )
```

```python
import functools

import jax
import jax.numpy as jnp
import numpy as np
from jax import lax
from jax.experimental import pallas as pl
from jax.experimental.pallas import tpu as pltpu
from jax.sharding import PartitionSpec as P

HEAD = 96
LANES = 128
EPS = 1e-05
ROPE_BASE = 100000.0
LOG2E = 1.4426950408889634
LN2 = 0.6931471805599453
BF = jnp.bfloat16
F32 = jnp.float32
MESH = pl.DeviceIdType.MESH
rem, div = lax.rem, lax.div

NN = (((1,), (0,)), ((), ()))
NT = (((1,), (1,)), ((), ()))
TN = (((0,), (0,)), ((), ()))


def dot(a, b, dims):
    return lax.dot_general(a, b, dims, preferred_element_type=F32)


class Sizes:
    def __init__(self, n_dp, n_tensor, rows, width, q_cols, k_cols, hidden):
        self.N, self.T, self.R, self.D = n_dp, n_tensor, rows, width
        self.PZ = n_dp // 2
        self.H = n_tensor // 2
        self.L = rows * n_tensor
        self.S = width // n_dp
        self.F = hidden
        self.nq, self.nk = q_cols // HEAD, k_cols // HEAD
        self.G = self.nq // self.nk
        self.nh = self.nq + 2 * self.nk
        self.HA, self.PA = self.nh * HEAD, self.nh * LANES
        self.HQ, self.PQ = self.nq * HEAD, self.nq * LANES
        self.HO = -(-self.HQ // LANES) * LANES
        self.HG, self.PG = (self.G + 2) * HEAD, (self.G + 2) * LANES
        self.cols = (self.HG,) * self.nk + (self.HO, hidden, hidden, hidden)
        self.NW = self.nk + 4
        self.WO, self.WG, self.WU, self.WD = range(self.nk, self.nk + 4)


def scratch_list(z):
    dma = pltpu.SemaphoreType.DMA
    items = [
        ("xv", pltpu.VMEM((z.R, z.D), BF)),
        ("normed", pltpu.VMEM((z.L, z.D), BF)),
        ("ogr", pltpu.VMEM((z.L, z.D), BF)),
        ("n2", pltpu.VMEM((z.L, z.D), BF)),
        ("part", pltpu.VMEM((z.L, z.D), BF)),
        ("rbuf_a", pltpu.VMEM((2, 2 * z.H - 1, z.R // 2, z.D), BF)),
        ("kin", pltpu.VMEM((z.S, z.nk * HEAD), BF)),
        ("vin", pltpu.VMEM((z.S, z.nk * HEAD), BF)),
        ("gain", pltpu.VMEM((8, z.D), F32)),
        ("dwd", pltpu.VMEM((z.D, z.F), BF)),
        ("perm", pltpu.VMEM((z.HG, z.PG), BF)),
        ("cos", pltpu.VMEM((z.L, LANES), F32)),
        ("sin", pltpu.VMEM((z.L, LANES), F32)),
        ("q4", pltpu.VMEM((z.nk, z.T, z.G * z.R, LANES), BF)),
        ("kk", pltpu.VMEM((z.nk, z.L, LANES), BF)),
        ("vv", pltpu.VMEM((z.nk, z.L, LANES), BF)),
        ("o4", pltpu.VMEM((z.nk, z.T, z.G * z.R, LANES), BF)),
        ("do4", pltpu.VMEM((z.nk, z.T, z.G * z.R, LANES), BF)),
        ("lse", pltpu.VMEM((z.nk, z.T, 1, z.G * z.R), F32)),
        ("dlt", pltpu.VMEM((z.nk, z.T, 1, z.G * z.R), F32)),
        ("middle", pltpu.VMEM((z.R, z.D), F32)),
        ("mgrad", pltpu.VMEM((z.R, z.D), F32)),
        ("gsum", pltpu.VMEM((1, z.D), F32)),
        ("gs", pltpu.VMEM((2, 2, z.D), F32)),
        ("gz", pltpu.VMEM((z.PZ, 2, z.D), F32)),
        ("gt", pltpu.VMEM((z.T, 2, z.D), F32)),
        ("s_loc", dma((16,))),
        ("s_agS", dma((4, 2, z.H + 1, 2))),
        ("s_agR", dma((4, 2, z.H + 1, 2))),
        ("s_rsS", dma((4, 2, z.H + 1, 2))),
        ("s_rsR", dma((4, 2, z.H + 1, 2))),
        ("s_zgS", dma((z.NW, z.PZ))),
        ("s_zgR", dma((z.NW, z.PZ))),
        ("s_sgS", dma((z.NW, z.PZ))),
        ("s_sgR", dma((z.NW, z.PZ))),
        ("s_zrS", dma((z.NW, z.PZ))),
        ("s_zrR", dma((z.NW, z.PZ))),
        ("s_srS", dma((z.NW, z.PZ))),
        ("s_srR", dma((z.NW, z.PZ))),
        ("s_free", pltpu.SemaphoreType.REGULAR((2,))),
        ("s_gS", dma((3, max(z.T, z.PZ)))),
        ("s_gR", dma((3, max(z.T, z.PZ)))),
    ]
    if z.HO != z.HQ:
        items.append(("qin", pltpu.VMEM((z.S, z.HQ), BF)))
    if z.T <= 4:
        items.append(("rbuf_b", pltpu.VMEM((2, 2 * z.H - 1, z.R // 2, z.D), BF)))
    for w in range(z.NW):
        items.append((f"w{w}", pltpu.VMEM((z.D, z.cols[w]), BF)))
        items.append((f"sib{w}", pltpu.VMEM((z.PZ, z.S, z.cols[w]), BF)))
        items.append((f"lin{w}", pltpu.VMEM((z.PZ, z.S, z.cols[w]), BF)))
    return items


class Ring:
    def __init__(self, z):
        self.z = z
        self.dp = lax.axis_index("dp")
        t = lax.axis_index("tensor")
        self.t = t
        ycount = z.T // 2
        x, y = rem(t, 2), div(t, 2)
        self.r = y * (1 - x) + (z.T - 1 - y) * x
        self.ycount = ycount
        self.to = ((self.dp, self.index(1)), (self.dp, self.index(-1)))

    def index(self, step):
        z = self.z
        r = rem(self.r + step + z.T, z.T)
        far = div(r, self.ycount)
        return (1 - far) * 2 * r + far * (2 * (z.T - 1 - r) + 1)

    def off(self, step):
        return pl.multiple_of(self.index(step) * self.z.R, self.z.R)


class Gather:
    def __init__(self, ring, buf, s_send, s_recv):
        self.ring, self.buf, self.ss, self.rs = ring, buf, s_send, s_recv
        self.half = ring.z.R // 2

    def last(self, d, h):
        return self.ring.z.H if h == d else self.ring.z.H - 1

    def copy(self, d, k, h):
        sign = -1 if d == 0 else 1
        origin = self.ring.off(sign * (k - 1))
        piece = self.buf.at[pl.ds(pl.multiple_of(origin + h * self.half, self.half), self.half)]
        return pltpu.make_async_remote_copy(
            src_ref=piece, dst_ref=piece, send_sem=self.ss.at[d, k, h], recv_sem=self.rs.at[d, k, h],
            device_id=self.ring.to[d], device_id_type=MESH,
        )

    def start(self):
        for same in (True, False):
            for d in (0, 1):
                h = d if same else 1 - d
                if self.last(d, h) >= 1:
                    self.copy(d, 1, h).start()

    def step(self, k, same):
        for d in (0, 1):
            h = d if same else 1 - d
            if k <= self.last(d, h):
                self.copy(d, k, h).wait_recv()
                if k + 1 <= self.last(d, h):
                    self.copy(d, k + 1, h).start()

    def finish(self):
        for d in (0, 1):
            for h in (0, 1):
                for k in range(1, self.last(d, h) + 1):
                    self.copy(d, k, h).wait_send()


class Scatter:
    def __init__(self, ring, buf, rbuf, s_send, s_recv):
        self.ring, self.buf, self.rbuf, self.ss, self.rs = ring, buf, rbuf, s_send, s_recv
        self.half = ring.z.R // 2

    def piece(self, step, h):
        off = self.ring.off(step)
        return self.buf.at[pl.ds(pl.multiple_of(off + h * self.half, self.half), self.half)]

    def copy(self, d, k, h):
        dist = self.ring.z.H - k + 1
        return pltpu.make_async_remote_copy(
            src_ref=self.piece(dist if d == 0 else -dist, h), dst_ref=self.rbuf.at[d, self.slot(d, k, h)],
            send_sem=self.ss.at[d, k, h], recv_sem=self.rs.at[d, k, h],
            device_id=self.ring.to[d], device_id_type=MESH,
        )

    def first(self, d, h):
        return 1 if h == d else 2

    def slot(self, d, k, h):
        return k - 1 if h == d else self.ring.z.H + k - 2

    def send(self, k, same, ways=(0, 1)):
        for d in ways:
            h = d if same else 1 - d
            if k < self.first(d, h):
                continue
            if k > self.first(d, h):
                self.copy(d, k - 1, h).wait_recv()
                dist = self.ring.z.H - k + 1
                piece = self.piece(dist if d == 0 else -dist, h)
                add_into(piece, self.rbuf.at[d, self.slot(d, k - 1, h)])
            self.copy(d, k, h).start()

    def arrive(self):
        for h in (0, 1):
            for d in (0, 1):
                if self.ring.z.H >= self.first(d, h):
                    self.copy(d, self.ring.z.H, h).wait_recv()

    def rows(self, lo, n):
        h = div(lo, self.half)
        last = self.ring.z.H - 1
        off = lo - h * self.half
        own = pl.ds(pl.multiple_of(self.ring.off(0) + lo, n), n)
        total = self.buf[own, :].astype(F32)
        for d in (0, 1):
            total = total + self.rbuf[d, last + last * (h if d == 0 else 1 - h), pl.ds(pl.multiple_of(off, n), n), :].astype(F32)
        return total

    def finish(self):
        for d in (0, 1):
            for h in (0, 1):
                for k in range(self.first(d, h), self.ring.z.H + 1):
                    self.copy(d, k, h).wait_send()


def add_into(dst, src):
    rows = dst.shape[0]
    step = 32

    def body(i, _):
        at = pl.ds(pl.multiple_of(i * step, step), step)
        dst[at, :] = (dst[at, :].astype(F32) + src[at, :].astype(F32)).astype(dst.dtype)
        return 0

    lax.fori_loop(0, rows // step, body, 0)


class Line:
    def __init__(self, z, s, ws, gs):
        self.z, self.s, self.ws, self.gs = z, s, ws, gs
        dp, t = lax.axis_index("dp"), lax.axis_index("tensor")
        self.t = t
        self.p, self.c = div(dp, 2), rem(dp, 2)
        self.sibling = (dp + 1 - 2 * self.c, t)

    def shard(self, w, q, core):
        return self.ws[w].at[pl.ds(pl.multiple_of((2 * q + core) * self.z.S, self.z.S), self.z.S)]

    def remote(self, src, dst, send, recv, to):
        return pltpu.make_async_remote_copy(
            src_ref=src, dst_ref=dst, send_sem=send, recv_sem=recv, device_id=to, device_id_type=MESH
        )

    def chip(self, q):
        return (2 * q + self.c, self.t)

    def others(self):
        return (2, 3, 1) if self.four else tuple(range(1, self.z.PZ))

    @property
    def four(self):
        return self.z.PZ == 4

    def only(self, d, chips, fn):
        if not self.four:
            fn()
        elif chips[d]:
            cond = self.p == chips[d][0]
            for q in chips[d][1:]:
                cond = cond | (self.p == q)
            pl.when(cond)(fn)

    def ag_copy(self, w, d):
        src = self.shard(w, self.p, self.c)
        to = self.chip(rem(self.p + d, self.z.PZ))
        return self.remote(src, src, self.s.s_zgS.at[w, d], self.s.s_zgR.at[w, self.p], to)

    def ag_relay_copy(self, w, q):
        src = self.shard(w, q, self.c)
        return self.remote(src, src, self.s.s_zgS.at[w, 0], self.s.s_zgR.at[w, q], self.chip(3 if q == 1 else 0))

    def ag_sib(self, w, q):
        src = self.shard(w, q, self.c)
        return self.remote(src, src, self.s.s_sgS.at[w, q], self.s.s_sgR.at[w, q], self.sibling)

    def ag_wait(self, w, q):
        src = self.shard(w, q, self.c)
        self.remote(src, src, self.s.s_zgS.at[w, 0], self.s.s_zgR.at[w, q], self.sibling).wait_recv()

    def ag_near(self, w):
        for d in (1, 3) if self.four else self.others():
            self.only(d, {1: (0, 1, 2), 3: (1, 2, 3)}, lambda d=d: self.ag_copy(w, d).start())
        self.ag_sib(w, self.p).start()

    def ag_far(self, w):
        if self.four:
            self.ag_relay(w)
            for d in (2, 3, 1):
                self.only(d, {1: (3,), 2: (0, 3), 3: (0,)}, lambda d=d: self.ag_copy(w, d).start())

    def ag_relay(self, w):
        for q, via in ((1, 2), (2, 1)):
            @pl.when(self.p == via)
            def _(q=q):
                self.ag_wait(w, q)
                self.ag_relay_copy(w, q).start()
                self.ag_sib(w, q).start()

    def ag_recv(self, w):
        order = (1, 2, 0, 3) if self.four else range(self.z.PZ)
        for q in order:
            here = self.p != q
            if self.four and q in (1, 2):
                here = here & (self.p != 3 - q)

            @pl.when(here)
            def _(q=q):
                self.ag_wait(w, q)
                self.ag_sib(w, q).start()

    def ag_drain(self, w):
        for q in range(self.z.PZ):
            self.ag_sib(w, q).wait_recv()

    def ag_finish(self, w):
        for d in self.others():
            self.only(d, {1: (0, 1, 2, 3), 2: (0, 3), 3: (0, 1, 2, 3)}, lambda d=d: self.ag_copy(w, d).wait_send())
        if self.four:
            for q, via in ((1, 2), (2, 1)):
                @pl.when(self.p == via)
                def _(q=q):
                    self.ag_relay_copy(w, q).wait_send()
        for q in range(self.z.PZ):
            self.ag_sib(w, q).wait_send()

    def gshard(self, w, q, core):
        return self.gs[w].at[pl.ds(pl.multiple_of((2 * q + core) * self.z.S, self.z.S), self.z.S)]

    def rs_sib_copy(self, w, q):
        return self.remote(
            self.gshard(w, q, 1 - self.c), getattr(self.s, f"sib{w}").at[q],
            self.s.s_srS.at[w, q], self.s.s_srR.at[w, q], self.sibling,
        )

    def rs_sib_start(self, w):
        for q in range(self.z.PZ):
            self.rs_sib_copy(w, q).start()

    def rs_sib_sum(self, w):
        for q in range(self.z.PZ):
            self.rs_sib_copy(w, q).wait_recv()
            add_into(self.gshard(w, q, self.c), getattr(self.s, f"sib{w}").at[q])

    def rs_copy(self, w, d):
        p = self.p
        q = rem(p + d, self.z.PZ)
        to, slot = q, p
        if self.four and d == 1:
            far = div(p, 3)
            to, slot = q + 2 * far, p - far
        if self.four and d == 3:
            far = 1 - div(p + 3, 4)
            to, slot = q - 2 * far, p + far
        return self.remote(
            self.gshard(w, q, self.c), getattr(self.s, f"lin{w}").at[slot],
            self.s.s_zrS.at[w, d], self.s.s_zrR.at[w, slot], self.chip(to),
        )

    def rs_wait(self, w, slot):
        lin = getattr(self.s, f"lin{w}")
        self.remote(
            lin.at[slot], lin.at[slot], self.s.s_zrS.at[w, 0], self.s.s_zrR.at[w, slot], self.sibling
        ).wait_recv()

    def rs_first(self, w):
        for d in (3, 1) if self.four else self.others():
            self.only(d, {3: (0, 1, 2), 1: (1, 2, 3)}, lambda d=d: self.rs_copy(w, d).start())

    def rs_rest(self, w):
        if self.four:
            for d in (2, 1, 3):
                self.only(d, {1: (0,), 2: (0, 3), 3: (3,)}, lambda d=d: self.rs_copy(w, d).start())
            self.rs_relay(w)

    def rs_relay(self, w):
        lin = getattr(self.s, f"lin{w}")
        for via in (1, 2):
            @pl.when(self.p == via)
            def _(via=via):
                self.rs_wait(w, via)
                add_into(self.gshard(w, (via + 2) % 4, self.c), lin.at[via])
                self.rs_copy(w, 2).start()

    def rs_final(self, w, out_vmem):
        p = self.p
        lin = getattr(self.s, f"lin{w}")
        out = out_vmem.at[:, pl.ds(0, self.z.cols[w])]
        copy_f32(out, self.gshard(w, p, self.c))
        for q in range(self.z.PZ):
            here = p != q
            if self.four and q in (0, 3):
                here = here & (p != 3 - q)

            @pl.when(here)
            def _(q=q):
                self.rs_wait(w, q)
                add_into(out, lin.at[q])

    def rs_finish(self, w):
        for q in range(self.z.PZ):
            self.rs_sib_copy(w, q).wait_send()
        for d in self.others():
            self.rs_copy(w, d).wait_send()


def copy_f32(dst, src):
    rows = dst.shape[0]
    step = 32

    def body(i, _):
        at = pl.ds(pl.multiple_of(i * step, step), step)
        dst[at, :] = src[at, :].astype(F32)
        return 0

    lax.fori_loop(0, rows // step, body, 0)


def kernel(z, names, *refs):
    (x_hbm, og_hbm, len_ref, ga_in, gf_in, freq_ref, *rest) = refs
    qkv_hbm, rest = rest[:3], rest[3:]
    w_hbm, rest = rest[:4], rest[4:]
    mixed_hbm, tg_hbm, ga_out, gf_out, *rest = rest
    oqkv_hbm, rest = rest[:3], rest[3:]
    o_hbm, rest = rest[:4], rest[4:]

    class Scratch:
        pass

    s = Scratch()
    for name, ref in zip(names, rest, strict=True):
        setattr(s, name, ref)
    ws = [getattr(s, f"w{w}") for w in range(z.NW)]
    w_out, w_gate, w_up, w_down = ws[z.nk:]
    s.mid, s.dqkv = s.n2, s.n2
    if z.HO == z.HQ:
        s.qin = getattr(s, f"sib{z.WO}").at[0]
    one_rbuf = not hasattr(s, "rbuf_b")
    if one_rbuf:
        s.rbuf_b = s.rbuf_a
    R, D, L, F, T = z.R, z.D, z.L, z.F, z.T
    ring = Ring(z)
    line = Line(z, s, ws, [s.dwd.at[:, pl.ds(g * z.HG, z.HG)] for g in range(z.nk)] + ws[z.nk:z.WD] + [s.dwd])
    dp, t, p, c = ring.dp, ring.t, line.p, line.c
    own_off = pl.multiple_of(t * R, R)
    own_rows = pl.ds(own_off, R)

    loc = [pltpu.make_async_copy(x_hbm, s.xv, s.s_loc.at[0]),
           pltpu.make_async_copy(og_hbm, s.ogr.at[own_rows], s.s_loc.at[1])]
    for i, (src, dst) in enumerate(zip(qkv_hbm, (s.qin, s.kin, s.vin), strict=True)):
        loc.append(pltpu.make_async_copy(src, dst, s.s_loc.at[2 + i]))
    for i, w in enumerate((z.WO, z.WG, z.WU, z.WD)):
        loc.append(pltpu.make_async_copy(w_hbm[i], line.shard(w, p, c), s.s_loc.at[5 + i]))
    for i in (2, 3, 4, 0, 5, 6, 1, 7, 8):
        loc[i].start()
    for i, ref in enumerate((ga_in, gf_in)):
        s.gain[i:i + 1, :] = ref[...].reshape(1, D)
    ga_ref, gf_ref = s.gain.at[0:1], s.gain.at[1:2]

    bar = pltpu.get_barrier_semaphore()
    peers = [line.sibling]
    peers += [(rem(p + d, z.PZ) * 2 + c, t) for d in range(1, z.PZ)]
    peers += [(dp, rem(t + d, T)) for d in range(1, T)]
    for peer in peers:
        pl.semaphore_signal(bar, 1, device_id=peer, device_id_type=MESH)
    pl.semaphore_wait(bar, len(peers))

    for i in (2, 3, 4):
        loc[i].wait()
    gc = z.G * HEAD
    for g in range(z.nk):
        line.shard(g, p, c)[...] = jnp.concatenate([
            s.qin[:, g * gc:(g + 1) * gc], s.kin[:, g * HEAD:(g + 1) * HEAD], s.vin[:, g * HEAD:(g + 1) * HEAD],
        ], axis=1)
        line.ag_near(g)

    loc[0].wait()
    NR = 32

    def norm_rows(i, _):
        at = pl.ds(pl.multiple_of(i * NR, NR), NR)
        x = s.xv[at, :].astype(F32)
        f = lax.rsqrt(jnp.mean(x * x, axis=-1, keepdims=True) + EPS)
        s.normed[pl.ds(pl.multiple_of(own_off + i * NR, NR), NR), :] = (x * f * ga_ref[...]).astype(BF)
        return 0

    lax.fori_loop(0, R // NR, norm_rows, 0)
    ag_x = Gather(ring, s.normed, s.s_agS.at[0], s.s_agR.at[0])
    ag_x.start()

    l0 = len_ref[0, 0]
    lane = lax.broadcasted_iota(jnp.int32, (R, LANES), 1)

    def table_rows(i, _):
        at = pl.ds(pl.multiple_of(i * R, R), R)
        place = lax.broadcasted_iota(jnp.int32, (R, LANES), 0) + i * R
        pos = place - jnp.where(place >= l0, l0, 0)
        ang = pos.astype(F32) * freq_ref[...]
        s.cos[at, :] = jnp.cos(ang)
        sn = jnp.sin(ang)
        s.sin[at, :] = jnp.where(lane < 64, -sn, sn)
        return 0

    lax.fori_loop(0, T, table_rows, 0)
    half = HEAD // 2
    rowi = lax.broadcasted_iota(jnp.int32, (z.HG, LANES), 0)
    coli = lax.broadcasted_iota(jnp.int32, (z.HG, LANES), 1)
    inside = (coli < half) | ((coli >= 64) & (coli < 64 + half))
    src = jnp.where(inside, jnp.where(coli < half, coli, coli - (64 - half)), -100 * HEAD)
    for h in range(z.G + 2):
        s.perm[:, h * LANES:(h + 1) * LANES] = jnp.where(rowi == src + h * HEAD, 1.0, 0.0).astype(BF)

    for g in range(z.nk):
        line.ag_far(g)
    ag_x.step(1, True)
    loc[1].wait()
    ag_og = Gather(ring, s.ogr, s.s_agS.at[1], s.s_agR.at[1])
    ag_x.step(1, False)
    loc[5].wait()
    line.ag_near(z.WO)

    wp = s.part
    for g in range(z.nk):
        line.ag_recv(g)
    line.ag_far(z.WO)
    loc[6].wait()
    line.ag_near(z.WG)
    for g in range(z.nk):
        line.ag_drain(g)
        wp[g * z.PG:(g + 1) * z.PG, :] = dot(s.perm[...], ws[g][...], (((0,), (1,)), ((), ()))).astype(BF)
    qscale = HEAD ** -0.5 * LOG2E

    def qkv(step):
        off = ring.off(step)
        blk = ring.index(step)
        a = s.normed[pl.ds(off, R), :]
        cs, sn = s.cos[pl.ds(off, R), :], s.sin[pl.ds(off, R), :]
        for g in range(z.nk):
            y = dot(a, wp[g * z.PG:(g + 1) * z.PG, :], NT)
            for j in range(z.G + 2):
                yj = y[:, j * LANES:(j + 1) * LANES]
                if j <= z.G:
                    rot = yj * cs + pltpu.roll(yj, 64, 1) * sn
                if j < z.G:
                    s.q4[g, blk, j * R:(j + 1) * R, :] = (rot * qscale).astype(BF)
                elif j == z.G:
                    s.kk[g, pl.ds(off, R), :] = rot.astype(BF)
                else:
                    s.vv[g, pl.ds(off, R), :] = yj.astype(BF)

    qkv(0)
    for k in range(1, z.H):
        if k > 1:
            ag_x.step(k, True)
            ag_x.step(k, False)
        qkv(k)
        qkv(-k)
    ag_x.step(z.H, True)
    qkv(z.H)
    ag_og.start()

    line.ag_recv(z.WO)
    line.ag_far(z.WG)
    loc[7].wait()
    line.ag_near(z.WU)

    def row_form(col):
        wide = jnp.broadcast_to(col, (col.shape[0], LANES))
        return jnp.transpose(wide)[0:1, :]

    GR = z.G * R

    def allowed(qb, kb, diagonal, heads=z.G):
        qs = rem(lax.broadcasted_iota(jnp.int32, (1, heads * R), 1), R) + qb * R
        keys = lax.broadcasted_iota(jnp.int32, (R, heads * R), 0) + kb * R
        ok = keys >= jnp.where(qs >= l0, l0, 0)
        return ok & (keys <= qs) if diagonal else ok

    HP = 1

    def attend(qb):
        def one(i, _):
            g, j = div(i, z.G // HP), rem(i, z.G // HP)
            at = pl.ds(pl.multiple_of(j * HP * R, R), HP * R)
            q = s.q4[g, qb, at, :]
            scores = []
            for kb in range(qb + 1):
                st = dot(s.kk[g, kb * R:(kb + 1) * R, :], q, NT)
                scores.append(jnp.where(allowed(qb, kb, kb == qb, HP), st, -1e30))
            peak = jnp.max(scores[0], axis=0, keepdims=True)
            for st in scores[1:]:
                peak = jnp.maximum(peak, jnp.max(st, axis=0, keepdims=True))
            total, out = 0.0, 0.0
            for kb in range(qb + 1):
                e = jnp.exp2(scores[kb] - peak)
                total = total + jnp.sum(e, axis=0, keepdims=True)
                out = out + dot(s.vv[g, kb * R:(kb + 1) * R, :], e.astype(BF), TN)
            s.o4[g, qb, at, :] = jnp.transpose(out / total).astype(BF)
            s.lse[g, qb, :, at] = peak + jnp.log2(total)
            return 0

        lax.fori_loop(0, z.nk * z.G // HP, one, 0)

    hops = [(k, same) for k in range(1, z.H + 1) for same in (True, False)]
    for qb in range(T):
        attend(qb)
        if qb == 0:
            ag_og.step(*hops.pop(0))

    ag_x.finish()
    rs_o = Scatter(ring, s.part, s.rbuf_a, s.s_rsS.at[0], s.s_rsR.at[0])
    NB = 768 if T <= 4 else 512

    qperm = s.perm[0:z.G * HEAD, 0:z.G * LANES]

    def unpadded(blk):
        out = []
        for g in range(z.nk):
            pads = [s.o4[g, blk, j * R:(j + 1) * R, :] for j in range(z.G)]
            out.append(dot(jnp.concatenate(pads, axis=1), qperm, NT).astype(BF))
        return jnp.concatenate(out, axis=1) if z.nk > 1 else out[0]

    def out_block(step):
        off, blk = ring.off(step), ring.index(step)
        a = unpadded(blk)

        def cols(n, _):
            at = pl.ds(pl.multiple_of(n * NB, NB), NB)
            s.part[pl.ds(off, R), at] = dot(a, w_out[at, 0:z.HQ], NT).astype(BF)
            return 0

        lax.fori_loop(0, D // NB, cols, 0)

    def scatter(rs, block, between=None):
        for k in range(1, z.H + 1):
            dist = z.H - k + 1
            block(dist)
            if k > 1:
                rs.send(k, False, (0,))
                block(-dist)
                rs.send(k, False, (1,))
            rs.send(k, True)
            if between is not None:
                between(k)
        block(0)

    line.ag_drain(z.WO)

    def between_o(k):
        if k == z.H:
            for hop in hops:
                ag_og.step(*hop)
            line.ag_recv(z.WG)
            line.ag_far(z.WU)
            loc[8].wait()
            line.ag_near(z.WD)

    scatter(rs_o, out_block, between_o)
    rs_o.arrive()

    def middle_rows(i, _):
        lo = i * NR
        at = pl.ds(pl.multiple_of(lo, NR), NR)
        m = s.xv[at, :].astype(F32) + rs_o.rows(lo, NR)
        s.middle[at, :] = m
        f = lax.rsqrt(jnp.mean(m * m, axis=-1, keepdims=True) + EPS)
        s.n2[pl.ds(pl.multiple_of(own_off + lo, NR), NR), :] = (m * f * gf_ref[...]).astype(BF)
        return 0

    lax.fori_loop(0, R // NR, middle_rows, 0)
    ag_n2 = Gather(ring, s.n2, s.s_agS.at[2], s.s_agR.at[2])
    ag_n2.start()
    ag_og.finish()

    ag_m = Gather(ring, s.mid, s.s_agS.at[3], s.s_agR.at[3])
    rs_n = Scatter(ring, s.part, s.rbuf_a, s.s_rsS.at[1], s.s_rsR.at[1])
    rs_f = Scatter(ring, s.ogr, s.rbuf_b, s.s_rsS.at[2], s.s_rsR.at[2])
    FB = 512 if T <= 4 else 256

    def free(i):
        for d in (0, 1):
            pl.semaphore_signal(s.s_free.at[i], 1, device_id=ring.to[d], device_id_type=MESH)

    def await_free(i):
        pl.semaphore_wait(s.s_free.at[i], 2)

    def ffn_phase(gl, ul, hid):
        def wgrad(w, rows_ref, act_ref):
            if w != z.WD:
                line.ag_finish(w)
            DB = 512

            def tile(i, _):
                at = pl.ds(pl.multiple_of(i * DB, DB), DB)
                line.gs[w][at, :] = dot(rows_ref[:, at], act_ref[...], TN).astype(BF)
                return 0

            lax.fori_loop(0, D // DB, tile, 0)
            line.rs_sib_start(w)

        def gate_up(step):
            rows = pl.ds(ring.off(step), R)

            def cols(n, _):
                at = pl.ds(pl.multiple_of(n * FB, FB), FB)
                a = s.n2[rows, :]
                g = dot(a, w_gate[:, at], NN)
                u = dot(a, w_up[:, at], NN)
                gl[rows, at] = g.astype(BF)
                ul[rows, at] = u.astype(BF)
                hid[rows, at] = (g / (1.0 + jnp.exp(-g)) * u).astype(BF)
                return 0

            lax.fori_loop(0, F // FB, cols, 0)

        line.ag_drain(z.WG)
        ag_n2.step(1, True)
        line.ag_far(z.WD)
        ag_n2.step(1, False)
        line.ag_recv(z.WU)
        line.ag_drain(z.WU)
        gate_up(0)
        for k in range(1, z.H):
            if k > 1:
                ag_n2.step(k, True)
                ag_n2.step(k, False)
            gate_up(k)
            gate_up(-k)
        ag_n2.step(z.H, True)
        gate_up(z.H)
        wgrad(z.WD, s.ogr, hid)
        rs_o.finish()
        line.ag_recv(z.WD)
        line.rs_sib_sum(z.WD)
        line.rs_first(z.WD)
        line.ag_drain(z.WD)

        def act_grads(step):
            rows = pl.ds(ring.off(step), R)

            def cols(n, _):
                at = pl.ds(pl.multiple_of(n * FB, FB), FB)
                hg = dot(s.ogr[rows, :], w_down[:, at], NN)
                g = gl[rows, at].astype(F32)
                u = ul[rows, at].astype(F32)
                sg = 1.0 / (1.0 + jnp.exp(-g))
                silu = g * sg
                gl[rows, at] = (hg * u * (sg + silu * (1.0 - sg))).astype(BF)
                ul[rows, at] = (hg * silu).astype(BF)
                return 0

            lax.fori_loop(0, F // FB, cols, 0)

            def back(n, _):
                at = pl.ds(pl.multiple_of(n * NB, NB), NB)
                s.part[rows, at] = (
                    dot(gl[rows, :], w_gate[at, :], NT) + dot(ul[rows, :], w_up[at, :], NT)
                ).astype(BF)
                return 0

            lax.fori_loop(0, D // NB, back, 0)

        def between_n(k):
            if k == z.H:
                line.rs_rest(z.WD)

        scatter(rs_n, act_grads, between_n)

        wgrad(z.WG, s.n2, gl)
        wgrad(z.WU, s.n2, ul)
        ag_n2.finish()
        free(0)
        line.rs_sib_sum(z.WG)
        line.rs_first(z.WG)
        rs_n.arrive()

        s.gsum[...] = jnp.zeros_like(s.gsum)

        def norm_back(i, _):
            lo = i * NR
            at = pl.ds(pl.multiple_of(lo, NR), NR)
            ng = rs_n.rows(lo, NR)
            m = s.middle[at, :]
            f = lax.rsqrt(jnp.mean(m * m, axis=-1, keepdims=True) + EPS)
            zz = m * f
            s.gsum[0:1, :] += jnp.sum(ng * zz, axis=0, keepdims=True)
            dz = ng * gf_ref[...]
            own = pl.ds(pl.multiple_of(own_off + lo, NR), NR)
            mg = s.ogr[own, :].astype(F32) + f * (dz - zz * jnp.mean(dz * zz, axis=-1, keepdims=True))
            s.mgrad[at, :] = mg
            s.mid[own, :] = mg.astype(BF)
            return 0

        lax.fori_loop(0, R // NR, norm_back, 0)
        rs_n.finish()
        await_free(0)
        ag_m.start()
        line.rs_sib_sum(z.WU)
        line.rs_first(z.WU)

        def down_block(step):
            rows = pl.ds(ring.off(step), R)

            def cols(n, _):
                at = pl.ds(pl.multiple_of(n * NB, NB), NB)
                s.ogr[rows, at] = dot(hid[rows, :], w_down[at, :], NT).astype(BF)
                return 0

            lax.fori_loop(0, D // NB, cols, 0)

        for k in range(1, z.H + 1):
            down_block(k)
            if k < z.H:
                down_block(-k)
        down_block(0)
        ag_m.step(1, True)
        line.rs_rest(z.WG)

    pl.run_scoped(ffn_phase, pltpu.VMEM((L, F), BF), pltpu.VMEM((L, F), BF), pltpu.VMEM((L, F), BF))

    def do_block(step):
        off, blk = ring.off(step), ring.index(step)
        a = dot(s.mid[pl.ds(off, R), :], w_out[:, 0:z.HQ], NN).astype(BF)
        for h in range(z.nq):
            g, j = h // z.G, h % z.G
            if j == 0:
                d = dot(a[:, g * z.G * HEAD:(g + 1) * z.G * HEAD], qperm, NN)
            dh = d[:, j * LANES:(j + 1) * LANES]
            at = pl.ds(j * R, R)
            s.do4[g, blk, at, :] = dh.astype(BF)
            dl = jnp.sum(dh * s.o4[g, blk, at, :].astype(F32), axis=-1, keepdims=True)
            s.dlt[g, blk, :, at] = row_form(dl)

    do_block(0)
    for k in range(1, z.H):
        if k > 1:
            ag_m.step(k, True)
        ag_m.step(k, False)
        do_block(k)
        do_block(-k)
    ag_m.step(z.H, True)
    do_block(z.H)

    rs_f.send(1, True)
    rs_f_steps = [(k, same) for k in range(2, z.H + 1) for same in (False, True)]

    def outputs(chunks):
        def run(stage):
            copies = []
            for i, w in enumerate(chunks):
                slot = stage.at[i % 2]
                if i >= 2:
                    copies[i - 2].wait()
                line.rs_final(w, slot)
                cp = pltpu.make_async_copy(slot.at[:, pl.ds(0, z.cols[w])], o_hbm[w - z.nk], s.s_loc.at[9 + i % 2])
                cp.start()
                copies.append(cp)
            for cp in copies[-2:]:
                cp.wait()

        pl.run_scoped(run, pltpu.VMEM((2, z.S, max(z.cols)), F32))

    def back_phase(dq, dk, dv, att):
        dk[...] = jnp.zeros_like(dk)
        dv[...] = jnp.zeros_like(dv)

        def back_block(qb):
            def pair(kb, diagonal):
                for g in range(z.nk):
                    at = pl.ds(kb * R, R) if diagonal else pl.ds(pl.multiple_of(kb * R, R), R)
                    q, do = s.q4[g, qb], s.do4[g, qb]
                    kk, vv = s.kk[g, at, :], s.vv[g, at, :]
                    e = jnp.exp2(dot(kk, q, NT) - s.lse[g, qb, 0:1, :])
                    pt = jnp.where(allowed(qb, kb, diagonal), e, 0.0)
                    dpt = dot(vv, do, NT)
                    ds = (pt * (dpt - s.dlt[g, qb, 0:1, :])).astype(BF)
                    dv[g, at, :] += dot(pt.astype(BF), do, NN)
                    dk[g, at, :] += dot(ds, q, NN)
                    if diagonal:
                        dq[g, qb] = dot(ds, kk, TN)
                    else:
                        dq[g, qb] += dot(ds, kk, TN)

            def off_diagonal(kb, _):
                pair(kb, False)
                return 0

            pair(qb, True)
            if qb > 0:
                lax.fori_loop(0, qb, off_diagonal, 0)

        line.ag_finish(z.WO)
        DB = 512

        def unpad(i, _):
            att[pl.ds(pl.multiple_of(i * R, R), R), :] = unpadded(i)
            return 0

        lax.fori_loop(0, T, unpad, 0)

        def tile(i, _):
            at = pl.ds(pl.multiple_of(i * DB, DB), DB)
            w_out[at, 0:z.HQ] = dot(s.mid[:, at], att[...], TN).astype(BF)
            return 0

        lax.fori_loop(0, D // DB, tile, 0)
        line.rs_sib_start(z.WO)
        line.rs_rest(z.WU)
        for qb in range(T):
            back_block(qb)
            if qb == min(1, T - 1):
                line.rs_sib_sum(z.WO)
                line.rs_first(z.WO)
            if qb == T - 1:
                line.rs_rest(z.WO)
            if rs_f_steps:
                rs_f.send(*rs_f_steps.pop(0))

        ag_m.finish()

        def unrotate(i, _):
            rows = pl.ds(pl.multiple_of(i * R, R), R)
            cs, sn = s.cos[rows, :], s.sin[rows, :]
            for g in range(z.nk):
                heads = []
                for j in range(z.G + 2):
                    if j < z.G:
                        v = dq[g, i, j * R:(j + 1) * R, :] * (HEAD ** -0.5)
                    elif j == z.G:
                        v = dk[g, rows, :] * LN2
                    else:
                        v = dv[g, rows, :]
                    if j <= z.G:
                        v = v * cs - pltpu.roll(v, 64, 1) * sn
                    heads.append(v.astype(BF))
                four = jnp.concatenate(heads, axis=1)
                s.dqkv[rows, g * z.HG:(g + 1) * z.HG] = dot(four, s.perm[...], NT).astype(BF)
            return 0

        lax.fori_loop(0, T, unrotate, 0)

    pl.run_scoped(
        back_phase,
        pltpu.VMEM((z.nk, T, z.G * R, LANES), F32),
        pltpu.VMEM((z.nk, L, LANES), F32),
        pltpu.VMEM((z.nk, L, LANES), F32),
        pltpu.VMEM((L, z.HQ), BF),
    )
    for step in rs_f_steps:
        rs_f.send(*step)

    def mixed_rows(i, _):
        lo = i * NR
        at = pl.ds(pl.multiple_of(lo, NR), NR)
        s.ogr[pl.ds(pl.multiple_of(own_off + lo, NR), NR), :] = (s.middle[at, :] + rs_f.rows(lo, NR)).astype(BF)
        return 0

    out_mixed = pltpu.make_async_copy(s.ogr.at[own_rows], mixed_hbm, s.s_loc.at[14])

    def qkv_outputs(stage, q_out, k_out, v_out):
        last()
        for g in range(z.nk):
            line.rs_final(g, stage.at[g])
        cuts = (0, gc, gc + HEAD, gc + 2 * HEAD)
        copies = []
        for i, out in enumerate((q_out, k_out, v_out)):
            parts = [stage[g, :, cuts[i]:cuts[i + 1]] for g in range(z.nk)]
            out[...] = jnp.concatenate(parts, axis=1) if z.nk > 1 else parts[0]
            copies.append(pltpu.make_async_copy(out, oqkv_hbm[i], s.s_loc.at[11 + i]))
            copies[-1].start()
        for cp in copies:
            cp.wait()

    def ffn_out():
        rs_f.arrive()
        lax.fori_loop(0, R // NR, mixed_rows, 0)
        out_mixed.start()

    if one_rbuf:
        ffn_out()
        free(1)
        await_free(1)

    rs_q = Scatter(ring, s.part, s.rbuf_a, s.s_rsS.at[3], s.s_rsR.at[3])

    def qkv_back(step):
        rows = pl.ds(ring.off(step), R)

        def cols(n, _):
            at = pl.ds(pl.multiple_of(n * NB, NB), NB)
            tot = dot(s.dqkv[rows, 0:z.HG], ws[0][at, :], NT)
            for g in range(1, z.nk):
                tot = tot + dot(s.dqkv[rows, g * z.HG:(g + 1) * z.HG], ws[g][at, :], NT)
            s.part[rows, at] = tot.astype(BF)
            return 0

        lax.fori_loop(0, D // NB, cols, 0)

    s.gs[c] = jnp.zeros_like(s.gs[c])

    def qkv_grads(k):
        if k == z.H:
            line.rs_sib_sum(z.nk - 1)
            line.rs_first(z.nk - 1)
            for g in range(z.nk - 1):
                line.rs_rest(g)
            if not one_rbuf:
                ffn_out()
        if k > 1:
            return
        outputs([z.WD])
        line.rs_finish(z.WD)
        for g in range(z.nk):
            def qkv_tile(i, _, g=g):
                at = pl.ds(pl.multiple_of(i * 512, 512), 512)
                grad = dot(s.normed[:, at], s.dqkv[:, g * z.HG:(g + 1) * z.HG], TN)
                part = jnp.sum(grad * ws[g][at, :].astype(F32), axis=-1, keepdims=True)
                s.gs[c, 0:1, at] += row_form(part)
                s.dwd[at, g * z.HG:(g + 1) * z.HG] = grad.astype(BF)
                return 0

            lax.fori_loop(0, D // 512, qkv_tile, 0)
            line.rs_sib_start(g)
            if g > 0:
                line.rs_sib_sum(g - 1)
                line.rs_first(g - 1)

    scatter(rs_q, qkv_back, qkv_grads)
    line.rs_rest(z.nk - 1)
    s.gs[c, 0:1, :] = s.gs[c, 0:1, :] / ga_ref[...]
    s.gs[c, 1:2, :] = s.gsum[0:1, :]

    def g_copy(stage, d, ref, slot, to):
        return pltpu.make_async_remote_copy(
            src_ref=ref.at[slot], dst_ref=ref.at[slot], send_sem=s.s_gS.at[stage, d], recv_sem=s.s_gR.at[stage, d],
            device_id=to, device_id_type=MESH,
        )

    g0 = g_copy(0, 0, s.gs, c, line.sibling)
    g0.start()
    g0.wait_recv()
    s.gz[p] = s.gs[0] + s.gs[1]
    g1 = [g_copy(1, d, s.gz, p, (rem(p + d, z.PZ) * 2 + c, t)) for d in range(1, z.PZ)]
    for cp in g1:
        cp.start()
    for cp in g1:
        cp.wait_recv()
    tot = s.gz[0]
    for q in range(1, z.PZ):
        tot = tot + s.gz[q]
    s.gt[t] = tot
    g2 = [g_copy(2, d, s.gt, t, (dp, rem(t + d, T))) for d in range(1, T)]
    for cp in g2:
        cp.start()
    def last_rows(i, _):
        lo = i * NR
        at = pl.ds(pl.multiple_of(lo, NR), NR)
        ng = rs_q.rows(lo, NR)
        x = s.xv[at, :].astype(F32)
        f = lax.rsqrt(jnp.mean(x * x, axis=-1, keepdims=True) + EPS)
        zz = x * f
        dz = ng * ga_ref[...]
        s.mgrad[at, :] += f * (dz - zz * jnp.mean(dz * zz, axis=-1, keepdims=True))
        return 0

    out_tg = pltpu.make_async_copy(s.mgrad, tg_hbm, s.s_loc.at[15])

    def last():
        rs_q.arrive()
        lax.fori_loop(0, R // NR, last_rows, 0)
        out_tg.start()

    outputs([z.WG, z.WU, z.WO])
    pl.run_scoped(
        qkv_outputs, pltpu.VMEM((z.nk, z.S, z.HG), F32), pltpu.VMEM((z.S, z.HQ), F32),
        pltpu.VMEM((z.S, z.nk * HEAD), F32), pltpu.VMEM((z.S, z.nk * HEAD), F32),
    )

    for cp in g2:
        cp.wait_recv()
    tot = s.gt[0]
    for q in range(1, T):
        tot = tot + s.gt[q]
    ga_out[...] = tot[0:1, :].reshape(D)
    gf_out[...] = tot[1:2, :].reshape(D)

    out_mixed.wait()
    rs_f.finish()
    out_tg.wait()
    rs_q.finish()
    g0.wait_send()
    for cp in g1 + g2:
        cp.wait_send()
    for w in list(range(z.nk)) + [z.WD]:
        line.ag_finish(w)
    for w in range(z.NW):
        if w != z.WD:
            line.rs_finish(w)


def hand_out(count, *refs):
    src, dst, sem, held = refs[:count], refs[count:2 * count], refs[2 * count], refs[2 * count + 1:]
    first = [pltpu.make_async_copy(a, v, sem.at[0, i]) for i, (a, v) in enumerate(zip(src, held, strict=True))]
    second = [pltpu.make_async_copy(v, b, sem.at[1, i]) for i, (b, v) in enumerate(zip(dst, held, strict=True))]
    for cp in first:
        cp.start()
    for cp, onward in zip(first, second, strict=True):
        cp.wait()
        onward.start()
    for cp in second:
        cp.wait()


def body(tokens, seq_lengths, gain_attn, query_weight, key_matrix, value_matrix, out_weight,
         gain_ffn, gate_weight, up_weight, down_weight, out_grad):
    n_dp, n_tensor = lax.axis_size("dp"), lax.axis_size("tensor")
    z = Sizes(n_dp, n_tensor, tokens.shape[0], tokens.shape[1], query_weight.shape[1],
              key_matrix.shape[1], gate_weight.shape[1])
    shards = [
        query_weight, key_matrix, value_matrix,
        jnp.pad(out_weight.T, ((0, 0), (0, z.HO - z.HQ))), gate_weight, up_weight, down_weight.T,
    ]
    grads = [jax.ShapeDtypeStruct((z.S, n), F32) for n in (z.HQ, z.nk * HEAD, z.nk * HEAD) + z.cols[z.nk:]]
    j = np.arange(LANES) % 64
    freq = np.where(j < HEAD // 2, ROPE_BASE ** (-(2.0 * j) / HEAD), 0.0).astype(np.float32)[None, :]
    items = scratch_list(z)
    names = [name for name, _ in items]
    hbm = pl.BlockSpec(memory_space=pl.ANY)
    vmem = pl.BlockSpec(memory_space=pltpu.VMEM)
    flops = 2 * 3 * z.L * z.D * sum(z.cols)
    outs = pl.pallas_call(
        functools.partial(kernel, z, names),
        out_shape=(
            jax.ShapeDtypeStruct((z.R, z.D), BF),
            jax.ShapeDtypeStruct((z.R, z.D), F32),
            jax.ShapeDtypeStruct((z.D,), F32),
            jax.ShapeDtypeStruct((z.D,), F32),
            *grads,
        ),
        in_specs=[hbm, hbm, pl.BlockSpec(memory_space=pltpu.SMEM), vmem, vmem, vmem] + [hbm] * 7,
        out_specs=[hbm, hbm, vmem, vmem] + [hbm] * 7,
        scratch_shapes=[shape for _, shape in items],
        compiler_params=pltpu.CompilerParams(
            collective_id=0, has_side_effects=True, vmem_limit_bytes=67_000_000
        ),
        cost_estimate=pl.CostEstimate(flops=flops, bytes_accessed=16_000_000, transcendentals=0),
        name="layer",
    )(tokens, out_grad, seq_lengths, gain_attn, gain_ffn, jnp.asarray(freq), *shards)
    count = len(outs)
    shapes = [jax.ShapeDtypeStruct(a.shape, a.dtype) for a in outs]
    outs = pl.pallas_call(
        functools.partial(hand_out, count),
        out_shape=tuple(shapes),
        in_specs=[hbm] * count, out_specs=[hbm] * count,
        scratch_shapes=[pltpu.SemaphoreType.DMA((2, count))] + [pltpu.VMEM(a.shape, a.dtype) for a in shapes],
        compiler_params=pltpu.CompilerParams(vmem_limit_bytes=67_000_000),
        name="hand_out",
    )(*outs)
    mixed, tokens_grad, ga_grad, gf_grad, q_g, k_g, v_g, out_g, gate_g, up_g, down_g = outs
    return (
        mixed, tokens_grad, ga_grad, q_g, k_g, v_g, out_g[:, :z.HQ].T, gf_grad, gate_g, up_g, down_g.T,
    )


def solution(mesh):
    rows = P(("dp", "tensor"), None)
    split, turned = P("dp", "tensor"), P("tensor", "dp")
    return jax.shard_map(
        body, mesh=mesh,
        in_specs=(rows, P("dp", None), P(), split, split, split, turned, P(), split, split, turned, rows),
        out_specs=(rows, rows, P(), split, split, split, turned, P(), split, split, turned),
        check_vma=False,
    )
```
